128 devices in a mesh: dp: 8 (over x, z_hi), tensor: 8 (over z_lo, y), section: 2 (over core).
Axes of the slice: x: 4, y: 4, z: 4 (z_hi: 2, z_lo: 2; z = z_hi * 2 + z_lo), core: 2. Of those that a mesh axis runs over, the one named last changes fastest.
Arguments:
- text_hidden: bfloat16 [2, 8, 128, 8192], P(None, 'dp', None, 'tensor'), may hold values from -6 to 6
- image_tokens: bfloat16 [8, 3200, 8192], P('dp', 'section', 'tensor'), may hold values from -6 to 6
- attn_gain: float32 [2, 8192], P('section'), may hold values from 0.25 to 1.75
- w_query: bfloat16 [2, 8192, 4096], P('section', None, 'tensor'), may hold values from -0.0625 to 0.0625
- w_keyval: bfloat16 [2, 8192, 8, 256], P('section', 'tensor'), may hold values from -0.09375 to 0.09375
- q_gain: float32 [2, 128], P('section'), may hold values from 0.5 to 2
- k_gain: float32 [2, 128], P('section'), may hold values from 0.5 to 2
- w_out: bfloat16 [2, 4096, 8192], P('section', 'tensor'), may hold values from -0.375 to 0.375
- gate: float32 [2], P('section'), may hold values from 0.3 to 1.5
- image_choice: int32 [2, 8, 2], P(None, 'dp'), may hold values from 0 to 7
- valid_tiles: int32 [8], replicated, may hold values from 1 to 2
Outputs:
- layer_outputs: bfloat16 [2, 2, 8, 128, 8192], P('section', None, 'dp', None, 'tensor')
The draws below stay inside these ranges and needn't reach their ends.
Inputs may be any that keep to these rules, and one draw needn't show every extreme that they name: `image_choice`: image indices.
All inputs are finite; a program needn't handle non-finite values.
Results may differ from the reference program's by a relative error of at most 0.029.
Values may be sent and summed in bfloat16 or wider, within the bound.
A program may use at most 128 MiB of HBM per device.

```python
import jax
import jax.numpy as jnp
from jax import lax

D = 8192
HEADS = 32
KV_HEADS = 8
HD = 128
TILES = 2
TILE_TOK = 1600
PATCHES = 3200
SEQ = 128
MB = 2
LAYERS = 2
IMAGES = 8
SEQS = 8
N_TENSOR = 8


def touch_ends(drawn, key, low, top_value):
    index_at = [jax.random.randint(jax.random.fold_in(key, axis), (), 0, length) for axis, length in enumerate(drawn.shape)]
    main_axis = drawn.shape.index(max(drawn.shape))
    neighbour = index_at[:main_axis] + [(index_at[main_axis] + 1) % drawn.shape[main_axis]] + index_at[main_axis + 1:]
    return drawn.at[tuple(index_at)].set(low).at[tuple(neighbour)].set(top_value)


def raised(values, stream_key, source, target, blocks, factor):
    owner, partner = [(jnp.arange(values.shape[position]) // (values.shape[position] // blocks)).reshape([-1 if axis == position else 1 for axis in range(values.ndim)]) for position in (source, target)]
    chosen = jax.random.permutation(stream_key, blocks)[partner]
    strong = (owner == chosen) | (owner == (partner + blocks // 2) % blocks)
    return jnp.where(strong, factor * values, values)


def block_scale(own_key, shape, split, smallest, largest):
    factor_of = 1.0
    for dim, blocks in split:
        heights = jax.random.uniform(jax.random.fold_in(jax.random.fold_in(own_key, 6), dim), (blocks,), jnp.float32, smallest / len(split), largest / len(split))
        factor_of = factor_of * jnp.repeat(jnp.exp(heights), shape[dim] // blocks).reshape((-1,) + (1,) * (len(shape) - 1 - dim))
    return factor_of


def gaussian(own_key, dims, spread, reach, split=(), kind=jnp.bfloat16):
    values = spread * jax.random.normal(own_key, dims, jnp.float32)
    if split:
        values = values * block_scale(own_key, dims, split, -0.22, 0.18)
    return jnp.clip(values, -reach, reach).astype(kind)


def gaussian_with(rng, extent, width, most, split, heavy, held_as=jnp.bfloat16):
    result = width * jax.random.normal(rng, extent, jnp.float32)
    if split:
        result = result * block_scale(rng, extent, split, -0.22, 0.18)
    return jnp.clip(raised(result, jax.random.fold_in(rng, 3), *heavy), -most, most).astype(held_as)


def setup_inputs(seed: int = 0) -> dict:
    splits = jax.random.split(jax.random.key(seed), 12)
    text_hidden = gaussian(splits[0], (MB, SEQS, SEQ, D), 1.0, 6.0, ((1, 8), (3, 8)))
    image_tokens = gaussian(splits[1], (IMAGES, PATCHES, D), 1.0, 6.0, ((0, 8), (1, 2), (2, 8)))
    attn_gain = jnp.clip(1.0 + 0.15 * jax.random.normal(splits[2], (LAYERS, D), jnp.float32), 0.25, 1.75)
    w_query = gaussian(splits[3], (LAYERS, D, HEADS * HD), D ** -0.5, 0.0625, ((0, 2), (2, 8)))
    w_keyval = gaussian_with(splits[4], (LAYERS, D, KV_HEADS, 2 * HD), D ** -0.5, 0.09375, ((0, 2), (1, 8)), (1, 2, 8, 2.0))
    q_gain = jnp.clip(0.5 + 1.5 * jax.random.uniform(splits[5], (LAYERS, HD), jnp.float32) ** block_scale(splits[5], (LAYERS, HD), ((0, 2),), -0.2, 0.2), 0.5, 2.0)
    k_gain = jnp.clip(0.5 + 1.5 * jax.random.uniform(splits[6], (LAYERS, HD), jnp.float32) ** block_scale(splits[6], (LAYERS, HD), ((0, 2),), -0.2, 0.2), 0.5, 2.0)
    w_out = gaussian_with(splits[7], (LAYERS, HEADS * HD, D), (HEADS * HD // 8) ** -0.5, 0.375, ((0, 2), (1, 8)), (1, 2, 8, 2.0))
    gate = jnp.clip(0.3 + 1.2 * jax.random.uniform(splits[8], (LAYERS,), jnp.float32) ** block_scale(splits[8], (LAYERS,), ((0, 2),), -0.2, 0.2), 0.3, 1.5)
    image_choice = touch_ends(jax.random.randint(splits[9], (MB, SEQS, 2), 0, IMAGES), jax.random.fold_in(splits[9], 1), 0, IMAGES - 1).astype(jnp.int32)
    valid_tiles = touch_ends(jax.random.randint(splits[10], (IMAGES,), 1, TILES + 1), jax.random.fold_in(splits[10], 1), 1, TILES).astype(jnp.int32)
    return {"text_hidden": text_hidden, "image_tokens": image_tokens, "attn_gain": attn_gain, "w_query": w_query, "w_keyval": w_keyval, "q_gain": q_gain, "k_gain": k_gain, "w_out": w_out, "gate": gate, "image_choice": image_choice, "valid_tiles": valid_tiles}


def rms_scale(values, gain):
    return values * lax.rsqrt(lax.optimization_barrier(jnp.mean(values * values, axis=-1, keepdims=True)) + 1e-05) * gain

def reference(text_hidden, image_tokens, attn_gain, w_query, w_keyval, q_gain, k_gain, w_out, gate, image_choice, valid_tiles):
    n_keys = IMAGES * PATCHES
    group_size = HEADS // KV_HEADS
    block_width = D // N_TENSOR
    flat_images = image_tokens.reshape(n_keys, D)
    tile_of = jnp.arange(PATCHES, dtype=jnp.int32) // TILE_TOK
    key_list = []
    val_list = []
    for layer in range(LAYERS):
        weight_flat = w_keyval[layer].reshape(D, KV_HEADS * 2 * HD)
        keyval = jnp.zeros((n_keys, KV_HEADS * 2 * HD), jnp.float32)
        for block in range(N_TENSOR):
            lower = block * block_width
            partial_sum = jnp.dot(flat_images[:, lower:lower + block_width], weight_flat[lower:lower + block_width], preferred_element_type=jnp.float32)
            partial_sum = lax.optimization_barrier(partial_sum.astype(jnp.bfloat16)).astype(jnp.float32)
            keyval = keyval + partial_sum
        keyval = keyval.reshape(n_keys, KV_HEADS, 2 * HD)
        keys = rms_scale(keyval[..., :HD], k_gain[layer]).astype(jnp.bfloat16)
        vals = keyval[..., HD:].astype(jnp.bfloat16)
        key_list.append(jnp.transpose(keys, (1, 0, 2)).reshape(KV_HEADS, IMAGES, PATCHES, HD))
        val_list.append(jnp.transpose(vals, (1, 0, 2)).reshape(KV_HEADS, IMAGES, PATCHES, HD))

    def apply_layer(hidden, layer, chosen):
        normed = rms_scale(hidden.astype(jnp.float32), attn_gain[layer]).astype(jnp.bfloat16)
        query = jnp.dot(normed.reshape(-1, D), w_query[layer], preferred_element_type=jnp.float32)
        query = query.reshape(SEQS, SEQ, KV_HEADS, group_size, HD)
        query = (rms_scale(query, q_gain[layer]) * HD ** (-0.5)).astype(jnp.bfloat16)
        keys_img = key_list[layer]
        vals_img = val_list[layer]

        def one_sequence(item):
            query_one, chosen_one = item
            first = chosen_one[0]
            second = chosen_one[1]
            keys_pair = jnp.concatenate([lax.dynamic_index_in_dim(keys_img, first, 1, keepdims=False), lax.dynamic_index_in_dim(keys_img, second, 1, keepdims=False)], axis=1).astype(jnp.float32)
            vals_pair = jnp.concatenate([lax.dynamic_index_in_dim(vals_img, first, 1, keepdims=False), lax.dynamic_index_in_dim(vals_img, second, 1, keepdims=False)], axis=1).astype(jnp.float32)
            allowed = jnp.concatenate([tile_of < valid_tiles[first], (tile_of < valid_tiles[second]) & (second != first)])
            scores = jnp.einsum('qkgd,knd->kgqn', query_one.astype(jnp.float32), keys_pair)
            scores = jnp.where(allowed[None, None, None, :], scores, -1e+30)
            peak = lax.optimization_barrier(jnp.max(scores, axis=-1, keepdims=True))
            expo = jnp.exp(scores - peak)
            weights = (expo / lax.optimization_barrier(jnp.sum(expo, axis=-1, keepdims=True))).astype(jnp.bfloat16)
            attended = jnp.einsum('kgqn,knd->qkgd', weights.astype(jnp.float32), vals_pair)
            return attended.astype(jnp.bfloat16).reshape(SEQ, HEADS * HD)
        attended = lax.map(one_sequence, (query, chosen))
        proj = jnp.dot(attended.reshape(-1, HEADS * HD), w_out[layer], preferred_element_type=jnp.float32)
        proj = proj.reshape(SEQS, SEQ, D)
        return (hidden.astype(jnp.float32) + jnp.tanh(gate[layer]) * proj).astype(jnp.bfloat16)
    results = [[None] * MB for layer in range(LAYERS)]
    for batch in range(MB):
        hidden = text_hidden[batch]
        for layer in range(LAYERS):
            hidden = apply_layer(hidden, layer, image_choice[batch])
            results[layer][batch] = hidden
    return jnp.stack([jnp.stack(results[layer]) for layer in range(LAYERS)])
```

```python
import functools

import jax
import jax.numpy as jnp
from jax import lax
from jax.experimental import pallas as pl
from jax.experimental.pallas import tpu as pltpu
from jax.sharding import PartitionSpec as P

TILE_TOK = 1600
PIECES = 10
MESH = pl.DeviceIdType.MESH
BF = jnp.bfloat16
F32 = jnp.float32


def position():
    dp = lax.axis_index("dp")
    tensor = lax.axis_index("tensor")
    return dp // 2, dp % 2, tensor // 4, tensor % 4, lax.axis_index("section")


def device(x, zh, zl, y, core):
    return (x * 2 + zh, zl * 4 + y, core)


def kv_kernel(
    tok_ref, w_ref, gain_ref, text_ref,
    out_ref, text_out_ref,
    tok, wgt, part, from_y1, from_y2, from_z, done,
    tok_sem, w_sem, loc_sem, core_sem, text_send, text_recv, send, recv,
):
    x, zh, zl, y, core = position()
    dp = x * 2 + zh
    tensor = zl * 4 + y
    half = tok_ref.shape[0]
    rows = half * 2 // PIECES
    y_up, y_dn = (y + 1) % 4, (y + 3) % 4
    x_up, x_dn = (x + 1) % 4, (x + 3) % 4
    to_y_up = device(x, zh, zl, y_up, core)
    to_y_dn = device(x, zh, zl, y_dn, core)
    to_z_lo = device(x, zh, 1 - zl, y, core)
    to_z_hi = device(x, 1 - zh, zl, y, core)
    to_x_up = device(x_up, zh, zl, y, core)
    to_x_dn = device(x_dn, zh, zl, y, core)
    to_core = device(x, zh, zl, y, 1 - core)

    def tensor_peer(step):
        return (dp, (tensor + step) % 8, core)

    barrier = pltpu.get_barrier_semaphore()
    for peer in [to_z_hi, to_x_up, to_x_dn, to_core] + [tensor_peer(s) for s in range(1, 8)]:
        pl.semaphore_signal(barrier, inc=1, device_id=peer, device_id_type=MESH)

    def first_row(piece):
        return pl.multiple_of(((piece + core * (PIECES // 2)) % PIECES) * rows, rows)

    def head_of(slot):
        ring = (y + 2) % 4 if slot < 2 else y_up if slot < 4 else y_dn if slot < 6 else y
        return (slot % 2) * 4 + ring

    def tok_copy(piece):
        return pltpu.make_async_copy(
            tok_ref.at[pl.ds(pl.multiple_of(piece * rows, rows), rows)],
            tok.at[pl.ds(pl.multiple_of(core * half + piece * rows, rows), rows)],
            tok_sem.at[piece],
        )

    def w_copy(slot):
        return pltpu.make_async_copy(w_ref.at[head_of(slot)], wgt.at[slot], w_sem.at[slot])

    def core_copy():
        return pltpu.make_async_remote_copy(
            src_ref=tok_ref,
            dst_ref=tok.at[pl.ds(pl.multiple_of(core * half, half), half)],
            send_sem=core_sem.at[0], recv_sem=core_sem.at[1],
            device_id=to_core, device_id_type=MESH,
        )

    def text_copy(step):
        return pltpu.make_async_remote_copy(
            src_ref=text_ref, dst_ref=text_out_ref.at[tensor],
            send_sem=text_send.at[step - 1], recv_sem=text_recv.at[step - 1],
            device_id=tensor_peer(step), device_id_type=MESH,
        )

    def text_own():
        return pltpu.make_async_copy(text_ref, text_out_ref.at[tensor], loc_sem.at[PIECES])

    def remote(kind, piece, src, dst, peer):
        return pltpu.make_async_remote_copy(
            src_ref=src, dst_ref=dst,
            send_sem=send.at[kind, piece], recv_sem=recv.at[kind, piece],
            device_id=peer, device_id_type=MESH,
        )

    def y1_copy(way, piece):
        at = pl.ds(first_row(piece), rows)
        return remote(way, piece, part.at[way, at], from_y1.at[way, at], (to_y_up, to_y_dn)[way])

    def y2_copy(way, piece):
        at = pl.ds(first_row(piece), rows)
        src = part.at[pl.ds(2 + 2 * way, 2), at]
        return remote(2 + way, piece, src, from_y2.at[pl.ds(2 * way, 2), at], (to_y_up, to_y_dn)[way])

    def z_copy(piece):
        at = pl.ds(first_row(piece), rows)
        return remote(4, piece, part.at[7 - zl, at], from_z.at[at], to_z_lo)

    def own_copy(way, piece):
        at = pl.ds(first_row(piece), rows)
        return remote(5 + way, piece, done.at[at], out_ref.at[dp, at], (to_z_hi, to_x_up, to_x_dn)[way])

    def own_local(piece):
        at = pl.ds(first_row(piece), rows)
        return pltpu.make_async_copy(done.at[at], out_ref.at[dp, at], loc_sem.at[piece])

    def pair_copy(way, piece):
        at = pl.ds(first_row(piece), rows)
        pair = x * 2 + 1 - zh
        return remote(8 + way, piece, out_ref.at[pair, at], out_ref.at[pair, at], (to_x_up, to_x_dn)[way])

    def forward_copy(way, piece):
        at = pl.ds(first_row(piece), rows)
        image = (x_dn * 2 + zh, x_up * 2 + 1 - zh)[way]
        return remote(10 + way, piece, out_ref.at[image, at], out_ref.at[image, at], (to_x_up, to_x_dn)[way])

    for slot in range(8):
        w_copy(slot).start()

    def start_tok(piece, carry):
        tok_copy(piece).start()
        return carry

    lax.fori_loop(0, PIECES // 2, start_tok, 0)
    text_own().start()
    pl.semaphore_wait(barrier, 11)
    core_copy().start()

    @pl.when(core == 0)
    def _():
        for step in range(1, 8):
            text_copy(step).start()

    def step_fn(it, carry):
        @pl.when(it < PIECES)
        def _():
            piece = it

            @pl.when(piece < PIECES // 2)
            def _():
                tok_copy(piece).wait()

            @pl.when(piece == PIECES // 2)
            def _():
                core_copy().wait_recv()

            at = pl.ds(first_row(piece), rows)
            for slot in range(8):
                @pl.when(it == 0)
                def _():
                    w_copy(slot).wait()

                part[slot, at, :] = jnp.dot(
                    tok[at, :], wgt[slot], preferred_element_type=F32
                ).astype(BF)
                if slot < 2:
                    y1_copy(slot, piece).start()

        @pl.when((it >= 1) & (it < PIECES + 1))
        def _():
            piece = it - 1
            at = pl.ds(first_row(piece), rows)
            for way, slot in ((0, 2), (1, 5)):
                y1_copy(way, piece).wait_recv()
                part[slot, at, :] = (
                    part[slot, at, :].astype(F32) + from_y1[way, at, :].astype(F32)
                ).astype(BF)
                y2_copy(way, piece).start()

        @pl.when((it >= 2) & (it < PIECES + 2))
        def _():
            piece = it - 2
            at = pl.ds(first_row(piece), rows)
            for way in range(2):
                y2_copy(way, piece).wait_recv()
            part[7 - zl, at, :] = (
                part[7 - zl, at, :].astype(F32)
                + from_y2[1 - zl, at, :].astype(F32)
                + from_y2[3 - zl, at, :].astype(F32)
            ).astype(BF)
            z_copy(piece).start()

        @pl.when((it >= 3) & (it < PIECES + 3))
        def _():
            piece = it - 3
            at = pl.ds(first_row(piece), rows)
            z_copy(piece).wait_recv()
            total = (
                part[6 + zl, at, :].astype(F32)
                + from_y2[zl, at, :].astype(F32)
                + from_y2[2 + zl, at, :].astype(F32)
                + from_z[at, :].astype(F32)
            )
            keys = total[:, :128]
            keys = keys * lax.rsqrt(jnp.mean(keys * keys, axis=-1, keepdims=True) + 1e-05)
            done[at, 0:128] = (keys * gain_ref[...]).astype(BF)
            done[at, 128:256] = total[:, 128:].astype(BF)
            for way in range(3):
                own_copy(way, piece).start()
            own_local(piece).start()

        @pl.when((it >= 4) & (it < PIECES + 4))
        def _():
            piece = it - 4
            own_copy(0, piece).wait_recv()
            for way in range(2):
                pair_copy(way, piece).start()

        @pl.when(it >= 5)
        def _():
            piece = it - 5
            own_copy(1, piece).wait_recv()
            pair_copy(1, piece).wait_recv()
            for way in range(2):
                forward_copy(way, piece).start()

        return carry

    lax.fori_loop(0, PIECES + 5, step_fn, 0)

    def finish(piece, carry):
        for way in range(2):
            y1_copy(way, piece).wait_send()
            y2_copy(way, piece).wait_send()
            pair_copy(way, piece).wait_send()
            forward_copy(way, piece).wait()
        for way in range(3):
            own_copy(way, piece).wait_send()
        z_copy(piece).wait_send()
        own_local(piece).wait()
        own_copy(2, piece).wait_recv()
        pair_copy(0, piece).wait_recv()
        return carry

    lax.fori_loop(0, PIECES, finish, 0)
    core_copy().wait_send()
    text_own().wait()

    @pl.when(core == 0)
    def _():
        for step in range(1, 8):
            text_copy(step).wait()


def image_pairs(tokens, weights, gain, text):
    half, width = tokens.shape
    heads = weights.shape[0]
    patches = half * 2
    any_spec = pl.BlockSpec(memory_space=pl.ANY)
    return pl.pallas_call(
        kv_kernel,
        name="kv",
        out_shape=[
            jax.ShapeDtypeStruct((8, patches, 256), BF),
            jax.ShapeDtypeStruct((8,) + text.shape, BF),
        ],
        in_specs=[any_spec, any_spec, pl.BlockSpec(memory_space=pltpu.VMEM), any_spec],
        out_specs=[any_spec, any_spec],
        scratch_shapes=[
            pltpu.VMEM((patches, width), BF),
            pltpu.VMEM((heads, width, 256), BF),
            pltpu.VMEM((heads, patches, 256), BF),
            pltpu.VMEM((2, patches, 256), BF),
            pltpu.VMEM((4, patches, 256), BF),
            pltpu.VMEM((patches, 256), BF),
            pltpu.VMEM((patches, 256), BF),
            pltpu.SemaphoreType.DMA((PIECES // 2,)),
            pltpu.SemaphoreType.DMA((8,)),
            pltpu.SemaphoreType.DMA((PIECES + 1,)),
            pltpu.SemaphoreType.DMA((2,)),
            pltpu.SemaphoreType.DMA((7,)),
            pltpu.SemaphoreType.DMA((7,)),
            pltpu.SemaphoreType.DMA((12, PIECES)),
            pltpu.SemaphoreType.DMA((12, PIECES)),
        ],
        compiler_params=pltpu.CompilerParams(
            collective_id=0, has_side_effects=True, vmem_limit_bytes=58 * 2**20
        ),
        cost_estimate=pl.CostEstimate(
            flops=2 * patches * width * heads * 256, bytes_accessed=40 * 2**20, transcendentals=0
        ),
    )(tokens, weights, gain, text)


Q_STEPS = 4
TILE_STEPS = 4
OUT_STEPS = 4
KEY_PARTS = ((0, 512), (512, 512), (1024, 576))


def layer_kernel(
    meta_ref, h_ref, gain_ref, wq_ref, qgain_ref, pair_ref, wo_ref, out_ref, acc, sq, query, total, norm, att
):
    step = pl.program_id(0)

    @pl.when(step < Q_STEPS)
    def _():
        @pl.when(step == 0)
        def _():
            acc[...] = jnp.zeros_like(acc)
            sq[...] = jnp.zeros_like(sq)

        for block in range(2):
            values = h_ref[block].astype(F32)
            sq[...] += jnp.sum(values * values, axis=-1, keepdims=True)
            scaled = (values * gain_ref[step * 2 + block]).astype(BF)
            acc[...] += jnp.dot(
                scaled, wq_ref[block * 1024:(block + 1) * 1024, :], preferred_element_type=F32
            )

        @pl.when(step == Q_STEPS - 1)
        def _():
            inverse = lax.rsqrt(sq[:, :1] * (1.0 / 8192.0) + 1e-05)
            for head in range(4):
                one = acc[:, head * 128:(head + 1) * 128] * inverse
                one = one * lax.rsqrt(jnp.mean(one * one, axis=-1, keepdims=True) + 1e-05)
                query[head * 128:(head + 1) * 128, :] = (one * qgain_ref[...] * 128.0 ** -0.5).astype(BF)
            total[...] = jnp.zeros_like(total)
            norm[...] = jnp.zeros_like(norm)

    tile = step - Q_STEPS

    @pl.when((tile >= 0) & (tile < TILE_STEPS) & (meta_ref[jnp.clip(tile, 0, 3) + 8] > 0))
    def _():
        for start, size in KEY_PARTS:
            scores = lax.dot_general(
                query[...], pair_ref[0, start:start + size, 0:128],
                (((1,), (1,)), ((), ())), preferred_element_type=F32,
            )
            expo = jnp.exp(scores)
            norm[...] += jnp.sum(expo, axis=-1, keepdims=True)
            total[...] += jnp.dot(
                expo.astype(BF), pair_ref[0, start:start + size, 128:256], preferred_element_type=F32
            )

    @pl.when(step >= Q_STEPS + TILE_STEPS)
    def _():
        @pl.when(step == Q_STEPS + TILE_STEPS)
        def _():
            for head in range(4):
                at = slice(head * 128, (head + 1) * 128)
                att[:, at] = (total[at, :] / norm[at, :1]).astype(BF)

        for block in range(2):
            out_ref[block] = jnp.dot(
                att[...], wo_ref[:, block * 1024:(block + 1) * 1024], preferred_element_type=F32
            ).astype(BF)


def layer_part(meta, hidden, gain, w_query, q_gain, pairs, w_out):
    attn_end = Q_STEPS + TILE_STEPS

    def out_step(i):
        return jnp.clip(i - attn_end, 0, OUT_STEPS - 1)

    def tile_map(i, m):
        j = jnp.clip(i - Q_STEPS, 0, TILE_STEPS - 1)
        return (m[j], m[j + 4], 0)

    return pl.pallas_call(
        layer_kernel,
        name="layer",
        out_shape=jax.ShapeDtypeStruct((8, 128, 1024), BF),
        grid_spec=pltpu.PrefetchScalarGridSpec(
            num_scalar_prefetch=1,
            grid=(Q_STEPS + TILE_STEPS + OUT_STEPS,),
            in_specs=[
                pl.BlockSpec((2, 128, 1024), lambda i, m: (jnp.minimum(i, Q_STEPS - 1), 0, 0)),
                pl.BlockSpec((8, 1, 1024), lambda i, m: (0, 0, 0)),
                pl.BlockSpec((2048, 512), lambda i, m: (jnp.minimum(i, Q_STEPS - 1), 0)),
                pl.BlockSpec((1, 128), lambda i, m: (0, 0)),
                pl.BlockSpec((1, TILE_TOK, 256), tile_map),
                pl.BlockSpec((512, 2048), lambda i, m: (0, out_step(i))),
            ],
            out_specs=pl.BlockSpec((2, 128, 1024), lambda i, m: (out_step(i), 0, 0)),
            scratch_shapes=[
                pltpu.VMEM((128, 512), F32),
                pltpu.VMEM((128, 128), F32),
                pltpu.VMEM((512, 128), BF),
                pltpu.VMEM((512, 128), F32),
                pltpu.VMEM((512, 128), F32),
                pltpu.VMEM((128, 512), BF),
            ],
        ),
        compiler_params=pltpu.CompilerParams(vmem_limit_bytes=48 * 2**20),
        cost_estimate=pl.CostEstimate(flops=4 * 10**9, bytes_accessed=20 * 2**20, transcendentals=3 * 10**6),
    )(meta, hidden, gain, w_query, q_gain, pairs, w_out)


def sum_kernel(
    first_core, second_core, part_ref, resid_ref, gate_ref, upd_ref, next_ref, came, rs_send, rs_recv, ag_send, ag_recv
):
    dp = lax.axis_index("dp")
    tensor = lax.axis_index("tensor")
    core = lax.axis_index("section")

    barrier = pltpu.get_barrier_semaphore()
    for step in range(8):
        peer = (tensor + step) % 8
        if step:
            pl.semaphore_signal(barrier, inc=1, device_id=(dp, peer, core), device_id_type=MESH)
        pl.semaphore_signal(barrier, inc=1, device_id=(dp, peer, 1 - core), device_id_type=MESH)
    pl.semaphore_wait(barrier, 15)

    def rs_copy(step):
        peer = (tensor + step) % 8
        return pltpu.make_async_remote_copy(
            src_ref=part_ref.at[peer], dst_ref=came.at[step - 1],
            send_sem=rs_send.at[step - 1], recv_sem=rs_recv.at[step - 1],
            device_id=(dp, peer, core), device_id_type=MESH,
        )

    def ag_copy(step):
        return pltpu.make_async_remote_copy(
            src_ref=upd_ref, dst_ref=next_ref.at[tensor],
            send_sem=ag_send.at[step], recv_sem=ag_recv.at[step],
            device_id=(dp, (tensor + step) % 8, 1 - core), device_id_type=MESH,
        )

    def reduce():
        for step in range(1, 8):
            rs_copy(step).start()
        total = part_ref[tensor].astype(F32)
        for step in range(1, 8):
            rs_copy(step).wait_recv()
            total = total + came[step - 1].astype(F32)
        upd_ref[...] = (resid_ref[...].astype(F32) + gate_ref[...] * total).astype(BF)

    if first_core and second_core:
        reduce()
    elif first_core:
        pl.when(core == 0)(reduce)
    else:
        pl.when(core == 1)(reduce)
    if first_core:
        @pl.when(core == 0)
        def _():
            for step in range(8):
                ag_copy(step).start()
            for step in range(8):
                ag_copy(step).wait_send()

        @pl.when(core == 1)
        def _():
            for step in range(8):
                ag_copy(step).wait_recv()

    def drain():
        for step in range(1, 8):
            rs_copy(step).wait_send()

    if first_core and second_core:
        drain()
    elif first_core:
        pl.when(core == 0)(drain)
    else:
        pl.when(core == 1)(drain)


def sum_and_pass(tick, first_core, second_core, part, resid, gate):
    vmem = pl.BlockSpec(memory_space=pltpu.VMEM)
    return pl.pallas_call(
        functools.partial(sum_kernel, first_core, second_core),
        name="sum" + str(tick),
        out_shape=[jax.ShapeDtypeStruct((128, 1024), BF), jax.ShapeDtypeStruct((8, 128, 1024), BF)],
        in_specs=[vmem] * 3,
        out_specs=[vmem] * 2,
        scratch_shapes=[
            pltpu.VMEM((7, 128, 1024), BF),
            pltpu.SemaphoreType.DMA((7,)),
            pltpu.SemaphoreType.DMA((7,)),
            pltpu.SemaphoreType.DMA((8,)),
            pltpu.SemaphoreType.DMA((8,)),
        ],
        compiler_params=pltpu.CompilerParams(
            collective_id=1 + tick, has_side_effects=True, vmem_limit_bytes=48 * 2**20
        ),
    )(part, resid, gate)


def tile_plan(chosen, valid_tiles):
    first, second = chosen[0], chosen[1]
    two = valid_tiles[first] > 1
    other = second != first
    two_other = other & (valid_tiles[second] > 1)
    one = jnp.int32(1)
    zero = jnp.int32(0)
    last_tile = jnp.where(two, one, zero)
    image = [first, first, jnp.where(other, second, first)]
    image.append(image[2])
    third_tile = jnp.where(other, zero, last_tile)
    tile = [zero, last_tile, third_tile, jnp.where(two_other, one, third_tile)]
    use = [one, last_tile, jnp.where(other, one, zero), jnp.where(two_other, one, zero)]
    return jnp.stack(image + tile + use).astype(jnp.int32)


def local(
    text_hidden,
    image_tokens,
    attn_gain,
    w_query,
    w_keyval,
    q_gain,
    k_gain,
    w_out,
    gate,
    image_choice,
    valid_tiles,
):
    core = lax.axis_index("section")
    tensor = lax.axis_index("tensor")
    text = text_hidden[:, 0]
    weights = jnp.transpose(w_keyval[0], (1, 0, 2))
    pairs, text_all = image_pairs(image_tokens[0], weights, k_gain, text)
    gate_row = jnp.broadcast_to(jnp.tanh(gate)[:, None], (1, 1024))
    gain = attn_gain.reshape(8, 1, 1024)
    received = None
    results = []
    for tick in range(3):
        own = text_all[:, min(tick, 1)]
        resid = text[min(tick, 1)]
        if received is None:
            hidden = own
        else:
            hidden = jnp.where(core == 0, own, received)
            resid = jnp.where(core == 0, resid, lax.dynamic_index_in_dim(received, tensor, 0, keepdims=False))
        chosen = jnp.where(core == 0, image_choice[min(tick, 1), 0], image_choice[max(tick - 1, 0), 0])
        meta = tile_plan(chosen, valid_tiles)
        part = layer_part(meta, hidden, gain, w_query[0], q_gain, pairs, w_out[0])
        updated, received = sum_and_pass(tick, tick < 2, tick > 0, part, resid, gate_row)
        results.append(updated)
    slots = [jnp.where(core == 0, results[batch], results[batch + 1]) for batch in range(2)]
    return jnp.stack(slots)[None, :, None]


def solution(mesh):
    placed = (
        P(None, "dp", None, "tensor"),
        P("dp", "section", "tensor"),
        P("section", None),
        P("section", None, "tensor"),
        P("section", "tensor", None, None),
        P("section", None),
        P("section", None),
        P("section", "tensor", None),
        P("section"),
        P(None, "dp", None),
        P(),
    )
    return jax.shard_map(
        local,
        mesh=mesh,
        in_specs=placed,
        out_specs=P("section", None, "dp", None, "tensor"),
        check_vma=False,
    )
```

```python
import functools

import jax
import jax.numpy as jnp
from jax import lax
from jax.experimental import pallas as pl
from jax.experimental.pallas import tpu as pltpu
from jax.sharding import PartitionSpec as P

TILE_TOK = 1600
PIECES = 20
EARLY = (1, 3, 4)
LATE = (2, 5, 6, 7)
MESH = pl.DeviceIdType.MESH
BF = jnp.bfloat16
F32 = jnp.float32


def position():
    dp = lax.axis_index("dp")
    tensor = lax.axis_index("tensor")
    return dp // 2, dp % 2, tensor // 4, tensor % 4, lax.axis_index("section")


def device(x, zh, zl, y, core):
    return (x * 2 + zh, zl * 4 + y, core)


def kv_kernel(
    tok_ref, w_ref, gain_ref, text_ref, wq_ref, wo_ref, par_ref,
    pairs_ref, text_out_ref, wq_out_ref, wo_out_ref, par_out_ref,
    tok, wgt, part, from_y1, from_y2, from_z, done,
    tok_sem, w_sem, loc_sem, core_send, core_recv, text_send, text_recv, send, recv,
):
    x, zh, zl, y, core = position()
    dp = x * 2 + zh
    tensor = zl * 4 + y
    half = tok_ref.shape[0]
    out_ref = pairs_ref.at[core]
    rows = half * 2 // PIECES
    y_up, y_dn = (y + 1) % 4, (y + 3) % 4
    x_up, x_dn = (x + 1) % 4, (x + 3) % 4
    to_y_up = device(x, zh, zl, y_up, core)
    to_y_dn = device(x, zh, zl, y_dn, core)
    to_z_lo = device(x, zh, 1 - zl, y, core)
    to_z_hi = device(x, 1 - zh, zl, y, core)
    to_x_up = device(x_up, zh, zl, y, core)
    to_x_dn = device(x_dn, zh, zl, y, core)
    to_core = device(x, zh, zl, y, 1 - core)

    def tensor_peer(step):
        return (dp, (tensor + step) % 8, core)

    barrier = pltpu.get_barrier_semaphore()
    for peer in [to_z_hi, to_x_up, to_x_dn, to_core] + [tensor_peer(s) for s in range(1, 8)]:
        pl.semaphore_signal(barrier, inc=1, device_id=peer, device_id_type=MESH)

    def first_row(piece):
        return pl.multiple_of(((piece + core * (PIECES // 2)) % PIECES) * rows, rows)

    def head_of(slot):
        ring = (y + 2) % 4 if slot < 2 else y_up if slot < 4 else y_dn if slot < 6 else y
        return (slot % 2) * 4 + ring

    def tok_copy(piece):
        return pltpu.make_async_copy(
            tok_ref.at[pl.ds(pl.multiple_of(piece * rows, rows), rows)],
            tok.at[pl.ds(pl.multiple_of(core * half + piece * rows, rows), rows)],
            tok_sem.at[piece],
        )

    def w_copy(slot):
        return pltpu.make_async_copy(w_ref.at[head_of(slot)], wgt.at[slot], w_sem.at[slot])

    def to_other_core(kind):
        src, dst = (
            (tok_ref, tok.at[pl.ds(pl.multiple_of(core * half, half), half)]),
            (par_ref, par_out_ref),
            (wq_ref, wq_out_ref),
            (wo_ref, wo_out_ref),
        )[kind]
        return pltpu.make_async_remote_copy(
            src_ref=src, dst_ref=dst, send_sem=core_send.at[kind], recv_sem=core_recv.at[kind],
            device_id=to_core, device_id_type=MESH,
        )

    def text_copy(step):
        return pltpu.make_async_remote_copy(
            src_ref=text_ref.at[core], dst_ref=text_out_ref.at[tensor],
            send_sem=text_send.at[step - 1], recv_sem=text_recv.at[step - 1],
            device_id=tensor_peer(step), device_id_type=MESH,
        )

    def remote(kind, piece, src, dst, peer):
        return pltpu.make_async_remote_copy(
            src_ref=src, dst_ref=dst,
            send_sem=send.at[kind, piece], recv_sem=recv.at[kind, piece],
            device_id=peer, device_id_type=MESH,
        )

    def y1_copy(way, piece):
        at = pl.ds(first_row(piece), rows)
        return remote(way, piece, part.at[way, at], from_y1.at[way, at], (to_y_up, to_y_dn)[way])

    def y2_copy(way, piece):
        at = pl.ds(first_row(piece), rows)
        src = part.at[pl.ds(2 + 2 * way, 2), at]
        return remote(2 + way, piece, src, from_y2.at[pl.ds(2 * way, 2), at], (to_y_up, to_y_dn)[way])

    def z_copy(piece):
        at = pl.ds(first_row(piece), rows)
        return remote(4, piece, part.at[7 - zl, at], from_z.at[at], to_z_lo)

    def own_copy(way, piece):
        at = pl.ds(first_row(piece), rows)
        return remote(5 + way, piece, done.at[at], out_ref.at[dp, at], (to_z_hi, to_x_up, to_x_dn)[way])

    def own_local(piece):
        at = pl.ds(first_row(piece), rows)
        return pltpu.make_async_copy(done.at[at], out_ref.at[dp, at], loc_sem.at[piece])

    def pair_copy(way, piece):
        at = pl.ds(first_row(piece), rows)
        pair = x * 2 + 1 - zh
        return remote(8 + way, piece, out_ref.at[pair, at], out_ref.at[pair, at], (to_x_up, to_x_dn)[way])

    def forward_copy(way, piece):
        at = pl.ds(first_row(piece), rows)
        image = (x_dn * 2 + zh, x_up * 2 + 1 - zh)[way]
        return remote(10 + way, piece, out_ref.at[image, at], out_ref.at[image, at], (to_x_up, to_x_dn)[way])

    def mirror(kind, image, piece):
        at = pl.ds(first_row(piece), rows)
        src = done.at[at] if kind == 0 else out_ref.at[image, at]
        return remote(12 + kind, piece, src, out_ref.at[image, at], to_core)

    def mirrors(piece):
        ring = ((x, zh), (x, 1 - zh), (x_dn, zh), (x_up, zh), (x_dn, 1 - zh), (x_up, 1 - zh))
        images = [a * 2 + b for a, b in ring] + [((x + 2) % 4) * 2 + zh, ((x + 2) % 4) * 2 + 1 - zh]
        return [functools.partial(mirror, kind, image, piece) for kind, image in enumerate(images)]

    for slot in range(8):
        w_copy(slot).start()

    def start_tok(piece, carry):
        tok_copy(piece).start()
        return carry

    lax.fori_loop(0, PIECES // 2, start_tok, 0)
    pl.semaphore_wait(barrier, 11)
    to_other_core(0).start()
    for step in EARLY:
        text_copy(step).start()
    for kind in range(1, 4):
        to_other_core(kind).start()

    def step_fn(it, carry):
        @pl.when(it < PIECES)
        def _():
            piece = it

            @pl.when(piece < PIECES // 2)
            def _():
                tok_copy(piece).wait()

            @pl.when(piece == PIECES // 2)
            def _():
                to_other_core(0).wait_recv()

            at = pl.ds(first_row(piece), rows)
            for slot in range(8):
                @pl.when(it == 0)
                def _():
                    w_copy(slot).wait()

                part[slot, at, :] = jnp.dot(
                    tok[at, :], wgt[slot], preferred_element_type=F32
                ).astype(BF)
                if slot < 2:
                    y1_copy(slot, piece).start()

        @pl.when((it >= 1) & (it < PIECES + 1))
        def _():
            piece = it - 1
            at = pl.ds(first_row(piece), rows)
            for way, slot in ((0, 2), (1, 5)):
                y1_copy(way, piece).wait_recv()
                part[slot, at, :] = (
                    part[slot, at, :].astype(F32) + from_y1[way, at, :].astype(F32)
                ).astype(BF)
                y2_copy(way, piece).start()

            @pl.when(piece == PIECES - 1)
            def _():
                for step in LATE:
                    text_copy(step).start()

        @pl.when((it >= 2) & (it < PIECES + 2))
        def _():
            piece = it - 2
            at = pl.ds(first_row(piece), rows)
            for way in range(2):
                y2_copy(way, piece).wait_recv()
            part[7 - zl, at, :] = (
                part[7 - zl, at, :].astype(F32)
                + from_y2[1 - zl, at, :].astype(F32)
                + from_y2[3 - zl, at, :].astype(F32)
            ).astype(BF)
            z_copy(piece).start()

        @pl.when((it >= 3) & (it < PIECES + 3))
        def _():
            piece = it - 3
            at = pl.ds(first_row(piece), rows)
            z_copy(piece).wait_recv()
            total = (
                part[6 + zl, at, :].astype(F32)
                + from_y2[zl, at, :].astype(F32)
                + from_y2[2 + zl, at, :].astype(F32)
                + from_z[at, :].astype(F32)
            )
            keys = total[:, :128]
            keys = keys * lax.rsqrt(jnp.mean(keys * keys, axis=-1, keepdims=True) + 1e-05)
            done[at, 0:128] = (keys * gain_ref[...]).astype(BF)
            done[at, 128:256] = total[:, 128:].astype(BF)
            for way in range(3):
                own_copy(way, piece).start()
            own_local(piece).start()
            mirrors(piece)[0]().start()

        @pl.when((it >= 4) & (it < PIECES + 4))
        def _():
            piece = it - 4
            own_copy(0, piece).wait_recv()
            for way in range(2):
                pair_copy(way, piece).start()
            mirrors(piece)[1]().start()

        @pl.when((it >= 5) & (it < PIECES + 5))
        def _():
            piece = it - 5
            own_copy(1, piece).wait_recv()
            pair_copy(1, piece).wait_recv()
            for way in range(2):
                forward_copy(way, piece).start()
            own_copy(2, piece).wait_recv()
            pair_copy(0, piece).wait_recv()
            for kind in range(2, 6):
                mirrors(piece)[kind]().start()

        @pl.when(it >= 6)
        def _():
            piece = it - 6
            for way in range(2):
                forward_copy(way, piece).wait_recv()
            for kind in range(6, 8):
                mirrors(piece)[kind]().start()

        return carry

    lax.fori_loop(0, PIECES + 6, step_fn, 0)

    def finish(piece, carry):
        for way in range(2):
            y1_copy(way, piece).wait_send()
            y2_copy(way, piece).wait_send()
            pair_copy(way, piece).wait_send()
            forward_copy(way, piece).wait_send()
        for way in range(3):
            own_copy(way, piece).wait_send()
        z_copy(piece).wait_send()
        own_local(piece).wait()
        for copy in mirrors(piece):
            copy().wait()
        return carry

    lax.fori_loop(0, PIECES, finish, 0)
    to_other_core(0).wait_send()
    for kind in range(1, 4):
        to_other_core(kind).wait()
    for step in range(1, 8):
        text_copy(step).wait()


def image_pairs(tokens, weights, gain, text, w_query, w_out, params):
    half, width = tokens.shape
    heads = weights.shape[0]
    patches = half * 2
    any_spec = pl.BlockSpec(memory_space=pl.ANY)

    def like(array):
        return jax.ShapeDtypeStruct(array.shape, array.dtype)

    return pl.pallas_call(
        kv_kernel,
        name="kv",
        out_shape=[
            jax.ShapeDtypeStruct((2, 8, patches, 256), BF),
            jax.ShapeDtypeStruct((8,) + text.shape[1:], BF),
            like(w_query),
            like(w_out),
            like(params),
        ],
        in_specs=[any_spec, any_spec, pl.BlockSpec(memory_space=pltpu.VMEM)] + [any_spec] * 4,
        out_specs=[any_spec] * 5,
        scratch_shapes=[
            pltpu.VMEM((patches, width), BF),
            pltpu.VMEM((heads, width, 256), BF),
            pltpu.VMEM((heads, patches, 256), BF),
            pltpu.VMEM((2, patches, 256), BF),
            pltpu.VMEM((4, patches, 256), BF),
            pltpu.VMEM((patches, 256), BF),
            pltpu.VMEM((patches, 256), BF),
            pltpu.SemaphoreType.DMA((PIECES // 2,)),
            pltpu.SemaphoreType.DMA((8,)),
            pltpu.SemaphoreType.DMA((PIECES,)),
            pltpu.SemaphoreType.DMA((4,)),
            pltpu.SemaphoreType.DMA((4,)),
            pltpu.SemaphoreType.DMA((7,)),
            pltpu.SemaphoreType.DMA((7,)),
            pltpu.SemaphoreType.DMA((20, PIECES)),
            pltpu.SemaphoreType.DMA((20, PIECES)),
        ],
        compiler_params=pltpu.CompilerParams(
            collective_id=0, has_side_effects=True, vmem_limit_bytes=58 * 2**20
        ),
        cost_estimate=pl.CostEstimate(
            flops=2 * patches * width * heads * 256, bytes_accessed=40 * 2**20, transcendentals=0
        ),
    )(tokens, weights, gain, text, w_query, w_out, params)


KEY_PARTS = ((0, 512), (512, 512), (1024, 576))


class LayerLoad:
    def __init__(self, layer, own, other, dst, sem):
        self.here = lax.axis_index("section") == layer
        self.own = pltpu.make_async_copy(own, dst, sem)
        self.other = pltpu.make_async_copy(other, dst, sem)

    def start(self):
        pl.when(self.here)(lambda: self.own.start())
        pl.when(jnp.logical_not(self.here))(lambda: self.other.start())

    def wait(self):
        self.own.wait()


def add_to_query(acc, sq, block, gain, weights):
    values = block.astype(F32)
    sq[...] += jnp.sum(values * values, axis=-1, keepdims=True)
    acc[...] += jnp.dot((values * gain).astype(BF), weights, preferred_element_type=F32)


def finish_query(acc, sq, q_gain, query):
    inverse = lax.rsqrt(sq[:, :1] * (1.0 / 8192.0) + 1e-05)
    for head in range(4):
        one = acc[:, head * 128:(head + 1) * 128] * inverse
        one = one * lax.rsqrt(jnp.mean(one * one, axis=-1, keepdims=True) + 1e-05)
        query[head * 128:(head + 1) * 128, :] = (one * q_gain * 128.0 ** -0.5).astype(BF)


def attend(layer, choice_ref, valid_ref, query, pairs_ref, att_ref, tiles, total, norm, sem, before=None):
    core = lax.axis_index("section")
    first = choice_ref[2 * core]
    second = choice_ref[2 * core + 1]
    other = second != first
    plan = (
        (first, 0, None),
        (first, 1, valid_ref[first] > 1),
        (second, 0, other),
        (second, 1, other & (valid_ref[second] > 1)),
    )

    def copy(slot):
        image, tile, _ = plan[slot]
        return pltpu.make_async_copy(
            pairs_ref.at[layer, image, pl.ds(tile * TILE_TOK, TILE_TOK)], tiles.at[slot], sem.at[slot]
        )

    def run(slot, fn):
        allowed = plan[slot][2]
        if allowed is None:
            fn()
        else:
            pl.when(allowed)(fn)

    for slot in range(4):
        run(slot, lambda slot=slot: copy(slot).start())
    total[...] = jnp.zeros_like(total)
    norm[...] = jnp.zeros_like(norm)
    if before is not None:
        before()

    def one(slot):
        copy(slot).wait()
        for start, size in KEY_PARTS:
            scores = lax.dot_general(
                query[...], tiles[slot, start:start + size, 0:128],
                (((1,), (1,)), ((), ())), preferred_element_type=F32,
            )
            expo = jnp.exp(scores)
            norm[...] += jnp.sum(expo, axis=-1, keepdims=True)
            total[...] += jnp.dot(
                expo.astype(BF), tiles[slot, start:start + size, 128:256], preferred_element_type=F32
            )

    for slot in range(4):
        run(slot, functools.partial(one, slot))
    for head in range(4):
        at = slice(head * 128, (head + 1) * 128)
        att_ref[:, at] = (total[at, :] / norm[at, :1]).astype(BF)


def first_attention(
    choice_ref, valid_ref, pairs_ref, text_ref, text_all_ref, wq_ref, wq_other_ref, par_ref, par_other_ref, att_ref,
    tiles, total, norm, sem, hidden, wq, par, acc, sq, query, load_sem, wq_sem,
):
    core = lax.axis_index("section")
    tensor = lax.axis_index("tensor")
    par_load = LayerLoad(0, par_ref, par_other_ref, par, load_sem.at[8])
    par_load.start()
    chunks = []
    for step in range(8):
        block = (tensor + step) % 8
        src = text_ref.at[core] if step == 0 else text_all_ref.at[block]
        at = pl.ds(pl.multiple_of(block * 1024, 1024), 1024)
        chunks.append((
            block,
            pltpu.make_async_copy(src, hidden.at[step], load_sem.at[step]),
            LayerLoad(0, wq_ref.at[at], wq_other_ref.at[at], wq.at[step], wq_sem.at[step]),
        ))
        chunks[-1][1].start()
        chunks[-1][2].start()

    def before():
        acc[...] = jnp.zeros_like(acc)
        sq[...] = jnp.zeros_like(sq)
        par_load.wait()
        for step, (block, text_load, wq_load) in enumerate(chunks):
            text_load.wait()
            wq_load.wait()
            add_to_query(acc, sq, hidden[step], par[pl.ds(block, 1), :], wq[step])
        finish_query(acc, sq, par[9:10, 0:128], query)

    attend(0, choice_ref, valid_ref, query, pairs_ref, att_ref, tiles, total, norm, sem, before)


def second_attention(choice_ref, valid_ref, pairs_ref, query_ref, att_ref, tiles, total, norm, sem):
    attend(1, choice_ref, valid_ref, query_ref, pairs_ref, att_ref, tiles, total, norm, sem)


ATTEND_SCRATCH = [
    pltpu.VMEM((4, TILE_TOK, 256), BF),
    pltpu.VMEM((512, 128), F32),
    pltpu.VMEM((512, 128), F32),
    pltpu.SemaphoreType.DMA((4,)),
]


def attention_first(choice, valid, pairs, text, text_all, wq, wq_other, par, par_other):
    any_spec = pl.BlockSpec(memory_space=pl.ANY)
    smem = pl.BlockSpec(memory_space=pltpu.SMEM)
    return pl.pallas_call(
        first_attention,
        name="attend0",
        out_shape=jax.ShapeDtypeStruct((128, 512), BF),
        in_specs=[smem, smem] + [any_spec] * 7,
        out_specs=pl.BlockSpec(memory_space=pltpu.VMEM),
        scratch_shapes=ATTEND_SCRATCH + [
            pltpu.VMEM((8, 128, 1024), BF),
            pltpu.VMEM((8, 1024, 512), BF),
            pltpu.VMEM((16, 1024), F32),
            pltpu.VMEM((128, 512), F32),
            pltpu.VMEM((128, 128), F32),
            pltpu.VMEM((512, 128), BF),
            pltpu.SemaphoreType.DMA((9,)),
            pltpu.SemaphoreType.DMA((8,)),
        ],
        compiler_params=pltpu.CompilerParams(vmem_limit_bytes=48 * 2**20),
        cost_estimate=pl.CostEstimate(flops=3 * 10**9, bytes_accessed=14 * 2**20, transcendentals=3 * 10**6),
    )(choice, valid, pairs, text, text_all, wq, wq_other, par, par_other)


def attention_second(choice, valid, pairs, query):
    any_spec = pl.BlockSpec(memory_space=pl.ANY)
    smem = pl.BlockSpec(memory_space=pltpu.SMEM)
    vmem = pl.BlockSpec(memory_space=pltpu.VMEM)
    return pl.pallas_call(
        second_attention,
        name="attend1",
        out_shape=jax.ShapeDtypeStruct((128, 512), BF),
        in_specs=[smem, smem, any_spec, vmem],
        out_specs=vmem,
        scratch_shapes=ATTEND_SCRATCH,
        compiler_params=pltpu.CompilerParams(vmem_limit_bytes=48 * 2**20),
        cost_estimate=pl.CostEstimate(flops=2 * 10**9, bytes_accessed=4 * 2**20, transcendentals=3 * 10**6),
    )(choice, valid, pairs, query)


def project_and_sum(layer, att_ref, wo_ref, wo_other_ref, wo, part, from_y1, from_y2, from_z, wo_sem, send, recv, greet):
    x, zh, zl, y, core = position()
    y_up, y_dn = (y + 1) % 4, (y + 3) % 4
    to_y_up = device(x, zh, zl, y_up, core)
    to_y_dn = device(x, zh, zl, y_dn, core)
    to_z_lo = device(x, zh, 1 - zl, y, core)

    def block_of(slot):
        ring = (y + 2) % 4 if slot < 2 else y_up if slot < 4 else y_dn if slot < 6 else y
        return (slot % 2) * 4 + ring

    order = (0, 1, 4, 3, 2, 5, 6, 7)
    loads = {}
    for slot in order:
        at = pl.ds(pl.multiple_of(block_of(slot) * 1024, 1024), 1024)
        loads[slot] = LayerLoad(layer, wo_ref.at[:, at], wo_other_ref.at[:, at], wo.at[slot], wo_sem.at[slot])
        loads[slot].start()

    def remote(kind, src, dst, peer):
        return pltpu.make_async_remote_copy(
            src_ref=src, dst_ref=dst, send_sem=send.at[kind], recv_sem=recv.at[kind],
            device_id=peer, device_id_type=MESH,
        )

    far = [remote(0, part.at[0], from_y1.at[0], to_y_up), remote(1, part.at[1], from_y1.at[1], to_y_dn)]
    near = {
        4: remote(2, part.at[4], from_y2.at[2], to_y_dn),
        3: remote(3, part.at[3], from_y2.at[1], to_y_up),
        2: remote(4, part.at[2], from_y2.at[0], to_y_up),
        5: remote(5, part.at[5], from_y2.at[3], to_y_dn),
    }
    across = remote(6, part.at[7 - zl], from_z, to_z_lo)

    def project(slot):
        loads[slot].wait()
        part[slot] = jnp.dot(att_ref[...], wo[slot], preferred_element_type=F32).astype(BF)

    project(0)
    greet()
    far[0].start()
    project(1)
    far[1].start()
    for slot in (4, 3):
        project(slot)
        near[slot].start()
    for slot in (2, 5, 6, 7):
        project(slot)
    for way, slot in ((0, 2), (1, 5)):
        far[way].wait_recv()
        part[slot] = (part[slot].astype(F32) + from_y1[way].astype(F32)).astype(BF)
        near[slot].start()
    for slot in (4, 3, 2, 5):
        near[slot].wait_recv()
    part[7 - zl] = (
        part[7 - zl].astype(F32) + from_y2[1 - zl].astype(F32) + from_y2[3 - zl].astype(F32)
    ).astype(BF)
    across.start()
    total = part[6 + zl].astype(F32) + from_y2[zl].astype(F32) + from_y2[2 + zl].astype(F32)
    across.wait_recv()
    total = total + from_z[...].astype(F32)

    def drain():
        for copy in far + [near[slot] for slot in (4, 3, 2, 5)] + [across]:
            copy.wait_send()

    return total, drain


SUM_SCRATCH = [
    pltpu.VMEM((8, 512, 1024), BF),
    pltpu.VMEM((8, 128, 1024), BF),
    pltpu.VMEM((2, 128, 1024), BF),
    pltpu.VMEM((4, 128, 1024), BF),
    pltpu.VMEM((128, 1024), BF),
    pltpu.SemaphoreType.DMA((8,)),
    pltpu.SemaphoreType.DMA((7,)),
    pltpu.SemaphoreType.DMA((7,)),
]


def greeting(peers):
    barrier = pltpu.get_barrier_semaphore()
    for peer in peers:
        pl.semaphore_signal(barrier, inc=1, device_id=peer, device_id_type=MESH)
    pl.semaphore_wait(barrier, len(peers))


def middle_kernel(
    att_ref, text_ref, wo_ref, wo_other_ref, wq_ref, wq_other_ref, par_ref, par_other_ref, query_ref, upd_ref,
    wo, part, from_y1, from_y2, from_z, wo_sem, send, recv,
    hidden, wq, par, acc, sq, wq_sem, ag_send, ag_recv, par_sem,
):
    x, zh, zl, y, core = position()
    y_up, y_dn = (y + 1) % 4, (y + 3) % 4
    to_y_up = device(x, zh, zl, y_up, core)
    to_y_dn = device(x, zh, zl, y_dn, core)
    to_z_lo = device(x, zh, 1 - zl, y, core)
    other = 1 - zl
    par_copies = [
        LayerLoad(layer, par_ref, par_other_ref, par.at[layer], par_sem.at[layer]) for layer in range(2)
    ]
    for copy in par_copies:
        copy.start()

    total, drain = project_and_sum(
        0, att_ref, wo_ref, wo_other_ref, wo, part, from_y1, from_y2, from_z, wo_sem, send, recv,
        lambda: greeting([to_y_up, to_y_dn, to_z_lo]),
    )
    order = [
        zl * 4 + y, zl * 4 + y_dn, zl * 4 + y_up, other * 4 + y,
        other * 4 + y_dn, other * 4 + y_up, zl * 4 + (y + 2) % 4, other * 4 + (y + 2) % 4,
    ]
    chunks = []
    for k, block in enumerate(order):
        at = pl.ds(pl.multiple_of(block * 1024, 1024), 1024)
        chunks.append(LayerLoad(1, wq_ref.at[at], wq_other_ref.at[at], wq.at[k], wq_sem.at[k]))
        chunks[k].start()
    for copy in par_copies:
        copy.wait()
    own = order[0]
    hidden[own] = (text_ref[core].astype(F32) + par[0, 8:9, :] * total).astype(BF)

    def remote(kind, block, peer, half=None):
        ref = hidden.at[block] if half is None else hidden.at[block, pl.ds(half * 64, 64)]
        return pltpu.make_async_remote_copy(
            src_ref=ref, dst_ref=ref, send_sem=ag_send.at[kind], recv_sem=ag_recv.at[kind],
            device_id=peer, device_id_type=MESH,
        )

    up, down, cross = remote(0, own, to_y_up), remote(1, own, to_y_dn), remote(2, own, to_z_lo)
    up.start()
    down.start()
    cross.start()
    upd_ref[...] = hidden[own]
    acc[...] = jnp.zeros_like(acc)
    sq[...] = jnp.zeros_like(sq)

    def use(k):
        chunks[k].wait()
        block = order[k]
        add_to_query(acc, sq, hidden[block], par[1, pl.ds(block, 1), :], wq[k])

    use(0)
    cross.wait_recv()
    cross_up, cross_down = remote(3, order[3], to_y_up), remote(4, order[3], to_y_dn)
    cross_up.start()
    cross_down.start()
    up.wait_recv()
    far_up = remote(5, order[1], to_y_up, 0)
    far_up.start()
    down.wait_recv()
    far_down = remote(6, order[2], to_y_dn, 1)
    far_down.start()
    use(1)
    use(2)
    use(3)
    cross_up.wait_recv()
    cross_far_up = remote(7, order[4], to_y_up, 0)
    cross_far_up.start()
    cross_down.wait_recv()
    cross_far_down = remote(8, order[5], to_y_dn, 1)
    cross_far_down.start()
    use(4)
    use(5)
    far_up.wait_recv()
    far_down.wait_recv()
    use(6)
    cross_far_up.wait_recv()
    cross_far_down.wait_recv()
    use(7)
    finish_query(acc, sq, par[1, 9:10, 0:128], query_ref)
    drain()
    for copy in (up, down, cross, cross_up, cross_down, far_up, far_down, cross_far_up, cross_far_down):
        copy.wait_send()


def last_kernel(
    att_ref, upd_ref, wo_ref, wo_other_ref, par_ref, par_other_ref, out_ref, wo, part, from_y1, from_y2, from_z, wo_sem, send, recv,
    par, last, core_send, core_recv, par_sem,
):
    x, zh, zl, y, core = position()
    to_y_up = device(x, zh, zl, (y + 1) % 4, core)
    to_y_dn = device(x, zh, zl, (y + 3) % 4, core)
    to_z_lo = device(x, zh, 1 - zl, y, core)
    to_core = device(x, zh, zl, y, 1 - core)
    par_copy = LayerLoad(1, par_ref, par_other_ref, par, par_sem.at[0])
    par_copy.start()
    send_first = pltpu.make_async_remote_copy(
        src_ref=upd_ref, dst_ref=out_ref.at[1], send_sem=core_send.at[0], recv_sem=core_recv.at[0],
        device_id=to_core, device_id_type=MESH,
    )
    send_last = pltpu.make_async_remote_copy(
        src_ref=last, dst_ref=out_ref.at[0], send_sem=core_send.at[1], recv_sem=core_recv.at[1],
        device_id=to_core, device_id_type=MESH,
    )

    def greet():
        greeting([to_y_up, to_y_dn, to_z_lo, to_core])

        @pl.when(core == 1)
        def _():
            send_first.start()

    total, drain = project_and_sum(
        1, att_ref, wo_ref, wo_other_ref, wo, part, from_y1, from_y2, from_z, wo_sem, send, recv, greet
    )
    par_copy.wait()
    new = (upd_ref[...].astype(F32) + par[8:9, :] * total).astype(BF)

    @pl.when(core == 0)
    def _():
        last[...] = new
        send_last.start()
        out_ref[0] = upd_ref[...]
        send_first.wait_recv()
        send_last.wait_send()

    @pl.when(core == 1)
    def _():
        out_ref[1] = new
        send_first.wait_send()
        send_last.wait_recv()

    drain()


def middle(att, text, *weights):
    any_spec = pl.BlockSpec(memory_space=pl.ANY)
    vmem = pl.BlockSpec(memory_space=pltpu.VMEM)
    return pl.pallas_call(
        middle_kernel,
        name="middle",
        out_shape=[jax.ShapeDtypeStruct((512, 128), BF), jax.ShapeDtypeStruct((128, 1024), BF)],
        in_specs=[vmem, vmem] + [any_spec] * 6,
        out_specs=[vmem] * 2,
        scratch_shapes=SUM_SCRATCH + [
            pltpu.VMEM((8, 128, 1024), BF),
            pltpu.VMEM((8, 1024, 512), BF),
            pltpu.VMEM((2, 16, 1024), F32),
            pltpu.VMEM((128, 512), F32),
            pltpu.VMEM((128, 128), F32),
            pltpu.SemaphoreType.DMA((8,)),
            pltpu.SemaphoreType.DMA((9,)),
            pltpu.SemaphoreType.DMA((9,)),
            pltpu.SemaphoreType.DMA((2,)),
        ],
        compiler_params=pltpu.CompilerParams(
            collective_id=1, has_side_effects=True, vmem_limit_bytes=56 * 2**20
        ),
    )(att, text, *weights)


def last_step(att, upd, *weights):
    any_spec = pl.BlockSpec(memory_space=pl.ANY)
    vmem = pl.BlockSpec(memory_space=pltpu.VMEM)
    return pl.pallas_call(
        last_kernel,
        name="last",
        out_shape=jax.ShapeDtypeStruct((2, 128, 1024), BF),
        in_specs=[vmem, vmem] + [any_spec] * 4,
        out_specs=vmem,
        scratch_shapes=SUM_SCRATCH + [
            pltpu.VMEM((16, 1024), F32),
            pltpu.VMEM((128, 1024), BF),
            pltpu.SemaphoreType.DMA((2,)),
            pltpu.SemaphoreType.DMA((2,)),
            pltpu.SemaphoreType.DMA((1,)),
        ],
        compiler_params=pltpu.CompilerParams(
            collective_id=2, has_side_effects=True, vmem_limit_bytes=56 * 2**20
        ),
    )(att, upd, *weights)


def local(
    text_hidden,
    image_tokens,
    attn_gain,
    w_query,
    w_keyval,
    q_gain,
    k_gain,
    w_out,
    gate,
    image_choice,
    valid_tiles,
):
    text = text_hidden[:, 0]
    weights = jnp.transpose(w_keyval[0], (1, 0, 2))
    params = jnp.concatenate(
        [
            attn_gain.reshape(8, 1024),
            jnp.broadcast_to(jnp.tanh(gate)[:, None], (1, 1024)),
            jnp.tile(q_gain, (7, 8)),
        ]
    )
    wq, wo = w_query[0], w_out[0]
    pairs, text_all, wq_other, wo_other, par_other = image_pairs(
        image_tokens[0], weights, k_gain, text, wq, wo, params
    )
    choice = image_choice.reshape(4)
    att = attention_first(choice, valid_tiles, pairs, text, text_all, wq, wq_other, params, par_other)
    query, updated = middle(att, text, wo, wo_other, wq, wq_other, params, par_other)
    att = attention_second(choice, valid_tiles, pairs, query)
    result = last_step(att, updated, wo, wo_other, params, par_other)
    return result[None, :, None]


def solution(mesh):
    placed = (
        P(None, "dp", None, "tensor"),
        P("dp", "section", "tensor"),
        P("section", None),
        P("section", None, "tensor"),
        P("section", "tensor", None, None),
        P("section", None),
        P("section", None),
        P("section", "tensor", None),
        P("section"),
        P(None, "dp", None),
        P(),
    )
    return jax.shard_map(
        local,
        mesh=mesh,
        in_specs=placed,
        out_specs=P("section", None, "dp", None, "tensor"),
        check_vma=False,
    )
```

```python
import functools

import jax
import jax.numpy as jnp
from jax import lax
from jax.experimental import pallas as pl
from jax.experimental.pallas import tpu as pltpu
from jax.sharding import PartitionSpec as P

TILE_TOK = 1600
PIECES = 20
MESH = pl.DeviceIdType.MESH
BF = jnp.bfloat16
F32 = jnp.float32


def position():
    dp = lax.axis_index("dp")
    tensor = lax.axis_index("tensor")
    return dp // 2, dp % 2, tensor // 4, tensor % 4, lax.axis_index("section")


def device(x, zh, zl, y, core):
    return (x * 2 + zh, zl * 4 + y, core)


def kv_kernel(
    tok_ref, w_ref, gain_ref, text_ref, wq_ref, wo_ref, attn_ref, small_ref,
    pairs_ref, text_out_ref, wq_out_ref, wo_out_ref, attn_out_ref, small_out_ref,
    tok, wgt, part, from_y1, from_y2, from_z, done,
    tok_sem, w_sem, loc_sem, core_send, core_recv, text_send, text_recv, send, recv,
):
    x, zh, zl, y, core = position()
    dp = x * 2 + zh
    half = tok_ref.shape[0]
    out_ref = pairs_ref.at[core]
    rows = half * 2 // PIECES
    y_up, y_dn = (y + 1) % 4, (y + 3) % 4
    x_up, x_dn = (x + 1) % 4, (x + 3) % 4
    to_y = (device(x, zh, zl, y_up, core), device(x, zh, zl, y_dn, core))
    to_x = (device(x_up, zh, zl, y, core), device(x_dn, zh, zl, y, core))
    to_z_lo = device(x, zh, 1 - zl, y, core)
    to_z_hi = device(x, 1 - zh, zl, y, core)
    to_core = device(x, zh, zl, y, 1 - core)
    peers = to_y + to_x + (to_z_lo, to_z_hi, to_core)

    barrier = pltpu.get_barrier_semaphore()
    for peer in peers:
        pl.semaphore_signal(barrier, inc=1, device_id=peer, device_id_type=MESH)

    def first_row(piece):
        return pl.multiple_of(((piece + core * (PIECES // 2)) % PIECES) * rows, rows)

    def rows_of(piece):
        return pl.ds(first_row(piece), rows)

    def head_of(ring, side):
        return side * 4 + ((y + 2) % 4, y_up, y_dn, y)[ring]

    def tok_copy(piece):
        return pltpu.make_async_copy(
            tok_ref.at[pl.ds(pl.multiple_of(piece * rows, rows), rows)],
            tok.at[pl.ds(pl.multiple_of(core * half + piece * rows, rows), rows)],
            tok_sem.at[piece],
        )

    def w_copy(ring, side):
        return pltpu.make_async_copy(
            w_ref.at[head_of(ring, side)], wgt.at[ring, side], w_sem.at[ring * 2 + side]
        )

    def to_other_core(kind):
        src, dst = (
            (tok_ref, tok.at[pl.ds(pl.multiple_of(core * half, half), half)]),
            (attn_ref, attn_out_ref),
            (small_ref, small_out_ref),
            (wq_ref, wq_out_ref),
            (wo_ref, wo_out_ref),
        )[kind]
        return pltpu.make_async_remote_copy(
            src_ref=src, dst_ref=dst, send_sem=core_send.at[kind], recv_sem=core_recv.at[kind],
            device_id=to_core, device_id_type=MESH,
        )

    def text_copy(kind):
        own = zl * 4
        other = (1 - zl) * 4
        block = (
            own + y, own + y, own + y, other + y, other + y, own + y_dn, own + y_up, other + y_dn, other + y_up
        )[kind]
        dst = text_out_ref.at[block]
        src = text_ref.at[core] if kind < 3 else dst
        if kind >= 5:
            at = pl.ds(((kind - 5) % 2) * 64, 64)
            src, dst = src.at[at], dst.at[at]
        peer = to_z_lo if kind == 2 else to_y[(0, 1, 2, 0, 1, 0, 1, 0, 1)[kind]]
        return pltpu.make_async_remote_copy(
            src_ref=src, dst_ref=dst, send_sem=text_send.at[kind], recv_sem=text_recv.at[kind],
            device_id=peer, device_id_type=MESH,
        )

    def remote(kind, piece, src, dst, peer):
        return pltpu.make_async_remote_copy(
            src_ref=src, dst_ref=dst,
            send_sem=send.at[kind, piece], recv_sem=recv.at[kind, piece],
            device_id=peer, device_id_type=MESH,
        )

    def y1_copy(way, piece):
        at = rows_of(piece)
        return remote(way, piece, part.at[0, way, at], from_y1.at[way, at], to_y[way])

    def y2_copy(way, piece):
        at = rows_of(piece)
        return remote(2 + way, piece, part.at[1 + way, :, at], from_y2.at[way, :, at], to_y[way])

    def z_copy(piece):
        at = rows_of(piece)
        return remote(4, piece, part.at[3, 1 - zl, at], from_z.at[at], to_z_lo)

    def own_copy(way, piece):
        at = rows_of(piece)
        return remote(5 + way, piece, done.at[at], out_ref.at[dp, at], to_z_hi if way == 0 else to_x[way - 1])

    def own_local(piece):
        at = rows_of(piece)
        return pltpu.make_async_copy(done.at[at], out_ref.at[dp, at], loc_sem.at[piece])

    def pair_copy(way, piece):
        ref = out_ref.at[x * 2 + 1 - zh, rows_of(piece)]
        return remote(8 + way, piece, ref, ref, to_x[way])

    def forward_copy(way, piece):
        image = (x_dn * 2 + zh, x_up * 2 + 1 - zh)[way]
        ref = out_ref.at[image, rows_of(piece)]
        return remote(10 + way, piece, ref, ref, to_x[way])

    def mirror(kind, piece):
        across = (x + 2) % 4
        place = (
            (x, zh), (x, 1 - zh), (x_dn, zh), (x_up, zh), (x_dn, 1 - zh), (x_up, 1 - zh), (across, zh), (across, 1 - zh)
        )[kind]
        ref = out_ref.at[place[0] * 2 + place[1], rows_of(piece)]
        return remote(12 + kind, piece, done.at[rows_of(piece)] if kind == 0 else ref, ref, to_core)

    for ring in range(4):
        for side in range(2):
            w_copy(ring, side).start()

    def start_tok(piece, carry):
        tok_copy(piece).start()
        return carry

    lax.fori_loop(0, PIECES // 2, start_tok, 0)
    pl.semaphore_wait(barrier, len(peers))
    for kind in range(3):
        text_copy(kind).start()
    for kind in range(5):
        to_other_core(kind).start()

    def add(ring, side, at, addend):
        part[ring, side, at, :] = (part[ring, side, at, :].astype(F32) + addend.astype(F32)).astype(BF)

    def step_fn(it, carry):
        @pl.when(it < PIECES)
        def _():
            piece = it

            @pl.when(piece < PIECES // 2)
            def _():
                tok_copy(piece).wait()

            @pl.when(piece == PIECES // 2)
            def _():
                to_other_core(0).wait_recv()

            at = rows_of(piece)
            for ring in range(4):
                for side in range(2):
                    @pl.when(it == 0)
                    def _():
                        w_copy(ring, side).wait()

                    part[ring, side, at, :] = jnp.dot(
                        tok[at, :], wgt[ring, side], preferred_element_type=F32
                    ).astype(BF)
                    if ring == 0:
                        y1_copy(side, piece).start()

        @pl.when((it >= 1) & (it < PIECES + 1))
        def _():
            piece = it - 1
            at = rows_of(piece)
            for way in range(2):
                y1_copy(way, piece).wait_recv()
                add(1 + way, way, at, from_y1[way, at, :])
                y2_copy(way, piece).start()

        @pl.when((it >= 2) & (it < PIECES + 2))
        def _():
            piece = it - 2
            at = rows_of(piece)
            for way in range(2):
                y2_copy(way, piece).wait_recv()
            add(
                3, 1 - zl, at,
                from_y2[0, 1 - zl, at, :].astype(F32) + from_y2[1, 1 - zl, at, :].astype(F32),
            )
            z_copy(piece).start()

            @pl.when(piece == PIECES - 1)
            def _():
                for kind in range(3):
                    text_copy(kind).wait_recv()
                for kind in range(3, 7):
                    text_copy(kind).start()

        @pl.when((it >= 3) & (it < PIECES + 3))
        def _():
            piece = it - 3
            at = rows_of(piece)
            z_copy(piece).wait_recv()
            total = (
                part[3, zl, at, :].astype(F32)
                + from_y2[0, zl, at, :].astype(F32) + from_y2[1, zl, at, :].astype(F32)
                + from_z[at, :].astype(F32)
            )
            keys = total[:, :128]
            keys = keys * lax.rsqrt(jnp.mean(keys * keys, axis=-1, keepdims=True) + 1e-05)
            done[at, 0:128] = (keys * gain_ref[...]).astype(BF)
            done[at, 128:256] = total[:, 128:].astype(BF)
            for way in range(3):
                own_copy(way, piece).start()
            own_local(piece).start()
            mirror(0, piece).start()

        @pl.when((it >= 4) & (it < PIECES + 4))
        def _():
            piece = it - 4
            own_copy(0, piece).wait_recv()
            for way in range(2):
                pair_copy(way, piece).start()
            mirror(1, piece).start()

        @pl.when((it >= 5) & (it < PIECES + 5))
        def _():
            piece = it - 5
            own_copy(1, piece).wait_recv()
            pair_copy(1, piece).wait_recv()
            for way in range(2):
                forward_copy(way, piece).start()
            own_copy(2, piece).wait_recv()
            pair_copy(0, piece).wait_recv()
            for kind in range(2, 6):
                mirror(kind, piece).start()

            @pl.when(piece == PIECES - 1)
            def _():
                for kind in range(3, 5):
                    text_copy(kind).wait_recv()
                    text_copy(kind + 4).start()

        @pl.when(it >= 6)
        def _():
            piece = it - 6
            for way in range(2):
                forward_copy(way, piece).wait_recv()
            for kind in range(6, 8):
                mirror(kind, piece).start()

        return carry

    lax.fori_loop(0, PIECES + 6, step_fn, 0)

    def finish(piece, carry):
        z_copy(piece).wait_send()
        for way in range(2):
            y1_copy(way, piece).wait_send()
            y2_copy(way, piece).wait_send()
        for way in range(2):
            pair_copy(way, piece).wait_send()
            forward_copy(way, piece).wait_send()
        for way in range(3):
            own_copy(way, piece).wait_send()
        own_local(piece).wait()
        for kind in range(8):
            mirror(kind, piece).wait()
        return carry

    lax.fori_loop(0, PIECES, finish, 0)
    to_other_core(0).wait_send()
    for kind in range(1, 5):
        to_other_core(kind).wait()
    for kind in range(9):
        text_copy(kind).wait_send()
    for kind in range(5, 9):
        text_copy(kind).wait_recv()


def image_pairs(tokens, weights, gain, text, w_query, w_out, attn_gain, small):
    half, width = tokens.shape
    heads = weights.shape[0]
    patches = half * 2
    any_spec = pl.BlockSpec(memory_space=pl.ANY)

    def like(array):
        return jax.ShapeDtypeStruct(array.shape, array.dtype)

    return pl.pallas_call(
        kv_kernel,
        name="kv",
        out_shape=[
            jax.ShapeDtypeStruct((2, 8, patches, 256), BF),
            jax.ShapeDtypeStruct((8,) + text.shape[1:], BF),
            like(w_query),
            like(w_out),
            like(attn_gain),
            like(small),
        ],
        in_specs=[any_spec, any_spec, pl.BlockSpec(memory_space=pltpu.VMEM)] + [any_spec] * 5,
        out_specs=[any_spec] * 6,
        scratch_shapes=[
            pltpu.VMEM((patches, width), BF),
            pltpu.VMEM((4, 2, width, 256), BF),
            pltpu.VMEM((4, 2, patches, 256), BF),
            pltpu.VMEM((2, patches, 256), BF),
            pltpu.VMEM((2, 2, patches, 256), BF),
            pltpu.VMEM((patches, 256), BF),
            pltpu.VMEM((patches, 256), BF),
            pltpu.SemaphoreType.DMA((PIECES // 2,)),
            pltpu.SemaphoreType.DMA((8,)),
            pltpu.SemaphoreType.DMA((PIECES,)),
            pltpu.SemaphoreType.DMA((5,)),
            pltpu.SemaphoreType.DMA((5,)),
            pltpu.SemaphoreType.DMA((9,)),
            pltpu.SemaphoreType.DMA((9,)),
            pltpu.SemaphoreType.DMA((20, PIECES)),
            pltpu.SemaphoreType.DMA((20, PIECES)),
        ],
        compiler_params=pltpu.CompilerParams(
            collective_id=0, has_side_effects=True, vmem_limit_bytes=60 * 2**20
        ),
        cost_estimate=pl.CostEstimate(
            flops=2 * patches * width * heads * 256, bytes_accessed=40 * 2**20, transcendentals=0
        ),
    )(tokens, weights, gain, text, w_query, w_out, attn_gain, small)


KEY_PARTS = ((0, 512), (512, 512), (1024, 576))


class LayerLoad:
    def __init__(self, layer, own, other, dst, sem):
        self.here = lax.axis_index("section") == layer
        self.own = pltpu.make_async_copy(own, dst, sem)
        self.other = pltpu.make_async_copy(other, dst, sem)

    def start(self):
        pl.when(self.here)(lambda: self.own.start())
        pl.when(jnp.logical_not(self.here))(lambda: self.other.start())

    def wait(self):
        self.own.wait()


def add_to_query(acc, sq, block, gain, weights):
    values = block.astype(F32)
    sq[...] += jnp.sum(values * values, axis=-1, keepdims=True)
    acc[...] += jnp.dot((values * gain).astype(BF), weights, preferred_element_type=F32)


def finish_query(acc, sq, q_gain, query):
    inverse = lax.rsqrt(sq[:, :1] * (1.0 / 8192.0) + 1e-05)
    for head in range(4):
        one = acc[:, head * 128:(head + 1) * 128] * inverse
        one = one * lax.rsqrt(jnp.mean(one * one, axis=-1, keepdims=True) + 1e-05)
        query[head * 128:(head + 1) * 128, :] = (one * q_gain * 128.0 ** -0.5).astype(BF)


def attend(layer, choice_ref, valid_ref, query, pairs_ref, att_ref, tiles, total, norm, sem, before=None):
    core = lax.axis_index("section")
    first = choice_ref[core, 0, 0]
    second = choice_ref[core, 0, 1]
    other = second != first
    plan = (
        (first, 0, None),
        (first, 1, valid_ref[first] > 1),
        (second, 0, other),
        (second, 1, other & (valid_ref[second] > 1)),
    )

    def copy(slot):
        image, tile, _ = plan[slot]
        return pltpu.make_async_copy(
            pairs_ref.at[layer, image, pl.ds(tile * TILE_TOK, TILE_TOK)], tiles.at[slot], sem.at[slot]
        )

    def run(slot, fn):
        allowed = plan[slot][2]
        if allowed is None:
            fn()
        else:
            pl.when(allowed)(fn)

    for slot in range(4):
        run(slot, lambda slot=slot: copy(slot).start())
    total[...] = jnp.zeros_like(total)
    norm[...] = jnp.zeros_like(norm)
    if before is not None:
        before()

    def one(slot):
        copy(slot).wait()
        for start, size in KEY_PARTS:
            scores = lax.dot_general(
                query[...], tiles[slot, start:start + size, 0:128],
                (((1,), (1,)), ((), ())), preferred_element_type=F32,
            )
            expo = jnp.exp(scores)
            norm[...] += jnp.sum(expo, axis=-1, keepdims=True)
            total[...] += jnp.dot(
                expo.astype(BF), tiles[slot, start:start + size, 128:256], preferred_element_type=F32
            )

    for slot in range(4):
        run(slot, functools.partial(one, slot))
    for head in range(4):
        at = slice(head * 128, (head + 1) * 128)
        att_ref[:, at] = (total[at, :] / norm[at, :1]).astype(BF)


def first_attention(
    choice_ref, valid_ref, pairs_ref, text_ref, text_all_ref, wq_ref, wq_other_ref,
    attn_ref, attn_other_ref, small_ref, small_other_ref, att_ref,
    tiles, total, norm, sem, hidden, wq, attn, small, acc, sq, query, load_sem, wq_sem,
):
    core = lax.axis_index("section")
    tensor = lax.axis_index("tensor")
    attn_load = LayerLoad(0, attn_ref, attn_other_ref, attn, load_sem.at[8])
    small_load = LayerLoad(0, small_ref, small_other_ref, small, load_sem.at[9])
    attn_load.start()
    small_load.start()
    chunks = []
    for step in range(8):
        block = (tensor + step) % 8
        src = text_ref.at[core] if step == 0 else text_all_ref.at[block]
        at = pl.ds(pl.multiple_of(block * 1024, 1024), 1024)
        chunks.append((
            at,
            pltpu.make_async_copy(src, hidden.at[step], load_sem.at[step]),
            LayerLoad(0, wq_ref.at[at], wq_other_ref.at[at], wq.at[step], wq_sem.at[step]),
        ))
        chunks[-1][1].start()
        chunks[-1][2].start()

    def before():
        acc[...] = jnp.zeros_like(acc)
        sq[...] = jnp.zeros_like(sq)
        attn_load.wait()
        small_load.wait()
        for step, (at, text_load, wq_load) in enumerate(chunks):
            text_load.wait()
            wq_load.wait()
            add_to_query(acc, sq, hidden[step], attn[:, at], wq[step])
        finish_query(acc, sq, small[0:1, :], query)

    attend(0, choice_ref, valid_ref, query, pairs_ref, att_ref, tiles, total, norm, sem, before)


def second_attention(choice_ref, valid_ref, pairs_ref, query_ref, att_ref, tiles, total, norm, sem):
    attend(1, choice_ref, valid_ref, query_ref, pairs_ref, att_ref, tiles, total, norm, sem)


ATTEND_SCRATCH = [
    pltpu.VMEM((4, TILE_TOK, 256), BF),
    pltpu.VMEM((512, 128), F32),
    pltpu.VMEM((512, 128), F32),
    pltpu.SemaphoreType.DMA((4,)),
]


def attention_first(choice, valid, *arrays):
    any_spec = pl.BlockSpec(memory_space=pl.ANY)
    smem = pl.BlockSpec(memory_space=pltpu.SMEM)
    return pl.pallas_call(
        first_attention,
        name="attend0",
        out_shape=jax.ShapeDtypeStruct((128, 512), BF),
        in_specs=[smem, smem] + [any_spec] * 9,
        out_specs=pl.BlockSpec(memory_space=pltpu.VMEM),
        scratch_shapes=ATTEND_SCRATCH + [
            pltpu.VMEM((8, 128, 1024), BF),
            pltpu.VMEM((8, 1024, 512), BF),
            pltpu.VMEM((1, 8192), F32),
            pltpu.VMEM((2, 128), F32),
            pltpu.VMEM((128, 512), F32),
            pltpu.VMEM((128, 128), F32),
            pltpu.VMEM((512, 128), BF),
            pltpu.SemaphoreType.DMA((10,)),
            pltpu.SemaphoreType.DMA((8,)),
        ],
        compiler_params=pltpu.CompilerParams(vmem_limit_bytes=60 * 2**20),
        cost_estimate=pl.CostEstimate(flops=3 * 10**9, bytes_accessed=14 * 2**20, transcendentals=3 * 10**6),
    )(choice, valid, *arrays)


def attention_second(choice, valid, pairs, query):
    any_spec = pl.BlockSpec(memory_space=pl.ANY)
    smem = pl.BlockSpec(memory_space=pltpu.SMEM)
    vmem = pl.BlockSpec(memory_space=pltpu.VMEM)
    return pl.pallas_call(
        second_attention,
        name="attend1",
        out_shape=jax.ShapeDtypeStruct((128, 512), BF),
        in_specs=[smem, smem, any_spec, vmem],
        out_specs=vmem,
        scratch_shapes=ATTEND_SCRATCH,
        compiler_params=pltpu.CompilerParams(vmem_limit_bytes=60 * 2**20),
        cost_estimate=pl.CostEstimate(flops=2 * 10**9, bytes_accessed=4 * 2**20, transcendentals=3 * 10**6),
    )(choice, valid, pairs, query)


Y_ROWS = 80
NEAR = pl.ds(0, Y_ROWS)
REST = pl.ds(Y_ROWS, 128 - Y_ROWS)
HALF = (pl.ds(0, 512), pl.ds(512, 512))


def project_and_sum(layer, att_ref, wo_ref, wo_other_ref, scratch, greet):
    wo, part, from_y1, from_y2, from_z, from_c, from_c1, from_c2, wo_sem, send, recv = scratch
    x, zh, zl, y, core = position()
    y_up, y_dn = (y + 1) % 4, (y + 3) % 4
    to_y = (device(x, zh, zl, y_up, core), device(x, zh, zl, y_dn, core))
    to_z = device(x, zh, 1 - zl, y, core)
    order = ((0, 0), (0, 1), (2, 0), (1, 1), (1, 0), (2, 1), (3, 0), (3, 1))
    loads = {}
    for ring, side in order:
        block = side * 4 + ((y + 2) % 4, y_up, y_dn, y)[ring]
        at = pl.ds(pl.multiple_of(block * 1024, 1024), 1024)
        loads[ring, side] = LayerLoad(
            layer, wo_ref.at[:, at], wo_other_ref.at[:, at], wo.at[ring, side], wo_sem.at[ring * 2 + side]
        )
        loads[ring, side].start()

    def remote(kind, src, dst, peer):
        return pltpu.make_async_remote_copy(
            src_ref=src, dst_ref=dst, send_sem=send.at[kind], recv_sem=recv.at[kind],
            device_id=peer, device_id_type=MESH,
        )

    far = [remote(way, part.at[0, way, NEAR], from_y1.at[way], to_y[way]) for way in range(2)]
    near = {
        (ring, side): remote(2 + ring * 2 + side - 2, part.at[ring, side, NEAR], from_y2.at[ring - 1, side], to_y[ring - 1])
        for ring in (1, 2) for side in range(2)
    }
    cross = [remote(6 + ring, part.at[ring, 1 - zl, REST], from_c.at[ring], to_z) for ring in range(4)]
    cross_far = [
        remote(10 + way, part.at[0, zl, REST, HALF[way]], from_c1.at[way], to_y[way]) for way in range(2)
    ]
    cross_near = [remote(12 + way, part.at[1 + way, zl, REST], from_c2.at[way], to_y[way]) for way in range(2)]
    last = remote(14, part.at[3, 1 - zl, NEAR], from_z, to_z)
    at_once = {(0, 0): far[0], (0, 1): far[1], (2, 0): near[2, 0], (1, 1): near[1, 1]}

    for ring, side in order:
        loads[ring, side].wait()
        part[ring, side] = jnp.dot(att_ref[...], wo[ring, side], preferred_element_type=F32).astype(BF)
        if (ring, side) == (0, 0):
            greet()
        if (ring, side) in at_once:
            at_once[ring, side].start()

        @pl.when(zl != side)
        def _():
            cross[ring].start()

    def add(ring, side, rows, columns, addend):
        part[ring, side, rows, columns] = (
            part[ring, side, rows, columns].astype(F32) + addend.astype(F32)
        ).astype(BF)

    every = slice(None)
    for way, key in ((0, (1, 0)), (1, (2, 1))):
        far[way].wait_recv()
        add(*key, NEAR, every, from_y1[way])
        near[key].start()
    cross[0].wait_recv()
    add(0, zl, REST, every, from_c[0])
    for way in range(2):
        cross_far[way].start()
    for ring in range(1, 4):
        cross[ring].wait_recv()
        add(ring, zl, REST, every, from_c[ring])
    for key in near:
        near[key].wait_recv()
    add(3, 1 - zl, NEAR, every, from_y2[0, 1 - zl].astype(F32) + from_y2[1, 1 - zl].astype(F32))
    last.start()
    for way in range(2):
        cross_far[way].wait_recv()
        add(1 + way, zl, REST, HALF[way], from_c1[way])
        cross_near[way].start()
    first = part[3, zl, NEAR, :].astype(F32) + from_y2[0, zl].astype(F32) + from_y2[1, zl].astype(F32)
    second = part[3, zl, REST, :].astype(F32)
    last.wait_recv()
    first = first + from_z[...].astype(F32)
    for way in range(2):
        cross_near[way].wait_recv()
        second = second + from_c2[way].astype(F32)

    def drain():
        for copy in far + list(near.values()) + cross + cross_far + cross_near + [last]:
            copy.wait_send()

    return first, second, drain


SUM_SCRATCH = [
    pltpu.VMEM((4, 2, 512, 1024), BF),
    pltpu.VMEM((4, 2, 128, 1024), BF),
    pltpu.VMEM((2, Y_ROWS, 1024), BF),
    pltpu.VMEM((2, 2, Y_ROWS, 1024), BF),
    pltpu.VMEM((Y_ROWS, 1024), BF),
    pltpu.VMEM((4, 128 - Y_ROWS, 1024), BF),
    pltpu.VMEM((2, 128 - Y_ROWS, 512), BF),
    pltpu.VMEM((2, 128 - Y_ROWS, 1024), BF),
    pltpu.SemaphoreType.DMA((8,)),
    pltpu.SemaphoreType.DMA((15,)),
    pltpu.SemaphoreType.DMA((15,)),
]


def greeting(peers):
    barrier = pltpu.get_barrier_semaphore()
    for peer in peers:
        pl.semaphore_signal(barrier, inc=1, device_id=peer, device_id_type=MESH)
    pl.semaphore_wait(barrier, len(peers))


def middle_kernel(
    att_ref, text_ref, wo_ref, wo_other_ref, wq_ref, wq_other_ref,
    attn_ref, attn_other_ref, small_ref, small_other_ref, query_ref, upd_ref, *scratch,
):
    hidden, wq, attn, small, text, acc, sq, wq_sem, ag_send, ag_recv, par_sem = scratch[len(SUM_SCRATCH):]
    x, zh, zl, y, core = position()
    y_up, y_dn = (y + 1) % 4, (y + 3) % 4
    to_up = device(x, zh, zl, y_up, core)
    to_dn = device(x, zh, zl, y_dn, core)
    to_z = device(x, zh, 1 - zl, y, core)
    par_copies = [
        LayerLoad(0, small_ref, small_other_ref, small.at[0], par_sem.at[0]),
        LayerLoad(1, small_ref, small_other_ref, small.at[1], par_sem.at[1]),
        LayerLoad(1, attn_ref, attn_other_ref, attn, par_sem.at[2]),
        pltpu.make_async_copy(text_ref.at[core], text, par_sem.at[3]),
    ]
    for copy in par_copies:
        copy.start()

    first, second, drain = project_and_sum(
        0, att_ref, wo_ref, wo_other_ref, scratch[:len(SUM_SCRATCH)], lambda: greeting([to_up, to_dn, to_z])
    )
    mine, across = zl * 4, (1 - zl) * 4
    own, left, right, far = mine + y, mine + y_dn, mine + y_up, mine + (y + 2) % 4
    z_own, z_left, z_right, z_far = across + y, across + y_dn, across + y_up, across + (y + 2) % 4
    order = [own, left, right, z_own, z_left, z_right, far, z_far]
    chunks = []
    for k, block in enumerate(order):
        at = pl.ds(pl.multiple_of(block * 1024, 1024), 1024)
        chunks.append(LayerLoad(1, wq_ref.at[at], wq_other_ref.at[at], wq.at[k], wq_sem.at[k]))
        chunks[k].start()
    for copy in par_copies:
        copy.wait()
    gate = small[0, 1:2, 0:1]

    def remote(kind, block, rows, peer, half=None):
        ref = hidden.at[block, rows] if half is None else hidden.at[block, rows, HALF[half]]
        return pltpu.make_async_remote_copy(
            src_ref=ref, dst_ref=ref, send_sem=ag_send.at[kind], recv_sem=ag_recv.at[kind],
            device_id=peer, device_id_type=MESH,
        )

    copies = [
        remote(0, own, NEAR, to_z), remote(1, own, NEAR, to_up), remote(2, own, NEAR, to_dn),
        remote(3, own, REST, to_up), remote(4, own, REST, to_dn), remote(5, own, REST, to_z),
        remote(6, left, REST, to_up, 0), remote(7, right, REST, to_dn, 1),
        remote(8, left, REST, to_z), remote(9, right, REST, to_z), remote(10, far, REST, to_z),
        remote(11, z_own, NEAR, to_up), remote(12, z_own, NEAR, to_dn),
        remote(13, left, NEAR, to_up, 0), remote(14, right, NEAR, to_dn, 1),
        remote(15, z_left, NEAR, to_up, 0), remote(16, z_right, NEAR, to_dn, 1),
    ]

    def begin(*kinds):
        for kind in kinds:
            copies[kind].start()

    def arrive(*kinds):
        for kind in kinds:
            copies[kind].wait_recv()

    def use(k):
        chunks[k].wait()
        block = order[k]
        at = pl.ds(pl.multiple_of(block * 1024, 1024), 1024)
        add_to_query(acc, sq, hidden[block], attn[:, at], wq[k])

    hidden[own, NEAR, :] = (text[NEAR, :].astype(F32) + gate * first).astype(BF)
    begin(0)
    hidden[own, REST, :] = (text[REST, :].astype(F32) + gate * second).astype(BF)
    begin(3, 4, 1, 2, 5)
    upd_ref[...] = hidden[own]
    acc[...] = jnp.zeros_like(acc)
    sq[...] = jnp.zeros_like(sq)
    use(0)
    arrive(3)
    begin(6, 8)
    arrive(4)
    begin(7, 9)
    arrive(0)
    begin(11, 12)
    arrive(1)
    begin(13)
    arrive(2)
    begin(14)
    use(1)
    use(2)
    arrive(6, 7)
    begin(10)
    arrive(11)
    begin(15)
    arrive(12)
    begin(16)
    arrive(5)
    use(3)
    arrive(8)
    use(4)
    arrive(9)
    use(5)
    arrive(13, 14)
    use(6)
    arrive(10, 15, 16)
    use(7)
    finish_query(acc, sq, small[1, 0:1, :], query_ref)
    drain()
    for copy in copies:
        copy.wait_send()


def last_kernel(
    att_ref, upd_ref, wo_ref, wo_other_ref, small_ref, small_other_ref, out_ref, *scratch,
):
    small, last, core_send, core_recv, par_sem = scratch[len(SUM_SCRATCH):]
    x, zh, zl, y, core = position()
    to_y_up = device(x, zh, zl, (y + 1) % 4, core)
    to_y_dn = device(x, zh, zl, (y + 3) % 4, core)
    to_z_lo = device(x, zh, 1 - zl, y, core)
    to_core = device(x, zh, zl, y, 1 - core)
    par_copy = LayerLoad(1, small_ref, small_other_ref, small, par_sem.at[0])
    par_copy.start()
    send_first = pltpu.make_async_remote_copy(
        src_ref=upd_ref, dst_ref=out_ref.at[1], send_sem=core_send.at[0], recv_sem=core_recv.at[0],
        device_id=to_core, device_id_type=MESH,
    )
    send_last = pltpu.make_async_remote_copy(
        src_ref=last, dst_ref=out_ref.at[0], send_sem=core_send.at[1], recv_sem=core_recv.at[1],
        device_id=to_core, device_id_type=MESH,
    )

    def greet():
        greeting([to_y_up, to_y_dn, to_z_lo, to_core])

        @pl.when(core == 1)
        def _():
            send_first.start()

    first, second, drain = project_and_sum(1, att_ref, wo_ref, wo_other_ref, scratch[:len(SUM_SCRATCH)], greet)
    par_copy.wait()
    gate = small[1:2, 0:1]
    last[NEAR, :] = (upd_ref[NEAR, :].astype(F32) + gate * first).astype(BF)
    last[REST, :] = (upd_ref[REST, :].astype(F32) + gate * second).astype(BF)

    @pl.when(core == 0)
    def _():
        send_last.start()
        out_ref[0] = upd_ref[...]
        send_first.wait_recv()
        send_last.wait_send()

    @pl.when(core == 1)
    def _():
        out_ref[1] = last[...]
        send_first.wait_send()
        send_last.wait_recv()

    drain()


def middle(att, text, *weights):
    any_spec = pl.BlockSpec(memory_space=pl.ANY)
    vmem = pl.BlockSpec(memory_space=pltpu.VMEM)
    return pl.pallas_call(
        middle_kernel,
        name="middle",
        out_shape=[jax.ShapeDtypeStruct((512, 128), BF), jax.ShapeDtypeStruct((128, 1024), BF)],
        in_specs=[vmem] + [any_spec] * 9,
        out_specs=[vmem] * 2,
        scratch_shapes=SUM_SCRATCH + [
            pltpu.VMEM((8, 128, 1024), BF),
            pltpu.VMEM((8, 1024, 512), BF),
            pltpu.VMEM((1, 8192), F32),
            pltpu.VMEM((2, 2, 128), F32),
            pltpu.VMEM((128, 1024), BF),
            pltpu.VMEM((128, 512), F32),
            pltpu.VMEM((128, 128), F32),
            pltpu.SemaphoreType.DMA((8,)),
            pltpu.SemaphoreType.DMA((17,)),
            pltpu.SemaphoreType.DMA((17,)),
            pltpu.SemaphoreType.DMA((4,)),
        ],
        compiler_params=pltpu.CompilerParams(
            collective_id=1, has_side_effects=True, vmem_limit_bytes=60 * 2**20
        ),
    )(att, text, *weights)


def last_step(att, upd, *weights):
    any_spec = pl.BlockSpec(memory_space=pl.ANY)
    vmem = pl.BlockSpec(memory_space=pltpu.VMEM)
    return pl.pallas_call(
        last_kernel,
        name="last",
        out_shape=jax.ShapeDtypeStruct((2, 128, 1024), BF),
        in_specs=[vmem, vmem] + [any_spec] * 4,
        out_specs=vmem,
        scratch_shapes=SUM_SCRATCH + [
            pltpu.VMEM((2, 128), F32),
            pltpu.VMEM((128, 1024), BF),
            pltpu.SemaphoreType.DMA((2,)),
            pltpu.SemaphoreType.DMA((2,)),
            pltpu.SemaphoreType.DMA((1,)),
        ],
        compiler_params=pltpu.CompilerParams(
            collective_id=2, has_side_effects=True, vmem_limit_bytes=60 * 2**20
        ),
    )(att, upd, *weights)


def local(
    text_hidden,
    image_tokens,
    attn_gain,
    w_query,
    w_keyval,
    q_gain,
    k_gain,
    w_out,
    gate,
    image_choice,
    valid_tiles,
):
    text = text_hidden[:, 0]
    weights = jnp.transpose(w_keyval[0], (1, 0, 2))
    small = jnp.concatenate([q_gain, jnp.broadcast_to(jnp.tanh(gate)[:, None], (1, 128))])
    wq, wo = w_query[0], w_out[0]
    pairs, text_all, wq_other, wo_other, attn_other, small_other = image_pairs(
        image_tokens[0], weights, k_gain, text, wq, wo, attn_gain, small
    )
    gains = (attn_gain, attn_other, small, small_other)
    att = attention_first(image_choice, valid_tiles, pairs, text, text_all, wq, wq_other, *gains)
    query, updated = middle(att, text, wo, wo_other, wq, wq_other, *gains)
    att = attention_second(image_choice, valid_tiles, pairs, query)
    result = last_step(att, updated, wo, wo_other, small, small_other)
    return result[None, :, None]


def solution(mesh):
    placed = (
        P(None, "dp", None, "tensor"),
        P("dp", "section", "tensor"),
        P("section", None),
        P("section", None, "tensor"),
        P("section", "tensor", None, None),
        P("section", None),
        P("section", None),
        P("section", "tensor", None),
        P("section"),
        P(None, "dp", None),
        P(),
    )
    return jax.shard_map(
        local,
        mesh=mesh,
        in_specs=placed,
        out_specs=P("section", None, "dp", None, "tensor"),
        check_vma=False,
    )
```

```python
import functools

import jax
import jax.numpy as jnp
from jax import lax
from jax.experimental import pallas as pl
from jax.experimental.pallas import tpu as pltpu
from jax.sharding import PartitionSpec as P

TILE_TOK = 1600
PIECES = 20
GROUP = 2
JOINT = 1
MESH = pl.DeviceIdType.MESH
BF = jnp.bfloat16
F32 = jnp.float32


def position():
    dp = lax.axis_index("dp")
    tensor = lax.axis_index("tensor")
    return dp // 2, dp % 2, tensor // 4, tensor % 4, lax.axis_index("section")


def device(x, zh, zl, y, core):
    return (x * 2 + zh, zl * 4 + y, core)


def kv_kernel(
    tok_ref, w_ref, gain_ref, q_gain_ref, gate_ref, text_ref, wq_ref, wo_ref, attn_ref,
    pairs_ref, text_out_ref, wq_out_ref, wo_out_ref, attn_out_ref, small_out_ref,
    small, tok, wgt, part, from_y1, from_y2, from_z, done,
    tok_sem, w_sem, loc_sem, core_send, core_recv, text_send, text_recv, send, recv, mirror_recv,
):
    x, zh, zl, y, core = position()
    dp = x * 2 + zh
    half = tok_ref.shape[0]
    out_ref = pairs_ref.at[core]
    rows = half * 2 // PIECES
    y_up, y_dn = (y + 1) % 4, (y + 3) % 4
    x_up, x_dn = (x + 1) % 4, (x + 3) % 4
    to_y = (device(x, zh, zl, y_up, core), device(x, zh, zl, y_dn, core))
    to_x = (device(x_up, zh, zl, y, core), device(x_dn, zh, zl, y, core))
    to_z_lo = device(x, zh, 1 - zl, y, core)
    to_z_hi = device(x, 1 - zh, zl, y, core)
    to_core = device(x, zh, zl, y, 1 - core)
    peers = to_y + to_x + (to_z_lo, to_z_hi, to_core)

    barrier = pltpu.get_barrier_semaphore()
    for peer in peers:
        pl.semaphore_signal(barrier, inc=1, device_id=peer, device_id_type=MESH)

    def first_row(piece):
        return pl.multiple_of(((piece + core * (PIECES // 2)) % PIECES) * rows, rows)

    def rows_of(piece):
        return pl.ds(first_row(piece), rows)

    def head_of(ring, side):
        return side * 4 + ((y + 2) % 4, y_up, y_dn, y)[ring]

    def tok_copy(piece):
        return pltpu.make_async_copy(
            tok_ref.at[pl.ds(pl.multiple_of(piece * rows, rows), rows)],
            tok.at[pl.ds(pl.multiple_of(core * half + piece * rows, rows), rows)],
            tok_sem.at[piece],
        )

    def w_copy(ring, side):
        return pltpu.make_async_copy(
            w_ref.at[head_of(ring, side)], wgt.at[ring, side], w_sem.at[ring * 2 + side]
        )

    def to_other_core(kind):
        src, dst = (
            (tok_ref, tok.at[pl.ds(pl.multiple_of(core * half, half), half)]),
            (attn_ref, attn_out_ref),
            (small, small_out_ref.at[core]),
            (wq_ref, wq_out_ref),
            (wo_ref, wo_out_ref),
        )[kind]
        return pltpu.make_async_remote_copy(
            src_ref=src, dst_ref=dst, send_sem=core_send.at[kind], recv_sem=core_recv.at[kind],
            device_id=to_core, device_id_type=MESH,
        )

    def text_copy(kind):
        own = zl * 4
        other = (1 - zl) * 4
        block = (
            own + y, own + y, own + y, other + y, other + y, own + y_dn, own + y_up, other + y_dn, other + y_up
        )[kind]
        dst = text_out_ref.at[block]
        src = text_ref.at[core] if kind < 3 else dst
        if kind >= 5:
            at = pl.ds(((kind - 5) % 2) * 64, 64)
            src, dst = src.at[at], dst.at[at]
        peer = to_z_lo if kind == 2 else to_y[(0, 1, 2, 0, 1, 0, 1, 0, 1)[kind]]
        return pltpu.make_async_remote_copy(
            src_ref=src, dst_ref=dst, send_sem=text_send.at[kind], recv_sem=text_recv.at[kind],
            device_id=peer, device_id_type=MESH,
        )

    def remote(kind, piece, src, dst, peer):
        return pltpu.make_async_remote_copy(
            src_ref=src, dst_ref=dst,
            send_sem=send.at[kind], recv_sem=recv.at[kind, piece],
            device_id=peer, device_id_type=MESH,
        )

    def y1_copy(way, piece):
        at = rows_of(piece)
        return remote(way, piece, part.at[0, way, at], from_y1.at[way, at], to_y[way])

    def y2_copy(way, piece):
        at = rows_of(piece)
        return remote(2 + way, piece, part.at[1 + way, :, at], from_y2.at[way, :, at], to_y[way])

    def z_copy(piece):
        at = rows_of(piece)
        return remote(4, piece, part.at[3, 1 - zl, at], from_z.at[at], to_z_lo)

    def own_copy(way, piece):
        at = rows_of(piece)
        return remote(5 + way, piece, done.at[at], out_ref.at[dp, at], to_z_hi if way == 0 else to_x[way - 1])

    def own_local(piece):
        at = rows_of(piece)
        return pltpu.make_async_copy(done.at[at], out_ref.at[dp, at], loc_sem.at[0])

    def pair_copy(way, piece):
        ref = out_ref.at[x * 2 + 1 - zh, rows_of(piece)]
        return remote(8 + way, piece, ref, ref, to_x[way])

    def forward_copy(way, piece):
        image = (x_dn * 2 + zh, x_up * 2 + 1 - zh)[way]
        ref = out_ref.at[image, rows_of(piece)]
        return remote(10 + way, piece, ref, ref, to_x[way])

    def mirror_copy(kind, at):
        across = (x + 2) % 4
        place = (
            (x, zh), (x, 1 - zh), (x_dn, zh), (x_up, zh), (x_dn, 1 - zh), (x_up, 1 - zh), (across, zh), (across, 1 - zh)
        )[kind]
        ref = out_ref.at[place[0] * 2 + place[1], at]
        return pltpu.make_async_remote_copy(
            src_ref=done.at[at] if kind == 0 else ref, dst_ref=ref,
            send_sem=send.at[12 + kind], recv_sem=mirror_recv.at[kind],
            device_id=to_core, device_id_type=MESH,
        )

    def mirror(kinds, piece):
        @pl.when(piece % GROUP == GROUP - 1)
        def _():
            at = pl.ds(first_row(piece - (GROUP - 1)), rows * GROUP)
            for kind in kinds:
                mirror_copy(kind, at).start()

    for ring in range(4):
        for side in range(2):
            w_copy(ring, side).start()

    def start_tok(piece, carry):
        tok_copy(piece).start()
        return carry

    lax.fori_loop(0, PIECES // 2, start_tok, 0)
    small[0:1, :] = q_gain_ref[...]
    small[1:2, :] = jnp.tanh(jnp.broadcast_to(gate_ref[0], (1, 128)))
    small_own = pltpu.make_async_copy(small, small_out_ref.at[core], loc_sem.at[1])
    small_own.start()
    pl.semaphore_wait(barrier, len(peers))
    to_other_core(0).start()
    text_copy(2).start()
    for kind in range(1, 5):
        to_other_core(kind).start()

    def add(ring, side, at, addend):
        part[ring, side, at, :] = (part[ring, side, at, :].astype(F32) + addend.astype(F32)).astype(BF)

    def step_fn(it, carry):
        @pl.when((it < PIECES) & (it % JOINT == 0))
        def _():
            piece = it

            @pl.when(piece < PIECES // 2)
            def _():
                for more in range(JOINT):
                    tok_copy(piece + more).wait()

            @pl.when(piece == PIECES // 2)
            def _():
                to_other_core(0).wait_recv()

            at = pl.ds(first_row(piece), rows * JOINT)
            for ring in range(4):
                for side in range(2):
                    @pl.when(it == 0)
                    def _():
                        w_copy(ring, side).wait()

                    part[ring, side, at, :] = jnp.dot(
                        tok[at, :], wgt[ring, side], preferred_element_type=F32
                    ).astype(BF)
                    if ring == 0:
                        for more in range(JOINT):
                            y1_copy(side, piece + more).start()

        @pl.when((it >= 1) & (it < PIECES + 1))
        def _():
            piece = it - 1
            at = rows_of(piece)
            for way in range(2):
                y1_copy(way, piece).wait_recv()
                add(1 + way, way, at, from_y1[way, at, :])
                y2_copy(way, piece).start()

            @pl.when(piece == PIECES - 1)
            def _():
                text_copy(2).wait_recv()
                for kind in (0, 1, 3, 4):
                    text_copy(kind).start()

        @pl.when((it >= 2) & (it < PIECES + 2))
        def _():
            piece = it - 2
            at = rows_of(piece)
            for way in range(2):
                y2_copy(way, piece).wait_recv()
            add(
                3, 1 - zl, at,
                from_y2[0, 1 - zl, at, :].astype(F32) + from_y2[1, 1 - zl, at, :].astype(F32),
            )
            z_copy(piece).start()

        @pl.when((it >= 3) & (it < PIECES + 3))
        def _():
            piece = it - 3
            at = rows_of(piece)
            z_copy(piece).wait_recv()
            total = (
                part[3, zl, at, :].astype(F32)
                + from_y2[0, zl, at, :].astype(F32) + from_y2[1, zl, at, :].astype(F32)
                + from_z[at, :].astype(F32)
            )
            keys = total[:, :128]
            keys = keys * lax.rsqrt(jnp.mean(keys * keys, axis=-1, keepdims=True) + 1e-05)
            done[at, 0:128] = (keys * gain_ref[...]).astype(BF)
            done[at, 128:256] = total[:, 128:].astype(BF)
            for way in range(3):
                own_copy(way, piece).start()
            own_local(piece).start()
            mirror((0,), piece)

        @pl.when((it >= 4) & (it < PIECES + 4))
        def _():
            piece = it - 4
            own_copy(0, piece).wait_recv()
            for way in range(2):
                pair_copy(way, piece).start()

            @pl.when(piece == PIECES - 1)
            def _():
                for kind in (0, 1):
                    text_copy(kind).wait_recv()
                    text_copy(kind + 5).start()
            mirror((1,), piece)

        @pl.when((it >= 5) & (it < PIECES + 5))
        def _():
            piece = it - 5
            own_copy(1, piece).wait_recv()
            pair_copy(1, piece).wait_recv()
            for way in range(2):
                forward_copy(way, piece).start()
            own_copy(2, piece).wait_recv()
            pair_copy(0, piece).wait_recv()
            mirror((2, 3, 4, 5), piece)

            @pl.when(piece == PIECES - 1)
            def _():
                for kind in (3, 4):
                    text_copy(kind).wait_recv()
                    text_copy(kind + 4).start()

        @pl.when(it >= 6)
        def _():
            piece = it - 6
            for way in range(2):
                forward_copy(way, piece).wait_recv()
            mirror((6, 7), piece)

        return carry

    lax.fori_loop(0, PIECES + 6, step_fn, 0)

    whole = pl.ds(0, half * 2)

    def sent(kind, ref):
        pltpu.make_async_remote_copy(
            src_ref=ref, dst_ref=ref, send_sem=send.at[kind], recv_sem=recv.at[kind, 0],
            device_id=to_core, device_id_type=MESH,
        ).wait_send()

    for way in range(2):
        sent(way, part.at[0, way])
        sent(2 + way, part.at[1 + way])
    for kind in range(4, 12):
        sent(kind, done)
    for kind in range(8):
        mirror_copy(kind, whole).wait()
    pltpu.make_async_copy(done, out_ref.at[dp], loc_sem.at[0]).wait()
    small_own.wait()
    to_other_core(0).wait_send()
    for kind in range(1, 5):
        to_other_core(kind).wait()
    for kind in range(9):
        text_copy(kind).wait_send()
    for kind in range(5, 9):
        text_copy(kind).wait_recv()


def image_pairs(tokens, weights, gain, q_gain, gate, text, w_query, w_out, attn_gain):
    half, width = tokens.shape
    heads = weights.shape[0]
    patches = half * 2
    any_spec = pl.BlockSpec(memory_space=pl.ANY)

    def like(array):
        return jax.ShapeDtypeStruct(array.shape, array.dtype)

    return pl.pallas_call(
        kv_kernel,
        name="kv",
        out_shape=[
            jax.ShapeDtypeStruct((2, 8, patches, 256), BF),
            jax.ShapeDtypeStruct((8,) + text.shape[1:], BF),
            like(w_query),
            like(w_out),
            like(attn_gain),
            jax.ShapeDtypeStruct((2, 2, 128), F32),
        ],
        in_specs=[any_spec] * 2
        + [pl.BlockSpec(memory_space=pltpu.VMEM)] * 2
        + [pl.BlockSpec(memory_space=pltpu.SMEM)]
        + [any_spec] * 4,
        out_specs=[any_spec] * 6,
        scratch_shapes=[
            pltpu.VMEM((2, 128), F32),
            pltpu.VMEM((patches, width), BF),
            pltpu.VMEM((4, 2, width, 256), BF),
            pltpu.VMEM((4, 2, patches, 256), BF),
            pltpu.VMEM((2, patches, 256), BF),
            pltpu.VMEM((2, 2, patches, 256), BF),
            pltpu.VMEM((patches, 256), BF),
            pltpu.VMEM((patches, 256), BF),
            pltpu.SemaphoreType.DMA((PIECES // 2,)),
            pltpu.SemaphoreType.DMA((8,)),
            pltpu.SemaphoreType.DMA((2,)),
            pltpu.SemaphoreType.DMA((5,)),
            pltpu.SemaphoreType.DMA((5,)),
            pltpu.SemaphoreType.DMA((9,)),
            pltpu.SemaphoreType.DMA((9,)),
            pltpu.SemaphoreType.DMA((20,)),
            pltpu.SemaphoreType.DMA((12, PIECES)),
            pltpu.SemaphoreType.DMA((8,)),
        ],
        compiler_params=pltpu.CompilerParams(
            collective_id=0, has_side_effects=True, vmem_limit_bytes=60 * 2**20
        ),
        cost_estimate=pl.CostEstimate(
            flops=2 * patches * width * heads * 256, bytes_accessed=40 * 2**20, transcendentals=0
        ),
    )(tokens, weights, gain, q_gain, gate, text, w_query, w_out, attn_gain)


KEY_PARTS = ((0, 512), (512, 512), (1024, 576))


class LayerLoad:
    def __init__(self, layer, own, other, dst, sem):
        self.here = lax.axis_index("section") == layer
        self.own = pltpu.make_async_copy(own, dst, sem)
        self.other = pltpu.make_async_copy(other, dst, sem)

    def start(self):
        pl.when(self.here)(lambda: self.own.start())
        pl.when(jnp.logical_not(self.here))(lambda: self.other.start())

    def wait(self):
        self.own.wait()


def add_to_query(acc, sq, block, gain, weights):
    values = block.astype(F32)
    sq[...] += jnp.sum(values * values, axis=-1, keepdims=True)
    acc[...] += jnp.dot((values * gain).astype(BF), weights, preferred_element_type=F32)


def finish_query(acc, sq, q_gain, query):
    inverse = lax.rsqrt(sq[:, :1] * (1.0 / 8192.0) + 1e-05)
    for head in range(4):
        one = acc[:, head * 128:(head + 1) * 128] * inverse
        one = one * lax.rsqrt(jnp.mean(one * one, axis=-1, keepdims=True) + 1e-05)
        query[head * 128:(head + 1) * 128, :] = (one * q_gain * 128.0 ** -0.5).astype(BF)


def attend(layer, choice_ref, valid_ref, query, pairs_ref, att_ref, tiles, total, norm, sem, before=None):
    core = lax.axis_index("section")
    first = choice_ref[core, 0, 0]
    second = choice_ref[core, 0, 1]
    other = second != first
    plan = (
        (first, 0, None),
        (first, 1, valid_ref[first] > 1),
        (second, 0, other),
        (second, 1, other & (valid_ref[second] > 1)),
    )

    def copy(slot):
        image, tile, _ = plan[slot]
        return pltpu.make_async_copy(
            pairs_ref.at[layer, image, pl.ds(tile * TILE_TOK, TILE_TOK)], tiles.at[slot], sem.at[slot]
        )

    def run(slot, fn):
        allowed = plan[slot][2]
        if allowed is None:
            fn()
        else:
            pl.when(allowed)(fn)

    for slot in range(4):
        run(slot, lambda slot=slot: copy(slot).start())
    total[...] = jnp.zeros_like(total)
    norm[...] = jnp.zeros_like(norm)
    if before is not None:
        before()

    def one(slot):
        copy(slot).wait()
        for start, size in KEY_PARTS:
            scores = lax.dot_general(
                query[...], tiles[slot, start:start + size, 0:128],
                (((1,), (1,)), ((), ())), preferred_element_type=F32,
            )
            expo = jnp.exp(scores)
            norm[...] += jnp.sum(expo, axis=-1, keepdims=True)
            total[...] += jnp.dot(
                expo.astype(BF), tiles[slot, start:start + size, 128:256], preferred_element_type=F32
            )

    for slot in range(4):
        run(slot, functools.partial(one, slot))
    for head in range(4):
        at = slice(head * 128, (head + 1) * 128)
        att_ref[:, at] = (total[at, :] / norm[at, :1]).astype(BF)


def first_attention(
    choice_ref, valid_ref, pairs_ref, text_ref, text_all_ref, wq_ref, wq_other_ref,
    attn_ref, attn_other_ref, small_ref, att_ref,
    tiles, total, norm, sem, hidden, wq, attn, small, acc, sq, query, load_sem, wq_sem,
):
    core = lax.axis_index("section")
    tensor = lax.axis_index("tensor")
    attn_load = LayerLoad(0, attn_ref, attn_other_ref, attn, load_sem.at[8])
    small_load = pltpu.make_async_copy(small_ref.at[0], small, load_sem.at[9])
    attn_load.start()
    small_load.start()
    chunks = []
    for step in range(8):
        block = (tensor + step) % 8
        src = text_ref.at[core] if step == 0 else text_all_ref.at[block]
        at = pl.ds(pl.multiple_of(block * 1024, 1024), 1024)
        chunks.append((
            at,
            pltpu.make_async_copy(src, hidden.at[step], load_sem.at[step]),
            LayerLoad(0, wq_ref.at[at], wq_other_ref.at[at], wq.at[step], wq_sem.at[step]),
        ))
        chunks[-1][1].start()
        chunks[-1][2].start()

    def before():
        acc[...] = jnp.zeros_like(acc)
        sq[...] = jnp.zeros_like(sq)
        attn_load.wait()
        small_load.wait()
        for step, (at, text_load, wq_load) in enumerate(chunks):
            text_load.wait()
            wq_load.wait()
            add_to_query(acc, sq, hidden[step], attn[:, at], wq[step])
        finish_query(acc, sq, small[0:1, :], query)

    attend(0, choice_ref, valid_ref, query, pairs_ref, att_ref, tiles, total, norm, sem, before)


def second_attention(choice_ref, valid_ref, pairs_ref, query_ref, att_ref, tiles, total, norm, sem):
    attend(1, choice_ref, valid_ref, query_ref, pairs_ref, att_ref, tiles, total, norm, sem)


ATTEND_SCRATCH = [
    pltpu.VMEM((4, TILE_TOK, 256), BF),
    pltpu.VMEM((512, 128), F32),
    pltpu.VMEM((512, 128), F32),
    pltpu.SemaphoreType.DMA((4,)),
]


def attention_first(choice, valid, *arrays):
    any_spec = pl.BlockSpec(memory_space=pl.ANY)
    smem = pl.BlockSpec(memory_space=pltpu.SMEM)
    return pl.pallas_call(
        first_attention,
        name="attend0",
        out_shape=jax.ShapeDtypeStruct((128, 512), BF),
        in_specs=[smem, smem] + [any_spec] * 8,
        out_specs=pl.BlockSpec(memory_space=pltpu.VMEM),
        scratch_shapes=ATTEND_SCRATCH + [
            pltpu.VMEM((8, 128, 1024), BF),
            pltpu.VMEM((8, 1024, 512), BF),
            pltpu.VMEM((1, 8192), F32),
            pltpu.VMEM((2, 128), F32),
            pltpu.VMEM((128, 512), F32),
            pltpu.VMEM((128, 128), F32),
            pltpu.VMEM((512, 128), BF),
            pltpu.SemaphoreType.DMA((10,)),
            pltpu.SemaphoreType.DMA((8,)),
        ],
        compiler_params=pltpu.CompilerParams(vmem_limit_bytes=60 * 2**20),
        cost_estimate=pl.CostEstimate(flops=3 * 10**9, bytes_accessed=14 * 2**20, transcendentals=3 * 10**6),
    )(choice, valid, *arrays)


def attention_second(choice, valid, pairs, query):
    any_spec = pl.BlockSpec(memory_space=pl.ANY)
    smem = pl.BlockSpec(memory_space=pltpu.SMEM)
    vmem = pl.BlockSpec(memory_space=pltpu.VMEM)
    return pl.pallas_call(
        second_attention,
        name="attend1",
        out_shape=jax.ShapeDtypeStruct((128, 512), BF),
        in_specs=[smem, smem, any_spec, vmem],
        out_specs=vmem,
        scratch_shapes=ATTEND_SCRATCH,
        compiler_params=pltpu.CompilerParams(vmem_limit_bytes=60 * 2**20),
        cost_estimate=pl.CostEstimate(flops=2 * 10**9, bytes_accessed=4 * 2**20, transcendentals=3 * 10**6),
    )(choice, valid, pairs, query)


Y_ROWS = 80
NEAR = pl.ds(0, Y_ROWS)
REST = pl.ds(Y_ROWS, 128 - Y_ROWS)
HALF = (pl.ds(0, 512), pl.ds(512, 512))


def project_and_sum(layer, att_ref, wo_ref, wo_other_ref, scratch, greet):
    wo, part, from_y1, from_y2, from_z, from_c, from_c1, from_c2, wo_sem, send, recv = scratch
    x, zh, zl, y, core = position()
    y_up, y_dn = (y + 1) % 4, (y + 3) % 4
    to_y = (device(x, zh, zl, y_up, core), device(x, zh, zl, y_dn, core))
    to_z = device(x, zh, 1 - zl, y, core)
    order = ((0, 0), (0, 1), (2, 0), (1, 1), (1, 0), (2, 1), (3, 0), (3, 1))
    loads = {}
    for ring, side in order:
        block = side * 4 + ((y + 2) % 4, y_up, y_dn, y)[ring]
        at = pl.ds(pl.multiple_of(block * 1024, 1024), 1024)
        loads[ring, side] = LayerLoad(
            layer, wo_ref.at[:, at], wo_other_ref.at[:, at], wo.at[ring, side], wo_sem.at[ring * 2 + side]
        )
        loads[ring, side].start()

    def remote(kind, src, dst, peer):
        return pltpu.make_async_remote_copy(
            src_ref=src, dst_ref=dst, send_sem=send.at[kind], recv_sem=recv.at[kind],
            device_id=peer, device_id_type=MESH,
        )

    far = [remote(way, part.at[0, way, NEAR], from_y1.at[way], to_y[way]) for way in range(2)]
    near = {
        (ring, side): remote(2 + ring * 2 + side - 2, part.at[ring, side, NEAR], from_y2.at[ring - 1, side], to_y[ring - 1])
        for ring in (1, 2) for side in range(2)
    }
    cross = [remote(6 + ring, part.at[ring, 1 - zl, REST], from_c.at[ring], to_z) for ring in range(4)]
    cross_far = [
        remote(10 + way, part.at[0, zl, REST, HALF[way]], from_c1.at[way], to_y[way]) for way in range(2)
    ]
    cross_near = [remote(12 + way, part.at[1 + way, zl, REST], from_c2.at[way], to_y[way]) for way in range(2)]
    last = remote(14, part.at[3, 1 - zl, NEAR], from_z, to_z)
    at_once = {(0, 0): far[0], (0, 1): far[1], (2, 0): near[2, 0], (1, 1): near[1, 1]}

    for ring, side in order:
        loads[ring, side].wait()
        part[ring, side] = jnp.dot(att_ref[...], wo[ring, side], preferred_element_type=F32).astype(BF)
        if (ring, side) == (0, 0):
            greet()
        if (ring, side) in at_once:
            at_once[ring, side].start()

        @pl.when(zl != side)
        def _():
            cross[ring].start()

    def add(ring, side, rows, columns, addend):
        part[ring, side, rows, columns] = (
            part[ring, side, rows, columns].astype(F32) + addend.astype(F32)
        ).astype(BF)

    every = slice(None)
    for way, key in ((0, (1, 0)), (1, (2, 1))):
        far[way].wait_recv()
        add(*key, NEAR, every, from_y1[way])
        near[key].start()
    cross[0].wait_recv()
    add(0, zl, REST, every, from_c[0])
    for way in range(2):
        cross_far[way].start()
    for ring in range(1, 4):
        cross[ring].wait_recv()
        add(ring, zl, REST, every, from_c[ring])
    for key in near:
        near[key].wait_recv()
    add(3, 1 - zl, NEAR, every, from_y2[0, 1 - zl].astype(F32) + from_y2[1, 1 - zl].astype(F32))
    last.start()
    for way in range(2):
        cross_far[way].wait_recv()
        add(1 + way, zl, REST, HALF[way], from_c1[way])
        cross_near[way].start()
    first = part[3, zl, NEAR, :].astype(F32) + from_y2[0, zl].astype(F32) + from_y2[1, zl].astype(F32)
    second = part[3, zl, REST, :].astype(F32)
    last.wait_recv()
    first = first + from_z[...].astype(F32)
    for way in range(2):
        cross_near[way].wait_recv()
        second = second + from_c2[way].astype(F32)

    def drain():
        for copy in far + list(near.values()) + cross + cross_far + cross_near + [last]:
            copy.wait_send()

    return first, second, drain


SUM_SCRATCH = [
    pltpu.VMEM((4, 2, 512, 1024), BF),
    pltpu.VMEM((4, 2, 128, 1024), BF),
    pltpu.VMEM((2, Y_ROWS, 1024), BF),
    pltpu.VMEM((2, 2, Y_ROWS, 1024), BF),
    pltpu.VMEM((Y_ROWS, 1024), BF),
    pltpu.VMEM((4, 128 - Y_ROWS, 1024), BF),
    pltpu.VMEM((2, 128 - Y_ROWS, 512), BF),
    pltpu.VMEM((2, 128 - Y_ROWS, 1024), BF),
    pltpu.SemaphoreType.DMA((8,)),
    pltpu.SemaphoreType.DMA((15,)),
    pltpu.SemaphoreType.DMA((15,)),
]


def greeting(peers):
    barrier = pltpu.get_barrier_semaphore()
    for peer in peers:
        pl.semaphore_signal(barrier, inc=1, device_id=peer, device_id_type=MESH)
    pl.semaphore_wait(barrier, len(peers))


def middle_kernel(
    att_ref, text_ref, wo_ref, wo_other_ref, wq_ref, wq_other_ref,
    attn_ref, attn_other_ref, small_ref, query_ref, upd_ref, *scratch,
):
    hidden, wq, attn, small, text, acc, sq, wq_sem, ag_send, ag_recv, par_sem = scratch[len(SUM_SCRATCH):]
    x, zh, zl, y, core = position()
    y_up, y_dn = (y + 1) % 4, (y + 3) % 4
    to_up = device(x, zh, zl, y_up, core)
    to_dn = device(x, zh, zl, y_dn, core)
    to_z = device(x, zh, 1 - zl, y, core)
    par_copies = [
        pltpu.make_async_copy(small_ref, small, par_sem.at[0]),
        LayerLoad(1, attn_ref, attn_other_ref, attn, par_sem.at[1]),
        pltpu.make_async_copy(text_ref.at[core], text, par_sem.at[2]),
    ]
    for copy in par_copies:
        copy.start()

    first, second, drain = project_and_sum(
        0, att_ref, wo_ref, wo_other_ref, scratch[:len(SUM_SCRATCH)], lambda: greeting([to_up, to_dn, to_z])
    )
    mine, across = zl * 4, (1 - zl) * 4
    own, left, right, far = mine + y, mine + y_dn, mine + y_up, mine + (y + 2) % 4
    z_own, z_left, z_right, z_far = across + y, across + y_dn, across + y_up, across + (y + 2) % 4
    order = [own, left, right, z_own, z_left, z_right, far, z_far]
    chunks = []
    for k, block in enumerate(order):
        at = pl.ds(pl.multiple_of(block * 1024, 1024), 1024)
        chunks.append(LayerLoad(1, wq_ref.at[at], wq_other_ref.at[at], wq.at[k], wq_sem.at[k]))
        chunks[k].start()
    for copy in par_copies:
        copy.wait()
    gate = small[0, 1:2, 0:1]

    def remote(kind, block, rows, peer, half=None):
        ref = hidden.at[block, rows] if half is None else hidden.at[block, rows, HALF[half]]
        return pltpu.make_async_remote_copy(
            src_ref=ref, dst_ref=ref, send_sem=ag_send.at[kind], recv_sem=ag_recv.at[kind],
            device_id=peer, device_id_type=MESH,
        )

    copies = [
        remote(0, own, NEAR, to_z), remote(1, own, NEAR, to_up), remote(2, own, NEAR, to_dn),
        remote(3, own, REST, to_up), remote(4, own, REST, to_dn), remote(5, own, REST, to_z),
        remote(6, left, REST, to_up, 0), remote(7, right, REST, to_dn, 1),
        remote(8, left, REST, to_z), remote(9, right, REST, to_z), remote(10, far, REST, to_z),
        remote(11, z_own, NEAR, to_up), remote(12, z_own, NEAR, to_dn),
        remote(13, left, NEAR, to_up, 0), remote(14, right, NEAR, to_dn, 1),
        remote(15, z_left, NEAR, to_up, 0), remote(16, z_right, NEAR, to_dn, 1),
    ]

    def begin(*kinds):
        for kind in kinds:
            copies[kind].start()

    def arrive(*kinds):
        for kind in kinds:
            copies[kind].wait_recv()

    def use(k):
        chunks[k].wait()
        block = order[k]
        at = pl.ds(pl.multiple_of(block * 1024, 1024), 1024)
        add_to_query(acc, sq, hidden[block], attn[:, at], wq[k])

    hidden[own, NEAR, :] = (text[NEAR, :].astype(F32) + gate * first).astype(BF)
    begin(0)
    hidden[own, REST, :] = (text[REST, :].astype(F32) + gate * second).astype(BF)
    begin(3, 4, 1, 2, 5)
    upd_ref[...] = hidden[own]
    acc[...] = jnp.zeros_like(acc)
    sq[...] = jnp.zeros_like(sq)
    use(0)
    arrive(3)
    begin(6, 8)
    arrive(4)
    begin(7, 9)
    arrive(0)
    begin(11, 12)
    arrive(1)
    begin(13)
    arrive(2)
    begin(14)
    use(1)
    use(2)
    arrive(6, 7)
    begin(10)
    arrive(11)
    begin(15)
    arrive(12)
    begin(16)
    arrive(5)
    use(3)
    arrive(8)
    use(4)
    arrive(9)
    use(5)
    arrive(13, 14)
    use(6)
    arrive(10, 15, 16)
    use(7)
    finish_query(acc, sq, small[1, 0:1, :], query_ref)
    drain()
    for copy in copies:
        copy.wait_send()


def last_kernel(
    att_ref, upd_ref, wo_ref, wo_other_ref, small_ref, out_ref, *scratch,
):
    small, last, core_send, core_recv, par_sem = scratch[len(SUM_SCRATCH):]
    x, zh, zl, y, core = position()
    to_y_up = device(x, zh, zl, (y + 1) % 4, core)
    to_y_dn = device(x, zh, zl, (y + 3) % 4, core)
    to_z_lo = device(x, zh, 1 - zl, y, core)
    to_core = device(x, zh, zl, y, 1 - core)
    par_copy = pltpu.make_async_copy(small_ref.at[1], small, par_sem.at[0])
    par_copy.start()
    send_first = pltpu.make_async_remote_copy(
        src_ref=upd_ref, dst_ref=out_ref.at[1], send_sem=core_send.at[0], recv_sem=core_recv.at[0],
        device_id=to_core, device_id_type=MESH,
    )
    send_last = pltpu.make_async_remote_copy(
        src_ref=last, dst_ref=out_ref.at[0], send_sem=core_send.at[1], recv_sem=core_recv.at[1],
        device_id=to_core, device_id_type=MESH,
    )

    def greet():
        greeting([to_y_up, to_y_dn, to_z_lo, to_core])

        @pl.when(core == 1)
        def _():
            send_first.start()

    first, second, drain = project_and_sum(1, att_ref, wo_ref, wo_other_ref, scratch[:len(SUM_SCRATCH)], greet)
    par_copy.wait()
    gate = small[1:2, 0:1]
    last[NEAR, :] = (upd_ref[NEAR, :].astype(F32) + gate * first).astype(BF)
    last[REST, :] = (upd_ref[REST, :].astype(F32) + gate * second).astype(BF)

    @pl.when(core == 0)
    def _():
        send_last.start()
        out_ref[0] = upd_ref[...]
        send_first.wait_recv()
        send_last.wait_send()

    @pl.when(core == 1)
    def _():
        out_ref[1] = last[...]
        send_first.wait_send()
        send_last.wait_recv()

    drain()


def middle(att, text, *weights):
    any_spec = pl.BlockSpec(memory_space=pl.ANY)
    vmem = pl.BlockSpec(memory_space=pltpu.VMEM)
    return pl.pallas_call(
        middle_kernel,
        name="middle",
        out_shape=[jax.ShapeDtypeStruct((512, 128), BF), jax.ShapeDtypeStruct((128, 1024), BF)],
        in_specs=[vmem] + [any_spec] * 8,
        out_specs=[vmem] * 2,
        scratch_shapes=SUM_SCRATCH + [
            pltpu.VMEM((8, 128, 1024), BF),
            pltpu.VMEM((8, 1024, 512), BF),
            pltpu.VMEM((1, 8192), F32),
            pltpu.VMEM((2, 2, 128), F32),
            pltpu.VMEM((128, 1024), BF),
            pltpu.VMEM((128, 512), F32),
            pltpu.VMEM((128, 128), F32),
            pltpu.SemaphoreType.DMA((8,)),
            pltpu.SemaphoreType.DMA((17,)),
            pltpu.SemaphoreType.DMA((17,)),
            pltpu.SemaphoreType.DMA((3,)),
        ],
        compiler_params=pltpu.CompilerParams(
            collective_id=1, has_side_effects=True, vmem_limit_bytes=60 * 2**20
        ),
    )(att, text, *weights)


def last_step(att, upd, *weights):
    any_spec = pl.BlockSpec(memory_space=pl.ANY)
    vmem = pl.BlockSpec(memory_space=pltpu.VMEM)
    return pl.pallas_call(
        last_kernel,
        name="last",
        out_shape=jax.ShapeDtypeStruct((2, 128, 1024), BF),
        in_specs=[vmem, vmem] + [any_spec] * 3,
        out_specs=vmem,
        scratch_shapes=SUM_SCRATCH + [
            pltpu.VMEM((2, 128), F32),
            pltpu.VMEM((128, 1024), BF),
            pltpu.SemaphoreType.DMA((2,)),
            pltpu.SemaphoreType.DMA((2,)),
            pltpu.SemaphoreType.DMA((1,)),
        ],
        compiler_params=pltpu.CompilerParams(
            collective_id=2, has_side_effects=True, vmem_limit_bytes=60 * 2**20
        ),
    )(att, upd, *weights)


def local(
    text_hidden,
    image_tokens,
    attn_gain,
    w_query,
    w_keyval,
    q_gain,
    k_gain,
    w_out,
    gate,
    image_choice,
    valid_tiles,
):
    text = text_hidden[:, 0]
    weights = jnp.transpose(w_keyval[0], (1, 0, 2))
    wq, wo = w_query[0], w_out[0]
    pairs, text_all, wq_other, wo_other, attn_other, small = image_pairs(
        image_tokens[0], weights, k_gain, q_gain, gate, text, wq, wo, attn_gain
    )
    gains = (attn_gain, attn_other, small)
    att = attention_first(image_choice, valid_tiles, pairs, text, text_all, wq, wq_other, *gains)
    query, updated = middle(att, text, wo, wo_other, wq, wq_other, *gains)
    att = attention_second(image_choice, valid_tiles, pairs, query)
    result = last_step(att, updated, wo, wo_other, small)
    return result[None, :, None]


def solution(mesh):
    placed = (
        P(None, "dp", None, "tensor"),
        P("dp", "section", "tensor"),
        P("section", None),
        P("section", None, "tensor"),
        P("section", "tensor", None, None),
        P("section", None),
        P("section", None),
        P("section", "tensor", None),
        P("section"),
        P(None, "dp", None),
        P(),
    )
    return jax.shard_map(
        local,
        mesh=mesh,
        in_specs=placed,
        out_specs=P("section", None, "dp", None, "tensor"),
        check_vma=False,
    )
```

```python
import functools

import jax
import jax.numpy as jnp
from jax import lax
from jax.experimental import pallas as pl
from jax.experimental.pallas import tpu as pltpu
from jax.sharding import PartitionSpec as P

TILE_TOK = 1600
PIECES = 20
GROUP = 2
JOINT = 1
MESH = pl.DeviceIdType.MESH
BF = jnp.bfloat16
F32 = jnp.float32


def position():
    dp = lax.axis_index("dp")
    tensor = lax.axis_index("tensor")
    return dp // 2, dp % 2, tensor // 4, tensor % 4, lax.axis_index("section")


def device(x, zh, zl, y, core):
    return (x * 2 + zh, zl * 4 + y, core)


def kv_kernel(
    tok_ref, w_ref, gain_ref, q_gain_ref, gate_ref, text_ref, wq_ref, wo_ref, attn_ref,
    pairs_ref, text_out_ref, wq_out_ref, wo_out_ref, attn_out_ref, small_out_ref,
    small, tok, wgt, part, from_y1, from_y2, from_z, done,
    tok_sem, w_sem, loc_sem, core_send, core_recv, text_send, text_recv, send, recv, mirror_recv,
):
    x, zh, zl, y, core = position()
    dp = x * 2 + zh
    half = tok_ref.shape[0]
    out_ref = pairs_ref.at[core]
    rows = half * 2 // PIECES
    y_up, y_dn = (y + 1) % 4, (y + 3) % 4
    x_up, x_dn = (x + 1) % 4, (x + 3) % 4
    to_y = (device(x, zh, zl, y_up, core), device(x, zh, zl, y_dn, core))
    to_x = (device(x_up, zh, zl, y, core), device(x_dn, zh, zl, y, core))
    to_z_lo = device(x, zh, 1 - zl, y, core)
    to_z_hi = device(x, 1 - zh, zl, y, core)
    to_core = device(x, zh, zl, y, 1 - core)
    peers = to_y + to_x + (to_z_lo, to_z_hi, to_core)

    barrier = pltpu.get_barrier_semaphore()
    for peer in peers:
        pl.semaphore_signal(barrier, inc=1, device_id=peer, device_id_type=MESH)

    def first_row(piece):
        return pl.multiple_of(((piece + core * (PIECES // 2)) % PIECES) * rows, rows)

    def rows_of(piece):
        return pl.ds(first_row(piece), rows)

    def head_of(ring, side):
        return side * 4 + ((y + 2) % 4, y_up, y_dn, y)[ring]

    def tok_copy(piece):
        return pltpu.make_async_copy(
            tok_ref.at[pl.ds(pl.multiple_of(piece * rows, rows), rows)],
            tok.at[pl.ds(pl.multiple_of(core * half + piece * rows, rows), rows)],
            tok_sem.at[piece],
        )

    def w_copy(ring, side):
        return pltpu.make_async_copy(
            w_ref.at[head_of(ring, side)], wgt.at[ring, side], w_sem.at[ring * 2 + side]
        )

    def to_other_core(kind):
        src, dst = (
            (tok_ref, tok.at[pl.ds(pl.multiple_of(core * half, half), half)]),
            (attn_ref, attn_out_ref),
            (small, small_out_ref.at[core]),
            (wq_ref, wq_out_ref),
            (wo_ref, wo_out_ref),
        )[kind]
        return pltpu.make_async_remote_copy(
            src_ref=src, dst_ref=dst, send_sem=core_send.at[kind], recv_sem=core_recv.at[kind],
            device_id=to_core, device_id_type=MESH,
        )

    def text_copy(kind):
        own = zl * 4
        other = (1 - zl) * 4
        block = (
            own + y, own + y, own + y, other + y, other + y, own + y_dn, own + y_up, other + y_dn, other + y_up
        )[kind]
        dst = text_out_ref.at[block]
        src = text_ref.at[core] if kind < 3 else dst
        if kind >= 5:
            at = pl.ds(((kind - 5) % 2) * 64, 64)
            src, dst = src.at[at], dst.at[at]
        peer = to_z_lo if kind == 2 else to_y[(0, 1, 2, 0, 1, 0, 1, 0, 1)[kind]]
        return pltpu.make_async_remote_copy(
            src_ref=src, dst_ref=dst, send_sem=text_send.at[kind], recv_sem=text_recv.at[kind],
            device_id=peer, device_id_type=MESH,
        )

    def remote(kind, piece, src, dst, peer):
        return pltpu.make_async_remote_copy(
            src_ref=src, dst_ref=dst,
            send_sem=send.at[kind], recv_sem=recv.at[kind, piece],
            device_id=peer, device_id_type=MESH,
        )

    def y1_copy(way, piece):
        at = rows_of(piece)
        return remote(way, piece, part.at[0, way, at], from_y1.at[way, at], to_y[way])

    def y2_copy(way, piece):
        at = rows_of(piece)
        return remote(2 + way, piece, part.at[1 + way, :, at], from_y2.at[way, :, at], to_y[way])

    def z_copy(piece):
        at = rows_of(piece)
        return remote(4, piece, part.at[3, 1 - zl, at], from_z.at[at], to_z_lo)

    def own_copy(way, piece):
        at = rows_of(piece)
        return remote(5 + way, piece, done.at[at], out_ref.at[dp, at], to_z_hi if way == 0 else to_x[way - 1])

    def own_local(piece):
        at = rows_of(piece)
        return pltpu.make_async_copy(done.at[at], out_ref.at[dp, at], loc_sem.at[0])

    def pair_copy(way, piece):
        ref = out_ref.at[x * 2 + 1 - zh, rows_of(piece)]
        return remote(8 + way, piece, ref, ref, to_x[way])

    def forward_copy(way, piece):
        image = (x_dn * 2 + zh, x_up * 2 + 1 - zh)[way]
        ref = out_ref.at[image, rows_of(piece)]
        return remote(10 + way, piece, ref, ref, to_x[way])

    def mirror_copy(kind, at):
        across = (x + 2) % 4
        place = (
            (x, zh), (x, 1 - zh), (x_dn, zh), (x_up, zh), (x_dn, 1 - zh), (x_up, 1 - zh), (across, zh), (across, 1 - zh)
        )[kind]
        ref = out_ref.at[place[0] * 2 + place[1], at]
        return pltpu.make_async_remote_copy(
            src_ref=done.at[at] if kind == 0 else ref, dst_ref=ref,
            send_sem=send.at[12 + kind], recv_sem=mirror_recv.at[kind],
            device_id=to_core, device_id_type=MESH,
        )

    def mirror(kinds, piece):
        @pl.when(piece % GROUP == GROUP - 1)
        def _():
            at = pl.ds(first_row(piece - (GROUP - 1)), rows * GROUP)
            for kind in kinds:
                mirror_copy(kind, at).start()

    for ring in range(4):
        for side in range(2):
            w_copy(ring, side).start()

    def start_tok(piece, carry):
        tok_copy(piece).start()
        return carry

    lax.fori_loop(0, PIECES // 2, start_tok, 0)
    small[0:1, :] = q_gain_ref[...]
    small[1:2, :] = jnp.tanh(jnp.broadcast_to(gate_ref[0], (1, 128)))
    small_own = pltpu.make_async_copy(small, small_out_ref.at[core], loc_sem.at[1])
    small_own.start()
    pl.semaphore_wait(barrier, len(peers))
    to_other_core(0).start()
    text_copy(2).start()
    for kind in range(1, 5):
        to_other_core(kind).start()

    def add(ring, side, at, addend):
        part[ring, side, at, :] = (part[ring, side, at, :].astype(F32) + addend.astype(F32)).astype(BF)

    def step_fn(it, carry):
        @pl.when((it < PIECES) & (it % JOINT == 0))
        def _():
            piece = it

            @pl.when(piece < PIECES // 2)
            def _():
                for more in range(JOINT):
                    tok_copy(piece + more).wait()

            @pl.when(piece == PIECES // 2)
            def _():
                to_other_core(0).wait_recv()

            at = pl.ds(first_row(piece), rows * JOINT)
            for ring in range(4):
                for side in range(2):
                    @pl.when(it == 0)
                    def _():
                        w_copy(ring, side).wait()

                    part[ring, side, at, :] = jnp.dot(
                        tok[at, :], wgt[ring, side], preferred_element_type=F32
                    ).astype(BF)
                    if ring == 0:
                        for more in range(JOINT):
                            y1_copy(side, piece + more).start()

        @pl.when((it >= 1) & (it < PIECES + 1))
        def _():
            piece = it - 1
            at = rows_of(piece)
            for way in range(2):
                y1_copy(way, piece).wait_recv()
                add(1 + way, way, at, from_y1[way, at, :])
                y2_copy(way, piece).start()

            @pl.when(piece == PIECES - 1)
            def _():
                text_copy(2).wait_recv()
                for kind in (0, 1, 3, 4):
                    text_copy(kind).start()

        @pl.when((it >= 2) & (it < PIECES + 2))
        def _():
            piece = it - 2
            at = rows_of(piece)
            for way in range(2):
                y2_copy(way, piece).wait_recv()
            add(
                3, 1 - zl, at,
                from_y2[0, 1 - zl, at, :].astype(F32) + from_y2[1, 1 - zl, at, :].astype(F32),
            )
            z_copy(piece).start()

        @pl.when((it >= 3) & (it < PIECES + 3))
        def _():
            piece = it - 3
            at = rows_of(piece)
            z_copy(piece).wait_recv()
            total = (
                part[3, zl, at, :].astype(F32)
                + from_y2[0, zl, at, :].astype(F32) + from_y2[1, zl, at, :].astype(F32)
                + from_z[at, :].astype(F32)
            )
            keys = total[:, :128]
            keys = keys * lax.rsqrt(jnp.mean(keys * keys, axis=-1, keepdims=True) + 1e-05)
            done[at, 0:128] = (keys * gain_ref[...]).astype(BF)
            done[at, 128:256] = total[:, 128:].astype(BF)
            for way in range(3):
                own_copy(way, piece).start()
            own_local(piece).start()
            mirror((0,), piece)

        @pl.when((it >= 4) & (it < PIECES + 4))
        def _():
            piece = it - 4
            own_copy(0, piece).wait_recv()
            for way in range(2):
                pair_copy(way, piece).start()

            @pl.when(piece == PIECES - 1)
            def _():
                for kind in (0, 1):
                    text_copy(kind).wait_recv()
                    text_copy(kind + 5).start()
            mirror((1,), piece)

        @pl.when((it >= 5) & (it < PIECES + 5))
        def _():
            piece = it - 5
            own_copy(1, piece).wait_recv()
            pair_copy(1, piece).wait_recv()
            for way in range(2):
                forward_copy(way, piece).start()
            own_copy(2, piece).wait_recv()
            pair_copy(0, piece).wait_recv()
            mirror((2, 3, 4, 5), piece)

            @pl.when(piece == PIECES - 1)
            def _():
                for kind in (3, 4):
                    text_copy(kind).wait_recv()
                    text_copy(kind + 4).start()

        @pl.when(it >= 6)
        def _():
            piece = it - 6
            for way in range(2):
                forward_copy(way, piece).wait_recv()
            mirror((6, 7), piece)

        return carry

    lax.fori_loop(0, PIECES + 6, step_fn, 0)

    whole = pl.ds(0, half * 2)

    def sent(kind, ref):
        pltpu.make_async_remote_copy(
            src_ref=ref, dst_ref=ref, send_sem=send.at[kind], recv_sem=recv.at[kind, 0],
            device_id=to_core, device_id_type=MESH,
        ).wait_send()

    for way in range(2):
        sent(way, part.at[0, way])
        sent(2 + way, part.at[1 + way])
    for kind in range(4, 12):
        sent(kind, done)
    for kind in range(8):
        mirror_copy(kind, whole).wait()
    pltpu.make_async_copy(done, out_ref.at[dp], loc_sem.at[0]).wait()
    small_own.wait()
    to_other_core(0).wait_send()
    for kind in range(1, 5):
        to_other_core(kind).wait()
    for kind in range(9):
        text_copy(kind).wait_send()
    for kind in range(5, 9):
        text_copy(kind).wait_recv()


def image_pairs(tokens, weights, gain, q_gain, gate, text, w_query, w_out, attn_gain):
    half, width = tokens.shape
    heads = weights.shape[0]
    patches = half * 2
    any_spec = pl.BlockSpec(memory_space=pl.ANY)

    def like(array):
        return jax.ShapeDtypeStruct(array.shape, array.dtype)

    return pl.pallas_call(
        kv_kernel,
        name="kv",
        out_shape=[
            jax.ShapeDtypeStruct((2, 8, patches, 256), BF),
            jax.ShapeDtypeStruct((8,) + text.shape[1:], BF),
            like(w_query),
            like(w_out),
            like(attn_gain),
            jax.ShapeDtypeStruct((2, 2, 128), F32),
        ],
        in_specs=[any_spec] * 2
        + [pl.BlockSpec(memory_space=pltpu.VMEM)] * 2
        + [pl.BlockSpec(memory_space=pltpu.SMEM)]
        + [any_spec] * 4,
        out_specs=[any_spec] * 6,
        scratch_shapes=[
            pltpu.VMEM((2, 128), F32),
            pltpu.VMEM((patches, width), BF),
            pltpu.VMEM((4, 2, width, 256), BF),
            pltpu.VMEM((4, 2, patches, 256), BF),
            pltpu.VMEM((2, patches, 256), BF),
            pltpu.VMEM((2, 2, patches, 256), BF),
            pltpu.VMEM((patches, 256), BF),
            pltpu.VMEM((patches, 256), BF),
            pltpu.SemaphoreType.DMA((PIECES // 2,)),
            pltpu.SemaphoreType.DMA((8,)),
            pltpu.SemaphoreType.DMA((2,)),
            pltpu.SemaphoreType.DMA((5,)),
            pltpu.SemaphoreType.DMA((5,)),
            pltpu.SemaphoreType.DMA((9,)),
            pltpu.SemaphoreType.DMA((9,)),
            pltpu.SemaphoreType.DMA((20,)),
            pltpu.SemaphoreType.DMA((12, PIECES)),
            pltpu.SemaphoreType.DMA((8,)),
        ],
        compiler_params=pltpu.CompilerParams(
            collective_id=0, has_side_effects=True, vmem_limit_bytes=60 * 2**20
        ),
        cost_estimate=pl.CostEstimate(
            flops=2 * patches * width * heads * 256, bytes_accessed=40 * 2**20, transcendentals=0
        ),
    )(tokens, weights, gain, q_gain, gate, text, w_query, w_out, attn_gain)


KEY_PARTS = ((0, 512), (512, 512), (1024, 576))


class LayerLoad:
    def __init__(self, layer, own, other, dst, sem):
        self.here = lax.axis_index("section") == layer
        self.own = pltpu.make_async_copy(own, dst, sem)
        self.other = pltpu.make_async_copy(other, dst, sem)

    def start(self):
        pl.when(self.here)(lambda: self.own.start())
        pl.when(jnp.logical_not(self.here))(lambda: self.other.start())

    def wait(self):
        self.own.wait()


def add_to_query(acc, sq, block, gain, weights):
    values = block.astype(F32)
    sq[...] += jnp.sum(values * values, axis=-1, keepdims=True)
    acc[...] += jnp.dot((values * gain).astype(BF), weights, preferred_element_type=F32)


def finish_query(acc, sq, q_gain, query):
    inverse = lax.rsqrt(sq[:, :1] * (1.0 / 8192.0) + 1e-05)
    for head in range(4):
        one = acc[:, head * 128:(head + 1) * 128] * inverse
        one = one * lax.rsqrt(jnp.mean(one * one, axis=-1, keepdims=True) + 1e-05)
        query[head * 128:(head + 1) * 128, :] = (one * q_gain * 128.0 ** -0.5).astype(BF)


def add_tile(query, tiles, image, tile, total, norm, weight=None):
    for start, size in KEY_PARTS:
        at = slice(tile * TILE_TOK + start, tile * TILE_TOK + start + size)
        scores = lax.dot_general(
            query[...], tiles[image, at, 0:128], (((1,), (1,)), ((), ())), preferred_element_type=F32
        )
        expo = jnp.exp(scores)
        sums = jnp.sum(expo, axis=-1, keepdims=True)
        values = jnp.dot(expo.astype(BF), tiles[image, at, 128:256], preferred_element_type=F32)
        norm[...] += sums if weight is None else sums * weight
        total[...] += values if weight is None else values * weight


def side_by_side(total, norm, att_ref):
    for head in range(4):
        at = slice(head * 128, (head + 1) * 128)
        att_ref[:, at] = (total[at, :] / norm[at, :1]).astype(BF)


def attend(layer, choice_ref, valid_ref, query, pairs_ref, att_ref, tiles, total, norm, sem, before=None):
    core = lax.axis_index("section")
    first = choice_ref[core, 0, 0]
    second = choice_ref[core, 0, 1]
    other = second != first
    plan = (
        (first, 0, None),
        (first, 1, valid_ref[first] > 1),
        (second, 0, other),
        (second, 1, other & (valid_ref[second] > 1)),
    )

    def copy(slot):
        image, tile, _ = plan[slot]
        return pltpu.make_async_copy(
            pairs_ref.at[layer, image, pl.ds(tile * TILE_TOK, TILE_TOK)], tiles.at[slot], sem.at[slot]
        )

    def run(slot, fn):
        allowed = plan[slot][2]
        if allowed is None:
            fn()
        else:
            pl.when(allowed)(fn)

    for slot in range(4):
        run(slot, lambda slot=slot: copy(slot).start())
    total[...] = jnp.zeros_like(total)
    norm[...] = jnp.zeros_like(norm)
    if before is not None:
        before()

    def one(slot):
        copy(slot).wait()
        add_tile(query, tiles, slot, 0, total, norm)

    for slot in range(4):
        run(slot, functools.partial(one, slot))
    side_by_side(total, norm, att_ref)


def first_attention(
    choice_ref, valid_ref, pairs_ref, text_ref, text_all_ref, wq_ref, wq_other_ref,
    attn_ref, attn_other_ref, small_ref, att_ref,
    tiles, total, norm, sem, hidden, wq, attn, small, acc, sq, query, load_sem, wq_sem,
):
    core = lax.axis_index("section")
    tensor = lax.axis_index("tensor")
    attn_load = LayerLoad(0, attn_ref, attn_other_ref, attn, load_sem.at[8])
    small_load = pltpu.make_async_copy(small_ref.at[0], small, load_sem.at[9])
    attn_load.start()
    small_load.start()
    chunks = []
    for step in range(8):
        block = (tensor + step) % 8
        src = text_ref.at[core] if step == 0 else text_all_ref.at[block]
        at = pl.ds(pl.multiple_of(block * 1024, 1024), 1024)
        chunks.append((
            at,
            pltpu.make_async_copy(src, hidden.at[step], load_sem.at[step]),
            LayerLoad(0, wq_ref.at[at], wq_other_ref.at[at], wq.at[step], wq_sem.at[step]),
        ))
        chunks[-1][1].start()
        chunks[-1][2].start()

    def before():
        acc[...] = jnp.zeros_like(acc)
        sq[...] = jnp.zeros_like(sq)
        attn_load.wait()
        small_load.wait()
        for step, (at, text_load, wq_load) in enumerate(chunks):
            text_load.wait()
            wq_load.wait()
            add_to_query(acc, sq, hidden[step], attn[:, at], wq[step])
        finish_query(acc, sq, small[0:1, :], query)

    attend(0, choice_ref, valid_ref, query, pairs_ref, att_ref, tiles, total, norm, sem, before)


ATTEND_SCRATCH = [
    pltpu.VMEM((4, TILE_TOK, 256), BF),
    pltpu.VMEM((512, 128), F32),
    pltpu.VMEM((512, 128), F32),
    pltpu.SemaphoreType.DMA((4,)),
]


def attention_first(choice, valid, *arrays):
    any_spec = pl.BlockSpec(memory_space=pl.ANY)
    smem = pl.BlockSpec(memory_space=pltpu.SMEM)
    return pl.pallas_call(
        first_attention,
        name="attend0",
        out_shape=jax.ShapeDtypeStruct((128, 512), BF),
        in_specs=[smem, smem] + [any_spec] * 8,
        out_specs=pl.BlockSpec(memory_space=pltpu.VMEM),
        scratch_shapes=ATTEND_SCRATCH + [
            pltpu.VMEM((8, 128, 1024), BF),
            pltpu.VMEM((8, 1024, 512), BF),
            pltpu.VMEM((1, 8192), F32),
            pltpu.VMEM((2, 128), F32),
            pltpu.VMEM((128, 512), F32),
            pltpu.VMEM((128, 128), F32),
            pltpu.VMEM((512, 128), BF),
            pltpu.SemaphoreType.DMA((10,)),
            pltpu.SemaphoreType.DMA((8,)),
        ],
        compiler_params=pltpu.CompilerParams(vmem_limit_bytes=60 * 2**20),
        cost_estimate=pl.CostEstimate(flops=3 * 10**9, bytes_accessed=14 * 2**20, transcendentals=3 * 10**6),
    )(choice, valid, *arrays)


Y_ROWS = 80
NEAR = pl.ds(0, Y_ROWS)
REST = pl.ds(Y_ROWS, 128 - Y_ROWS)
HALF = (pl.ds(0, 512), pl.ds(512, 512))


OUT_ORDER = ((0, 0), (0, 1), (2, 0), (1, 1), (1, 0), (2, 1), (3, 0), (3, 1))


def load_out(layer, wo_ref, wo_other_ref, scratch):
    wo, wo_sem = scratch[0], scratch[8]
    y = position()[3]
    loads = {}
    for ring, side in OUT_ORDER:
        block = side * 4 + ((y + 2) % 4, (y + 1) % 4, (y + 3) % 4, y)[ring]
        at = pl.ds(pl.multiple_of(block * 1024, 1024), 1024)
        loads[ring, side] = LayerLoad(
            layer, wo_ref.at[:, at], wo_other_ref.at[:, at], wo.at[ring, side], wo_sem.at[ring * 2 + side]
        )
        loads[ring, side].start()
    return loads


def project_and_sum(att_ref, loads, scratch, greet=None):
    wo, part, from_y1, from_y2, from_z, from_c, from_c1, from_c2, _, send, recv = scratch
    x, zh, zl, y, core = position()
    to_y = (device(x, zh, zl, (y + 1) % 4, core), device(x, zh, zl, (y + 3) % 4, core))
    to_z = device(x, zh, 1 - zl, y, core)

    def remote(kind, src, dst, peer):
        return pltpu.make_async_remote_copy(
            src_ref=src, dst_ref=dst, send_sem=send.at[kind], recv_sem=recv.at[kind],
            device_id=peer, device_id_type=MESH,
        )

    far = [remote(way, part.at[0, way, NEAR], from_y1.at[way], to_y[way]) for way in range(2)]
    near = {
        (ring, side): remote(2 + ring * 2 + side - 2, part.at[ring, side, NEAR], from_y2.at[ring - 1, side], to_y[ring - 1])
        for ring in (1, 2) for side in range(2)
    }
    cross = [remote(6 + ring, part.at[ring, 1 - zl, REST], from_c.at[ring], to_z) for ring in range(4)]
    cross_far = [
        remote(10 + way, part.at[0, zl, REST, HALF[way]], from_c1.at[way], to_y[way]) for way in range(2)
    ]
    cross_near = [remote(12 + way, part.at[1 + way, zl, REST], from_c2.at[way], to_y[way]) for way in range(2)]
    last = remote(14, part.at[3, 1 - zl, NEAR], from_z, to_z)
    at_once = {(0, 0): far[0], (0, 1): far[1], (2, 0): near[2, 0], (1, 1): near[1, 1]}

    for ring, side in OUT_ORDER:
        loads[ring, side].wait()
        part[ring, side] = jnp.dot(att_ref[...], wo[ring, side], preferred_element_type=F32).astype(BF)
        if (ring, side) == (0, 0) and greet is not None:
            greet()
        if (ring, side) in at_once:
            at_once[ring, side].start()

        @pl.when(zl != side)
        def _():
            cross[ring].start()

    def add(ring, side, rows, columns, addend):
        part[ring, side, rows, columns] = (
            part[ring, side, rows, columns].astype(F32) + addend.astype(F32)
        ).astype(BF)

    every = slice(None)
    for way, key in ((0, (1, 0)), (1, (2, 1))):
        far[way].wait_recv()
        add(*key, NEAR, every, from_y1[way])
        near[key].start()
    cross[0].wait_recv()
    add(0, zl, REST, every, from_c[0])
    for way in range(2):
        cross_far[way].start()
    for ring in range(1, 4):
        cross[ring].wait_recv()
        add(ring, zl, REST, every, from_c[ring])
    for key in near:
        near[key].wait_recv()
    add(3, 1 - zl, NEAR, every, from_y2[0, 1 - zl].astype(F32) + from_y2[1, 1 - zl].astype(F32))
    last.start()
    for way in range(2):
        cross_far[way].wait_recv()
        add(1 + way, zl, REST, HALF[way], from_c1[way])
        cross_near[way].start()
    first = part[3, zl, NEAR, :].astype(F32) + from_y2[0, zl].astype(F32) + from_y2[1, zl].astype(F32)
    second = part[3, zl, REST, :].astype(F32)
    last.wait_recv()
    first = first + from_z[...].astype(F32)
    for way in range(2):
        cross_near[way].wait_recv()
        second = second + from_c2[way].astype(F32)

    def drain():
        for copy in far + list(near.values()) + cross + cross_far + cross_near + [last]:
            copy.wait_send()

    return first, second, drain


SUM_SCRATCH = [
    pltpu.VMEM((4, 2, 512, 1024), BF),
    pltpu.VMEM((4, 2, 128, 1024), BF),
    pltpu.VMEM((2, Y_ROWS, 1024), BF),
    pltpu.VMEM((2, 2, Y_ROWS, 1024), BF),
    pltpu.VMEM((Y_ROWS, 1024), BF),
    pltpu.VMEM((4, 128 - Y_ROWS, 1024), BF),
    pltpu.VMEM((2, 128 - Y_ROWS, 512), BF),
    pltpu.VMEM((2, 128 - Y_ROWS, 1024), BF),
    pltpu.SemaphoreType.DMA((8,)),
    pltpu.SemaphoreType.DMA((15,)),
    pltpu.SemaphoreType.DMA((15,)),
]


def greeting(peers):
    barrier = pltpu.get_barrier_semaphore()
    for peer in peers:
        pl.semaphore_signal(barrier, inc=1, device_id=peer, device_id_type=MESH)
    pl.semaphore_wait(barrier, len(peers))


def text_kernel(
    choice_ref, valid_ref, att_ref, pairs_ref, text_ref, wo_ref, wo_other_ref, wq_ref, wq_other_ref,
    attn_ref, attn_other_ref, small_ref, out_ref, *scratch,
):
    count = len(SUM_SCRATCH)
    sums, last_sums = scratch[:count], scratch[count:2 * count]
    (
        images, hidden, wq, attn, small, text, acc, sq, query, total, norm, att, new,
        wq_sem, ag_send, ag_recv, par_sem, core_send, core_recv,
    ) = scratch[2 * count:]
    x, zh, zl, y, core = position()
    y_up, y_dn = (y + 1) % 4, (y + 3) % 4
    to_up = device(x, zh, zl, y_up, core)
    to_dn = device(x, zh, zl, y_dn, core)
    to_z = device(x, zh, 1 - zl, y, core)
    to_core = device(x, zh, zl, y, 1 - core)
    loads = load_out(0, wo_ref, wo_other_ref, sums)
    par_copies = [
        pltpu.make_async_copy(small_ref, small, par_sem.at[0]),
        LayerLoad(1, attn_ref, attn_other_ref, attn, par_sem.at[1]),
        pltpu.make_async_copy(text_ref.at[core], text, par_sem.at[2]),
    ]
    for copy in par_copies:
        copy.start()
    images_copy = pltpu.make_async_copy(pairs_ref.at[1], images, par_sem.at[3])

    first, second, drain = project_and_sum(
        att_ref, loads, sums, lambda: greeting([to_up, to_dn, to_z, to_core])
    )
    mine, across = zl * 4, (1 - zl) * 4
    own, left, right, far = mine + y, mine + y_dn, mine + y_up, mine + (y + 2) % 4
    z_own, z_left, z_right, z_far = across + y, across + y_dn, across + y_up, across + (y + 2) % 4
    order = [own, left, right, z_own, z_left, z_right, far, z_far]
    chunks = []
    for k, block in enumerate(order):
        at = pl.ds(pl.multiple_of(block * 1024, 1024), 1024)
        chunks.append(LayerLoad(1, wq_ref.at[at], wq_other_ref.at[at], wq.at[k], wq_sem.at[k]))
        chunks[k].start()
    images_copy.start()
    last_loads = load_out(1, wo_ref, wo_other_ref, last_sums)
    for copy in par_copies:
        copy.wait()
    gate = small[0, 1:2, 0:1]

    def remote(kind, block, rows, peer, half=None):
        ref = hidden.at[block, rows] if half is None else hidden.at[block, rows, HALF[half]]
        return pltpu.make_async_remote_copy(
            src_ref=ref, dst_ref=ref, send_sem=ag_send.at[kind], recv_sem=ag_recv.at[kind],
            device_id=peer, device_id_type=MESH,
        )

    copies = [
        remote(0, own, NEAR, to_z), remote(1, own, NEAR, to_up), remote(2, own, NEAR, to_dn),
        remote(3, own, REST, to_up), remote(4, own, REST, to_dn), remote(5, own, REST, to_z),
        remote(6, left, REST, to_up, 0), remote(7, right, REST, to_dn, 1),
        remote(8, left, REST, to_z), remote(9, right, REST, to_z), remote(10, far, REST, to_z),
        remote(11, z_own, NEAR, to_up), remote(12, z_own, NEAR, to_dn),
        remote(13, left, NEAR, to_up, 0), remote(14, right, NEAR, to_dn, 1),
        remote(15, z_left, NEAR, to_up, 0), remote(16, z_right, NEAR, to_dn, 1),
    ]

    def begin(*kinds):
        for kind in kinds:
            copies[kind].start()

    def arrive(*kinds):
        for kind in kinds:
            copies[kind].wait_recv()

    def use(k):
        chunks[k].wait()
        block = order[k]
        at = pl.ds(pl.multiple_of(block * 1024, 1024), 1024)
        add_to_query(acc, sq, hidden[block], attn[:, at], wq[k])

    hidden[own, NEAR, :] = (text[NEAR, :].astype(F32) + gate * first).astype(BF)
    begin(0)
    hidden[own, REST, :] = (text[REST, :].astype(F32) + gate * second).astype(BF)
    begin(3, 4, 1, 2, 5)
    send_first = pltpu.make_async_remote_copy(
        src_ref=hidden.at[own], dst_ref=out_ref.at[1], send_sem=core_send.at[0], recv_sem=core_recv.at[0],
        device_id=to_core, device_id_type=MESH,
    )
    send_last = pltpu.make_async_remote_copy(
        src_ref=new, dst_ref=out_ref.at[0], send_sem=core_send.at[1], recv_sem=core_recv.at[1],
        device_id=to_core, device_id_type=MESH,
    )

    @pl.when(core == 1)
    def _():
        send_first.start()

    @pl.when(core == 0)
    def _():
        out_ref[0] = hidden[own]

    acc[...] = jnp.zeros_like(acc)
    sq[...] = jnp.zeros_like(sq)
    use(0)
    arrive(3)
    begin(6, 8)
    arrive(4)
    begin(7, 9)
    arrive(0)
    begin(11, 12)
    arrive(1)
    begin(13)
    arrive(2)
    begin(14)
    use(1)
    use(2)
    arrive(6, 7)
    begin(10)
    arrive(11)
    begin(15)
    arrive(12)
    begin(16)
    arrive(5)
    use(3)
    arrive(8)
    use(4)
    arrive(9)
    use(5)
    arrive(13, 14)
    use(6)
    arrive(10, 15, 16)
    use(7)
    finish_query(acc, sq, small[1, 0:1, :], query)

    total[...] = jnp.zeros_like(total)
    norm[...] = jnp.zeros_like(norm)
    one_image, two_image = choice_ref[core, 0, 0], choice_ref[core, 0, 1]
    other = jnp.where(two_image != one_image, 1.0, 0.0)
    images_copy.wait()
    add_tile(query, images, one_image, 0, total, norm)
    add_tile(query, images, one_image, 1, total, norm, (valid_ref[one_image] - 1).astype(F32))
    add_tile(query, images, two_image, 0, total, norm, other)
    add_tile(query, images, two_image, 1, total, norm, other * (valid_ref[two_image] - 1).astype(F32))
    side_by_side(total, norm, att)

    first, second, last_drain = project_and_sum(att, last_loads, last_sums)
    gate = small[1, 1:2, 0:1]
    new[NEAR, :] = (hidden[own, NEAR, :].astype(F32) + gate * first).astype(BF)
    new[REST, :] = (hidden[own, REST, :].astype(F32) + gate * second).astype(BF)

    @pl.when(core == 0)
    def _():
        send_last.start()
        send_first.wait_recv()
        send_last.wait_send()

    @pl.when(core == 1)
    def _():
        out_ref[1] = new[...]
        send_first.wait_send()
        send_last.wait_recv()

    drain()
    last_drain()
    for copy in copies:
        copy.wait_send()


def text_steps(choice, valid, att, *arrays):
    any_spec = pl.BlockSpec(memory_space=pl.ANY)
    vmem = pl.BlockSpec(memory_space=pltpu.VMEM)
    smem = pl.BlockSpec(memory_space=pltpu.SMEM)
    return pl.pallas_call(
        text_kernel,
        name="text",
        out_shape=jax.ShapeDtypeStruct((2, 128, 1024), BF),
        in_specs=[smem, smem, vmem] + [any_spec] * len(arrays),
        out_specs=vmem,
        scratch_shapes=SUM_SCRATCH * 2 + [
            pltpu.VMEM(arrays[0].shape[1:], BF),
            pltpu.VMEM((8, 128, 1024), BF),
            pltpu.VMEM((8, 1024, 512), BF),
            pltpu.VMEM((1, 8192), F32),
            pltpu.VMEM((2, 2, 128), F32),
            pltpu.VMEM((128, 1024), BF),
            pltpu.VMEM((128, 512), F32),
            pltpu.VMEM((128, 128), F32),
            pltpu.VMEM((512, 128), BF),
            pltpu.VMEM((512, 128), F32),
            pltpu.VMEM((512, 128), F32),
            pltpu.VMEM((128, 512), BF),
            pltpu.VMEM((128, 1024), BF),
            pltpu.SemaphoreType.DMA((8,)),
            pltpu.SemaphoreType.DMA((17,)),
            pltpu.SemaphoreType.DMA((17,)),
            pltpu.SemaphoreType.DMA((4,)),
            pltpu.SemaphoreType.DMA((2,)),
            pltpu.SemaphoreType.DMA((2,)),
        ],
        compiler_params=pltpu.CompilerParams(
            collective_id=1, has_side_effects=True, vmem_limit_bytes=60 * 2**20
        ),
    )(choice, valid, att, *arrays)


def local(
    text_hidden,
    image_tokens,
    attn_gain,
    w_query,
    w_keyval,
    q_gain,
    k_gain,
    w_out,
    gate,
    image_choice,
    valid_tiles,
):
    text = text_hidden[:, 0]
    weights = jnp.transpose(w_keyval[0], (1, 0, 2))
    wq, wo = w_query[0], w_out[0]
    pairs, text_all, wq_other, wo_other, attn_other, small = image_pairs(
        image_tokens[0], weights, k_gain, q_gain, gate, text, wq, wo, attn_gain
    )
    gains = (attn_gain, attn_other, small)
    att = attention_first(image_choice, valid_tiles, pairs, text, text_all, wq, wq_other, *gains)
    result = text_steps(
        image_choice, valid_tiles, att, pairs, text, wo, wo_other, wq, wq_other, *gains
    )
    return result[None, :, None]


def solution(mesh):
    placed = (
        P(None, "dp", None, "tensor"),
        P("dp", "section", "tensor"),
        P("section", None),
        P("section", None, "tensor"),
        P("section", "tensor", None, None),
        P("section", None),
        P("section", None),
        P("section", "tensor", None),
        P("section"),
        P(None, "dp", None),
        P(),
    )
    return jax.shard_map(
        local,
        mesh=mesh,
        in_specs=placed,
        out_specs=P("section", None, "dp", None, "tensor"),
        check_vma=False,
    )
```

```python
import functools

import jax
import jax.numpy as jnp
from jax import lax
from jax.experimental import pallas as pl
from jax.experimental.pallas import tpu as pltpu
from jax.sharding import PartitionSpec as P

TILE_TOK = 1600
PIECES = 20
GROUP = 2
JOINT = 1
MESH = pl.DeviceIdType.MESH
BF = jnp.bfloat16
F32 = jnp.float32


def position():
    dp = lax.axis_index("dp")
    tensor = lax.axis_index("tensor")
    return dp // 2, dp % 2, tensor // 4, tensor % 4, lax.axis_index("section")


def device(x, zh, zl, y, core):
    return (x * 2 + zh, zl * 4 + y, core)


class LayerLoad:
    def __init__(self, layer, own, other, dst, sem):
        self.here = lax.axis_index("section") == layer
        self.own = pltpu.make_async_copy(own, dst, sem)
        self.other = pltpu.make_async_copy(other, dst, sem)

    def start(self):
        pl.when(self.here)(lambda: self.own.start())
        pl.when(jnp.logical_not(self.here))(lambda: self.other.start())

    def wait(self):
        self.own.wait()


def add_to_query(acc, sq, block, gain, weights):
    values = block.astype(F32)
    sq[...] += jnp.sum(values * values, axis=-1, keepdims=True)
    acc[...] += jnp.dot((values * gain).astype(BF), weights, preferred_element_type=F32)


def finish_query(acc, sq, q_gain, query):
    inverse = lax.rsqrt(sq[:, :1] * (1.0 / 8192.0) + 1e-05)
    for head in range(4):
        one = acc[:, head * 128:(head + 1) * 128] * inverse
        one = one * lax.rsqrt(jnp.mean(one * one, axis=-1, keepdims=True) + 1e-05)
        query[head * 128:(head + 1) * 128, :] = (one * q_gain * 128.0 ** -0.5).astype(BF)


def kv_kernel(
    tok_ref, w_ref, gain_ref, q_gain_ref, gate_ref, text_ref, wq_ref, wo_ref, attn_ref,
    pairs_ref, query_ref, wq_out_ref, wo_out_ref, attn_out_ref, small_out_ref,
    hidden, wq, attn, layer_small, acc, sq, small, tok, wgt, part, from_y1, from_y2, from_z, done,
    tok_sem, w_sem, loc_sem, core_send, core_recv, text_send, text_recv, send, recv, mirror_recv, load_sem, wq_sem,
):
    x, zh, zl, y, core = position()
    dp = x * 2 + zh
    half = tok_ref.shape[0]
    out_ref = pairs_ref.at[core]
    rows = half * 2 // PIECES
    y_up, y_dn = (y + 1) % 4, (y + 3) % 4
    x_up, x_dn = (x + 1) % 4, (x + 3) % 4
    to_y = (device(x, zh, zl, y_up, core), device(x, zh, zl, y_dn, core))
    to_x = (device(x_up, zh, zl, y, core), device(x_dn, zh, zl, y, core))
    to_z_lo = device(x, zh, 1 - zl, y, core)
    to_z_hi = device(x, 1 - zh, zl, y, core)
    to_core = device(x, zh, zl, y, 1 - core)
    peers = to_y + to_x + (to_z_lo, to_z_hi, to_core)

    barrier = pltpu.get_barrier_semaphore()
    for peer in peers:
        pl.semaphore_signal(barrier, inc=1, device_id=peer, device_id_type=MESH)

    def first_row(piece):
        return pl.multiple_of(((piece + core * (PIECES // 2)) % PIECES) * rows, rows)

    def rows_of(piece):
        return pl.ds(first_row(piece), rows)

    def head_of(ring, side):
        return side * 4 + ((y + 2) % 4, y_up, y_dn, y)[ring]

    def tok_copy(piece):
        return pltpu.make_async_copy(
            tok_ref.at[pl.ds(pl.multiple_of(piece * rows, rows), rows)],
            tok.at[pl.ds(pl.multiple_of(core * half + piece * rows, rows), rows)],
            tok_sem.at[piece],
        )

    def w_copy(ring, side):
        return pltpu.make_async_copy(
            w_ref.at[head_of(ring, side)], wgt.at[ring, side], w_sem.at[ring * 2 + side]
        )

    def to_other_core(kind):
        src, dst = (
            (tok_ref, tok.at[pl.ds(pl.multiple_of(core * half, half), half)]),
            (attn_ref, attn_out_ref),
            (small, small_out_ref.at[core]),
            (wq_ref, wq_out_ref),
            (wo_ref, wo_out_ref),
        )[kind]
        return pltpu.make_async_remote_copy(
            src_ref=src, dst_ref=dst, send_sem=core_send.at[kind], recv_sem=core_recv.at[kind],
            device_id=to_core, device_id_type=MESH,
        )

    def text_copy(kind):
        own = zl * 4
        other = (1 - zl) * 4
        block = (
            own + y, own + y, own + y, other + y, other + y, own + y_dn, own + y_up, other + y_dn, other + y_up
        )[kind]
        dst = hidden.at[block]
        src = text_ref.at[core] if kind < 3 else dst
        if kind >= 5:
            at = pl.ds(((kind - 5) % 2) * 64, 64)
            src, dst = src.at[at], dst.at[at]
        peer = to_z_lo if kind == 2 else to_y[(0, 1, 2, 0, 1, 0, 1, 0, 1)[kind]]
        return pltpu.make_async_remote_copy(
            src_ref=src, dst_ref=dst, send_sem=text_send.at[kind], recv_sem=text_recv.at[kind],
            device_id=peer, device_id_type=MESH,
        )

    def remote(kind, piece, src, dst, peer):
        return pltpu.make_async_remote_copy(
            src_ref=src, dst_ref=dst,
            send_sem=send.at[kind], recv_sem=recv.at[kind, piece],
            device_id=peer, device_id_type=MESH,
        )

    def y1_copy(way, piece):
        at = rows_of(piece)
        return remote(way, piece, part.at[0, way, at], from_y1.at[way, at], to_y[way])

    def y2_copy(way, piece):
        at = rows_of(piece)
        return remote(2 + way, piece, part.at[1 + way, :, at], from_y2.at[way, :, at], to_y[way])

    def z_copy(piece):
        at = rows_of(piece)
        return remote(4, piece, part.at[3, 1 - zl, at], from_z.at[at], to_z_lo)

    def own_copy(way, piece):
        at = rows_of(piece)
        return remote(5 + way, piece, done.at[at], out_ref.at[dp, at], to_z_hi if way == 0 else to_x[way - 1])

    def own_local(piece):
        at = rows_of(piece)
        return pltpu.make_async_copy(done.at[at], out_ref.at[dp, at], loc_sem.at[0])

    def pair_copy(way, piece):
        ref = out_ref.at[x * 2 + 1 - zh, rows_of(piece)]
        return remote(8 + way, piece, ref, ref, to_x[way])

    def forward_copy(way, piece):
        image = (x_dn * 2 + zh, x_up * 2 + 1 - zh)[way]
        ref = out_ref.at[image, rows_of(piece)]
        return remote(10 + way, piece, ref, ref, to_x[way])

    def mirror_copy(kind, at):
        across = (x + 2) % 4
        place = (
            (x, zh), (x, 1 - zh), (x_dn, zh), (x_up, zh), (x_dn, 1 - zh), (x_up, 1 - zh), (across, zh), (across, 1 - zh)
        )[kind]
        ref = out_ref.at[place[0] * 2 + place[1], at]
        return pltpu.make_async_remote_copy(
            src_ref=done.at[at] if kind == 0 else ref, dst_ref=ref,
            send_sem=send.at[12 + kind], recv_sem=mirror_recv.at[kind],
            device_id=to_core, device_id_type=MESH,
        )

    def mirror(kinds, piece):
        @pl.when(piece % GROUP == GROUP - 1)
        def _():
            at = pl.ds(first_row(piece - (GROUP - 1)), rows * GROUP)
            for kind in kinds:
                mirror_copy(kind, at).start()

    for ring in range(4):
        for side in range(2):
            w_copy(ring, side).start()

    def start_tok(piece, carry):
        tok_copy(piece).start()
        return carry

    lax.fori_loop(0, PIECES // 2, start_tok, 0)
    small[0:1, :] = q_gain_ref[...]
    small[1:2, :] = jnp.tanh(jnp.broadcast_to(gate_ref[0], (1, 128)))
    small_own = pltpu.make_async_copy(small, small_out_ref.at[core], loc_sem.at[1])
    small_own.start()
    text_own = pltpu.make_async_copy(text_ref.at[core], hidden.at[zl * 4 + y], load_sem.at[0])
    text_own.start()
    acc[...] = jnp.zeros_like(acc)
    sq[...] = jnp.zeros_like(sq)
    pl.semaphore_wait(barrier, len(peers))
    to_other_core(0).start()
    text_copy(2).start()
    for kind in range(1, 5):
        to_other_core(kind).start()

    own, other = zl * 4, (1 - zl) * 4
    blocks = [own + y, other + y, own + y_dn, own + y_up, other + y_dn, other + y_up]
    blocks += [own + (y + 2) % 4, other + (y + 2) % 4]
    columns = [pl.ds(pl.multiple_of(block * 1024, 1024), 1024) for block in blocks]

    def query_loads():
        return [
            LayerLoad(0, attn_ref, attn_out_ref, attn, load_sem.at[1]),
            pltpu.make_async_copy(small_out_ref.at[0], layer_small, load_sem.at[2]),
        ]

    def wq_load(k):
        return LayerLoad(0, wq_ref.at[columns[k]], wq_out_ref.at[columns[k]], wq.at[k], wq_sem.at[k])

    def use(*which):
        for k in which:
            wq_load(k).wait()
            add_to_query(acc, sq, hidden[blocks[k]], attn[:, columns[k]], wq[k])

    def add(ring, side, at, addend):
        part[ring, side, at, :] = (part[ring, side, at, :].astype(F32) + addend.astype(F32)).astype(BF)

    def step_fn(it, carry):
        @pl.when((it < PIECES) & (it % JOINT == 0))
        def _():
            piece = it

            @pl.when(piece < PIECES // 2)
            def _():
                for more in range(JOINT):
                    tok_copy(piece + more).wait()

            @pl.when(piece == PIECES // 2)
            def _():
                to_other_core(0).wait_recv()

            at = pl.ds(first_row(piece), rows * JOINT)
            for ring in range(4):
                for side in range(2):
                    @pl.when(it == 0)
                    def _():
                        w_copy(ring, side).wait()

                    part[ring, side, at, :] = jnp.dot(
                        tok[at, :], wgt[ring, side], preferred_element_type=F32
                    ).astype(BF)
                    if ring == 0:
                        for more in range(JOINT):
                            y1_copy(side, piece + more).start()

        @pl.when((it >= 1) & (it < PIECES + 1))
        def _():
            piece = it - 1
            at = rows_of(piece)
            for way in range(2):
                y1_copy(way, piece).wait_recv()
                add(1 + way, way, at, from_y1[way, at, :])
                y2_copy(way, piece).start()

            @pl.when(piece == PIECES - 1)
            def _():
                text_copy(2).wait_recv()
                for kind in (0, 1, 3, 4):
                    text_copy(kind).start()

        @pl.when((it >= 2) & (it < PIECES + 2))
        def _():
            piece = it - 2
            at = rows_of(piece)
            for way in range(2):
                y2_copy(way, piece).wait_recv()
            add(
                3, 1 - zl, at,
                from_y2[0, 1 - zl, at, :].astype(F32) + from_y2[1, 1 - zl, at, :].astype(F32),
            )
            z_copy(piece).start()

            @pl.when(piece == PIECES - 1)
            def _():
                small_own.wait()
                for kind in range(1, 4):
                    to_other_core(kind).wait_recv()
                for copy in query_loads():
                    copy.start()
                for k in range(8):
                    wq_load(k).start()

        @pl.when((it >= 3) & (it < PIECES + 3))
        def _():
            piece = it - 3
            at = rows_of(piece)
            z_copy(piece).wait_recv()
            total = (
                part[3, zl, at, :].astype(F32)
                + from_y2[0, zl, at, :].astype(F32) + from_y2[1, zl, at, :].astype(F32)
                + from_z[at, :].astype(F32)
            )
            keys = total[:, :128]
            keys = keys * lax.rsqrt(jnp.mean(keys * keys, axis=-1, keepdims=True) + 1e-05)
            done[at, 0:128] = (keys * gain_ref[...]).astype(BF)
            done[at, 128:256] = total[:, 128:].astype(BF)
            for way in range(3):
                own_copy(way, piece).start()
            own_local(piece).start()
            mirror((0,), piece)

        @pl.when((it >= 4) & (it < PIECES + 4))
        def _():
            piece = it - 4
            own_copy(0, piece).wait_recv()
            for way in range(2):
                pair_copy(way, piece).start()

            @pl.when(piece == PIECES - 1)
            def _():
                for kind in (0, 1):
                    text_copy(kind).wait_recv()
                    text_copy(kind + 5).start()
                text_own.wait()
                for copy in query_loads():
                    copy.wait()
                use(0, 1)
            mirror((1,), piece)

        @pl.when((it >= 5) & (it < PIECES + 5))
        def _():
            piece = it - 5
            own_copy(1, piece).wait_recv()
            pair_copy(1, piece).wait_recv()
            for way in range(2):
                forward_copy(way, piece).start()
            own_copy(2, piece).wait_recv()
            pair_copy(0, piece).wait_recv()
            mirror((2, 3, 4, 5), piece)

            @pl.when(piece == PIECES - 1)
            def _():
                for kind in (3, 4):
                    text_copy(kind).wait_recv()
                    text_copy(kind + 4).start()
                use(2, 3)

        @pl.when(it >= 6)
        def _():
            piece = it - 6
            for way in range(2):
                forward_copy(way, piece).wait_recv()
            mirror((6, 7), piece)

            @pl.when(piece == PIECES - 1)
            def _():
                use(4, 5)

        return carry

    lax.fori_loop(0, PIECES + 6, step_fn, 0)

    for kind in (5, 6):
        text_copy(kind).wait_recv()
    use(6)
    for kind in (7, 8):
        text_copy(kind).wait_recv()
    use(7)
    finish_query(acc, sq, layer_small[0:1, :], query_ref)

    whole = pl.ds(0, half * 2)

    def sent(kind, ref):
        pltpu.make_async_remote_copy(
            src_ref=ref, dst_ref=ref, send_sem=send.at[kind], recv_sem=recv.at[kind, 0],
            device_id=to_core, device_id_type=MESH,
        ).wait_send()

    for way in range(2):
        sent(way, part.at[0, way])
        sent(2 + way, part.at[1 + way])
    for kind in range(4, 12):
        sent(kind, done)
    for kind in range(8):
        mirror_copy(kind, whole).wait()
    pltpu.make_async_copy(done, out_ref.at[dp], loc_sem.at[0]).wait()
    for kind in range(4):
        to_other_core(kind).wait_send()
    to_other_core(4).wait()
    for kind in range(9):
        text_copy(kind).wait_send()


def image_pairs(tokens, weights, gain, q_gain, gate, text, w_query, w_out, attn_gain):
    half, width = tokens.shape
    heads = weights.shape[0]
    patches = half * 2
    any_spec = pl.BlockSpec(memory_space=pl.ANY)

    def like(array):
        return jax.ShapeDtypeStruct(array.shape, array.dtype)

    return pl.pallas_call(
        kv_kernel,
        name="kv",
        out_shape=[
            jax.ShapeDtypeStruct((2, 8, patches, 256), BF),
            jax.ShapeDtypeStruct((512, 128), BF),
            like(w_query),
            like(w_out),
            like(attn_gain),
            jax.ShapeDtypeStruct((2, 2, 128), F32),
        ],
        in_specs=[any_spec] * 2
        + [pl.BlockSpec(memory_space=pltpu.VMEM)] * 2
        + [pl.BlockSpec(memory_space=pltpu.SMEM)]
        + [any_spec] * 4,
        out_specs=[any_spec, pl.BlockSpec(memory_space=pltpu.VMEM)] + [any_spec] * 4,
        scratch_shapes=[
            pltpu.VMEM((8, 128, 1024), BF),
            pltpu.VMEM((8, 1024, 512), BF),
            pltpu.VMEM((1, 8192), F32),
            pltpu.VMEM((2, 128), F32),
            pltpu.VMEM((128, 512), F32),
            pltpu.VMEM((128, 128), F32),
            pltpu.VMEM((2, 128), F32),
            pltpu.VMEM((patches, width), BF),
            pltpu.VMEM((4, 2, width, 256), BF),
            pltpu.VMEM((4, 2, patches, 256), BF),
            pltpu.VMEM((2, patches, 256), BF),
            pltpu.VMEM((2, 2, patches, 256), BF),
            pltpu.VMEM((patches, 256), BF),
            pltpu.VMEM((patches, 256), BF),
            pltpu.SemaphoreType.DMA((PIECES // 2,)),
            pltpu.SemaphoreType.DMA((8,)),
            pltpu.SemaphoreType.DMA((2,)),
            pltpu.SemaphoreType.DMA((5,)),
            pltpu.SemaphoreType.DMA((5,)),
            pltpu.SemaphoreType.DMA((9,)),
            pltpu.SemaphoreType.DMA((9,)),
            pltpu.SemaphoreType.DMA((20,)),
            pltpu.SemaphoreType.DMA((12, PIECES)),
            pltpu.SemaphoreType.DMA((8,)),
            pltpu.SemaphoreType.DMA((3,)),
            pltpu.SemaphoreType.DMA((8,)),
        ],
        compiler_params=pltpu.CompilerParams(
            collective_id=0, has_side_effects=True, vmem_limit_bytes=60 * 2**20
        ),
        cost_estimate=pl.CostEstimate(
            flops=2 * patches * width * heads * 256, bytes_accessed=40 * 2**20, transcendentals=0
        ),
    )(tokens, weights, gain, q_gain, gate, text, w_query, w_out, attn_gain)


KEY_PARTS = ((0, 512), (512, 512), (1024, 576))


def add_tile(query, tiles, image, tile, total, norm, weight=None):
    for start, size in KEY_PARTS:
        at = slice(tile * TILE_TOK + start, tile * TILE_TOK + start + size)
        scores = lax.dot_general(
            query[...], tiles[image, at, 0:128], (((1,), (1,)), ((), ())), preferred_element_type=F32
        )
        expo = jnp.exp(scores)
        sums = jnp.sum(expo, axis=-1, keepdims=True)
        values = jnp.dot(expo.astype(BF), tiles[image, at, 128:256], preferred_element_type=F32)
        norm[...] += sums if weight is None else sums * weight
        total[...] += values if weight is None else values * weight


def side_by_side(total, norm, att_ref):
    for head in range(4):
        at = slice(head * 128, (head + 1) * 128)
        att_ref[:, at] = (total[at, :] / norm[at, :1]).astype(BF)


def attend(layer, choice_ref, valid_ref, query, pairs_ref, att_ref, tiles, total, norm, sem):
    core = lax.axis_index("section")
    first = choice_ref[core, 0, 0]
    second = choice_ref[core, 0, 1]
    other = second != first
    plan = (
        (first, 0, None),
        (first, 1, valid_ref[first] > 1),
        (second, 0, other),
        (second, 1, other & (valid_ref[second] > 1)),
    )

    def copy(slot):
        image, tile, _ = plan[slot]
        return pltpu.make_async_copy(
            pairs_ref.at[layer, image, pl.ds(tile * TILE_TOK, TILE_TOK)], tiles.at[slot], sem.at[slot]
        )

    def run(slot, fn):
        allowed = plan[slot][2]
        if allowed is None:
            fn()
        else:
            pl.when(allowed)(fn)

    for slot in range(4):
        run(slot, lambda slot=slot: copy(slot).start())
    total[...] = jnp.zeros_like(total)
    norm[...] = jnp.zeros_like(norm)

    def one(slot):
        copy(slot).wait()
        add_tile(query, tiles, slot, 0, total, norm)

    for slot in range(4):
        run(slot, functools.partial(one, slot))
    side_by_side(total, norm, att_ref)


def first_attention(choice_ref, valid_ref, pairs_ref, query_ref, att_ref, tiles, total, norm, sem):
    attend(0, choice_ref, valid_ref, query_ref, pairs_ref, att_ref, tiles, total, norm, sem)


ATTEND_SCRATCH = [
    pltpu.VMEM((4, TILE_TOK, 256), BF),
    pltpu.VMEM((512, 128), F32),
    pltpu.VMEM((512, 128), F32),
    pltpu.SemaphoreType.DMA((4,)),
]


def attention_first(choice, valid, pairs, query):
    any_spec = pl.BlockSpec(memory_space=pl.ANY)
    smem = pl.BlockSpec(memory_space=pltpu.SMEM)
    vmem = pl.BlockSpec(memory_space=pltpu.VMEM)
    return pl.pallas_call(
        first_attention,
        name="attend",
        out_shape=jax.ShapeDtypeStruct((128, 512), BF),
        in_specs=[smem, smem, any_spec, vmem],
        out_specs=vmem,
        scratch_shapes=ATTEND_SCRATCH,
        compiler_params=pltpu.CompilerParams(vmem_limit_bytes=60 * 2**20),
        cost_estimate=pl.CostEstimate(flops=2 * 10**9, bytes_accessed=4 * 2**20, transcendentals=3 * 10**6),
    )(choice, valid, pairs, query)


Y_ROWS = 80
NEAR = pl.ds(0, Y_ROWS)
REST = pl.ds(Y_ROWS, 128 - Y_ROWS)
HALF = (pl.ds(0, 512), pl.ds(512, 512))


OUT_ORDER = ((0, 0), (0, 1), (2, 0), (1, 1), (1, 0), (2, 1), (3, 0), (3, 1))


def load_out(layer, wo_ref, wo_other_ref, scratch):
    wo, wo_sem = scratch[0], scratch[8]
    y = position()[3]
    loads = {}
    for ring, side in OUT_ORDER:
        block = side * 4 + ((y + 2) % 4, (y + 1) % 4, (y + 3) % 4, y)[ring]
        at = pl.ds(pl.multiple_of(block * 1024, 1024), 1024)
        loads[ring, side] = LayerLoad(
            layer, wo_ref.at[:, at], wo_other_ref.at[:, at], wo.at[ring, side], wo_sem.at[ring * 2 + side]
        )
        loads[ring, side].start()
    return loads


def project_and_sum(att_ref, loads, scratch, greet=None):
    wo, part, from_y1, from_y2, from_z, from_c, from_c1, from_c2, _, send, recv = scratch
    x, zh, zl, y, core = position()
    to_y = (device(x, zh, zl, (y + 1) % 4, core), device(x, zh, zl, (y + 3) % 4, core))
    to_z = device(x, zh, 1 - zl, y, core)

    def remote(kind, src, dst, peer):
        return pltpu.make_async_remote_copy(
            src_ref=src, dst_ref=dst, send_sem=send.at[kind], recv_sem=recv.at[kind],
            device_id=peer, device_id_type=MESH,
        )

    far = [remote(way, part.at[0, way, NEAR], from_y1.at[way], to_y[way]) for way in range(2)]
    near = {
        (ring, side): remote(2 + ring * 2 + side - 2, part.at[ring, side, NEAR], from_y2.at[ring - 1, side], to_y[ring - 1])
        for ring in (1, 2) for side in range(2)
    }
    cross = [remote(6 + ring, part.at[ring, 1 - zl, REST], from_c.at[ring], to_z) for ring in range(4)]
    cross_far = [
        remote(10 + way, part.at[0, zl, REST, HALF[way]], from_c1.at[way], to_y[way]) for way in range(2)
    ]
    cross_near = [remote(12 + way, part.at[1 + way, zl, REST], from_c2.at[way], to_y[way]) for way in range(2)]
    last = remote(14, part.at[3, 1 - zl, NEAR], from_z, to_z)
    at_once = {(0, 0): far[0], (0, 1): far[1], (2, 0): near[2, 0], (1, 1): near[1, 1]}

    for ring, side in OUT_ORDER:
        loads[ring, side].wait()
        part[ring, side] = jnp.dot(att_ref[...], wo[ring, side], preferred_element_type=F32).astype(BF)
        if (ring, side) == (0, 0) and greet is not None:
            greet()
        if (ring, side) in at_once:
            at_once[ring, side].start()

        @pl.when(zl != side)
        def _():
            cross[ring].start()

    def add(ring, side, rows, columns, addend):
        part[ring, side, rows, columns] = (
            part[ring, side, rows, columns].astype(F32) + addend.astype(F32)
        ).astype(BF)

    every = slice(None)
    for way, key in ((0, (1, 0)), (1, (2, 1))):
        far[way].wait_recv()
        add(*key, NEAR, every, from_y1[way])
        near[key].start()
    cross[0].wait_recv()
    add(0, zl, REST, every, from_c[0])
    for way in range(2):
        cross_far[way].start()
    for ring in range(1, 4):
        cross[ring].wait_recv()
        add(ring, zl, REST, every, from_c[ring])
    for key in near:
        near[key].wait_recv()
    add(3, 1 - zl, NEAR, every, from_y2[0, 1 - zl].astype(F32) + from_y2[1, 1 - zl].astype(F32))
    last.start()
    for way in range(2):
        cross_far[way].wait_recv()
        add(1 + way, zl, REST, HALF[way], from_c1[way])
        cross_near[way].start()
    first = part[3, zl, NEAR, :].astype(F32) + from_y2[0, zl].astype(F32) + from_y2[1, zl].astype(F32)
    second = part[3, zl, REST, :].astype(F32)
    last.wait_recv()
    first = first + from_z[...].astype(F32)
    for way in range(2):
        cross_near[way].wait_recv()
        second = second + from_c2[way].astype(F32)

    def drain():
        for copy in far + list(near.values()) + cross + cross_far + cross_near + [last]:
            copy.wait_send()

    return first, second, drain


SUM_SCRATCH = [
    pltpu.VMEM((4, 2, 512, 1024), BF),
    pltpu.VMEM((4, 2, 128, 1024), BF),
    pltpu.VMEM((2, Y_ROWS, 1024), BF),
    pltpu.VMEM((2, 2, Y_ROWS, 1024), BF),
    pltpu.VMEM((Y_ROWS, 1024), BF),
    pltpu.VMEM((4, 128 - Y_ROWS, 1024), BF),
    pltpu.VMEM((2, 128 - Y_ROWS, 512), BF),
    pltpu.VMEM((2, 128 - Y_ROWS, 1024), BF),
    pltpu.SemaphoreType.DMA((8,)),
    pltpu.SemaphoreType.DMA((15,)),
    pltpu.SemaphoreType.DMA((15,)),
]


def greeting(peers):
    barrier = pltpu.get_barrier_semaphore()
    for peer in peers:
        pl.semaphore_signal(barrier, inc=1, device_id=peer, device_id_type=MESH)
    pl.semaphore_wait(barrier, len(peers))


def text_kernel(
    choice_ref, valid_ref, att_ref, pairs_ref, text_ref, wo_ref, wo_other_ref, wq_ref, wq_other_ref,
    attn_ref, attn_other_ref, small_ref, out_ref, *scratch,
):
    count = len(SUM_SCRATCH)
    sums, last_sums = scratch[:count], scratch[count:2 * count]
    (
        images, hidden, wq, attn, small, text, acc, sq, query, total, norm, att, new,
        wq_sem, ag_send, ag_recv, par_sem, core_send, core_recv,
    ) = scratch[2 * count:]
    x, zh, zl, y, core = position()
    y_up, y_dn = (y + 1) % 4, (y + 3) % 4
    to_up = device(x, zh, zl, y_up, core)
    to_dn = device(x, zh, zl, y_dn, core)
    to_z = device(x, zh, 1 - zl, y, core)
    to_core = device(x, zh, zl, y, 1 - core)
    loads = load_out(0, wo_ref, wo_other_ref, sums)
    par_copies = [
        pltpu.make_async_copy(small_ref, small, par_sem.at[0]),
        LayerLoad(1, attn_ref, attn_other_ref, attn, par_sem.at[1]),
        pltpu.make_async_copy(text_ref.at[core], text, par_sem.at[2]),
    ]
    for copy in par_copies:
        copy.start()
    images_copy = pltpu.make_async_copy(pairs_ref.at[1], images, par_sem.at[3])

    first, second, drain = project_and_sum(
        att_ref, loads, sums, lambda: greeting([to_up, to_dn, to_z, to_core])
    )
    mine, across = zl * 4, (1 - zl) * 4
    own, left, right, far = mine + y, mine + y_dn, mine + y_up, mine + (y + 2) % 4
    z_own, z_left, z_right, z_far = across + y, across + y_dn, across + y_up, across + (y + 2) % 4
    order = [own, left, right, z_own, z_left, z_right, far, z_far]
    chunks = []
    for k, block in enumerate(order):
        at = pl.ds(pl.multiple_of(block * 1024, 1024), 1024)
        chunks.append(LayerLoad(1, wq_ref.at[at], wq_other_ref.at[at], wq.at[k], wq_sem.at[k]))
        chunks[k].start()
    images_copy.start()
    last_loads = load_out(1, wo_ref, wo_other_ref, last_sums)
    for copy in par_copies:
        copy.wait()
    gate = small[0, 1:2, 0:1]

    def remote(kind, block, rows, peer, half=None):
        ref = hidden.at[block, rows] if half is None else hidden.at[block, rows, HALF[half]]
        return pltpu.make_async_remote_copy(
            src_ref=ref, dst_ref=ref, send_sem=ag_send.at[kind], recv_sem=ag_recv.at[kind],
            device_id=peer, device_id_type=MESH,
        )

    copies = [
        remote(0, own, NEAR, to_z), remote(1, own, NEAR, to_up), remote(2, own, NEAR, to_dn),
        remote(3, own, REST, to_up), remote(4, own, REST, to_dn), remote(5, own, REST, to_z),
        remote(6, left, REST, to_up, 0), remote(7, right, REST, to_dn, 1),
        remote(8, left, REST, to_z), remote(9, right, REST, to_z), remote(10, far, REST, to_z),
        remote(11, z_own, NEAR, to_up), remote(12, z_own, NEAR, to_dn),
        remote(13, left, NEAR, to_up, 0), remote(14, right, NEAR, to_dn, 1),
        remote(15, z_left, NEAR, to_up, 0), remote(16, z_right, NEAR, to_dn, 1),
    ]

    def begin(*kinds):
        for kind in kinds:
            copies[kind].start()

    def arrive(*kinds):
        for kind in kinds:
            copies[kind].wait_recv()

    def use(k):
        chunks[k].wait()
        block = order[k]
        at = pl.ds(pl.multiple_of(block * 1024, 1024), 1024)
        add_to_query(acc, sq, hidden[block], attn[:, at], wq[k])

    hidden[own, NEAR, :] = (text[NEAR, :].astype(F32) + gate * first).astype(BF)
    begin(0)
    hidden[own, REST, :] = (text[REST, :].astype(F32) + gate * second).astype(BF)
    begin(3, 4, 1, 2, 5)
    send_first = pltpu.make_async_remote_copy(
        src_ref=hidden.at[own], dst_ref=out_ref.at[1], send_sem=core_send.at[0], recv_sem=core_recv.at[0],
        device_id=to_core, device_id_type=MESH,
    )
    send_last = pltpu.make_async_remote_copy(
        src_ref=new, dst_ref=out_ref.at[0], send_sem=core_send.at[1], recv_sem=core_recv.at[1],
        device_id=to_core, device_id_type=MESH,
    )

    @pl.when(core == 1)
    def _():
        send_first.start()

    @pl.when(core == 0)
    def _():
        out_ref[0] = hidden[own]

    acc[...] = jnp.zeros_like(acc)
    sq[...] = jnp.zeros_like(sq)
    use(0)
    arrive(3)
    begin(6, 8)
    arrive(4)
    begin(7, 9)
    arrive(0)
    begin(11, 12)
    arrive(1)
    begin(13)
    arrive(2)
    begin(14)
    use(1)
    use(2)
    arrive(6, 7)
    begin(10)
    arrive(11)
    begin(15)
    arrive(12)
    begin(16)
    arrive(5)
    use(3)
    arrive(8)
    use(4)
    arrive(9)
    use(5)
    arrive(13, 14)
    use(6)
    arrive(10, 15, 16)
    use(7)
    finish_query(acc, sq, small[1, 0:1, :], query)

    total[...] = jnp.zeros_like(total)
    norm[...] = jnp.zeros_like(norm)
    one_image, two_image = choice_ref[core, 0, 0], choice_ref[core, 0, 1]
    other = jnp.where(two_image != one_image, 1.0, 0.0)
    images_copy.wait()
    add_tile(query, images, one_image, 0, total, norm)
    add_tile(query, images, one_image, 1, total, norm, (valid_ref[one_image] - 1).astype(F32))
    add_tile(query, images, two_image, 0, total, norm, other)
    add_tile(query, images, two_image, 1, total, norm, other * (valid_ref[two_image] - 1).astype(F32))
    side_by_side(total, norm, att)

    first, second, last_drain = project_and_sum(att, last_loads, last_sums)
    gate = small[1, 1:2, 0:1]
    new[NEAR, :] = (hidden[own, NEAR, :].astype(F32) + gate * first).astype(BF)
    new[REST, :] = (hidden[own, REST, :].astype(F32) + gate * second).astype(BF)

    @pl.when(core == 0)
    def _():
        send_last.start()
        send_first.wait_recv()
        send_last.wait_send()

    @pl.when(core == 1)
    def _():
        out_ref[1] = new[...]
        send_first.wait_send()
        send_last.wait_recv()

    drain()
    last_drain()
    for copy in copies:
        copy.wait_send()


def text_steps(choice, valid, att, *arrays):
    any_spec = pl.BlockSpec(memory_space=pl.ANY)
    vmem = pl.BlockSpec(memory_space=pltpu.VMEM)
    smem = pl.BlockSpec(memory_space=pltpu.SMEM)
    return pl.pallas_call(
        text_kernel,
        name="text",
        out_shape=jax.ShapeDtypeStruct((2, 128, 1024), BF),
        in_specs=[smem, smem, vmem] + [any_spec] * len(arrays),
        out_specs=vmem,
        scratch_shapes=SUM_SCRATCH * 2 + [
            pltpu.VMEM(arrays[0].shape[1:], BF),
            pltpu.VMEM((8, 128, 1024), BF),
            pltpu.VMEM((8, 1024, 512), BF),
            pltpu.VMEM((1, 8192), F32),
            pltpu.VMEM((2, 2, 128), F32),
            pltpu.VMEM((128, 1024), BF),
            pltpu.VMEM((128, 512), F32),
            pltpu.VMEM((128, 128), F32),
            pltpu.VMEM((512, 128), BF),
            pltpu.VMEM((512, 128), F32),
            pltpu.VMEM((512, 128), F32),
            pltpu.VMEM((128, 512), BF),
            pltpu.VMEM((128, 1024), BF),
            pltpu.SemaphoreType.DMA((8,)),
            pltpu.SemaphoreType.DMA((17,)),
            pltpu.SemaphoreType.DMA((17,)),
            pltpu.SemaphoreType.DMA((4,)),
            pltpu.SemaphoreType.DMA((2,)),
            pltpu.SemaphoreType.DMA((2,)),
        ],
        compiler_params=pltpu.CompilerParams(
            collective_id=1, has_side_effects=True, vmem_limit_bytes=60 * 2**20
        ),
    )(choice, valid, att, *arrays)


def local(
    text_hidden,
    image_tokens,
    attn_gain,
    w_query,
    w_keyval,
    q_gain,
    k_gain,
    w_out,
    gate,
    image_choice,
    valid_tiles,
):
    text = text_hidden[:, 0]
    weights = jnp.transpose(w_keyval[0], (1, 0, 2))
    wq, wo = w_query[0], w_out[0]
    pairs, query, wq_other, wo_other, attn_other, small = image_pairs(
        image_tokens[0], weights, k_gain, q_gain, gate, text, wq, wo, attn_gain
    )
    gains = (attn_gain, attn_other, small)
    att = attention_first(image_choice, valid_tiles, pairs, query)
    result = text_steps(
        image_choice, valid_tiles, att, pairs, text, wo, wo_other, wq, wq_other, *gains
    )
    return result[None, :, None]


def solution(mesh):
    placed = (
        P(None, "dp", None, "tensor"),
        P("dp", "section", "tensor"),
        P("section", None),
        P("section", None, "tensor"),
        P("section", "tensor", None, None),
        P("section", None),
        P("section", None),
        P("section", "tensor", None),
        P("section"),
        P(None, "dp", None),
        P(),
    )
    return jax.shard_map(
        local,
        mesh=mesh,
        in_specs=placed,
        out_specs=P("section", None, "dp", None, "tensor"),
        check_vma=False,
    )
```

```python
import functools

import jax
import jax.numpy as jnp
from jax import lax
from jax.experimental import pallas as pl
from jax.experimental.pallas import tpu as pltpu
from jax.sharding import PartitionSpec as P

TILE_TOK = 1600
PIECES = 20
GROUP = 2
JOINT = 1
MESH = pl.DeviceIdType.MESH
BF = jnp.bfloat16
F32 = jnp.float32


def position():
    dp = lax.axis_index("dp")
    tensor = lax.axis_index("tensor")
    return dp // 2, dp % 2, tensor // 4, tensor % 4, lax.axis_index("section")


def device(x, zh, zl, y, core):
    return (x * 2 + zh, zl * 4 + y, core)


class LayerLoad:
    def __init__(self, layer, own, other, dst, sem):
        self.here = lax.axis_index("section") == layer
        self.own = pltpu.make_async_copy(own, dst, sem)
        self.other = pltpu.make_async_copy(other, dst, sem)

    def start(self):
        pl.when(self.here)(lambda: self.own.start())
        pl.when(jnp.logical_not(self.here))(lambda: self.other.start())

    def wait(self):
        self.own.wait()


def add_to_query(acc, sq, block, gain, weights):
    values = block.astype(F32)
    sq[...] += jnp.sum(values * values, axis=-1, keepdims=True)
    acc[...] += jnp.dot((values * gain).astype(BF), weights, preferred_element_type=F32)


def finish_query(acc, sq, q_gain, query):
    inverse = lax.rsqrt(sq[:, :1] * (1.0 / 8192.0) + 1e-05)
    for head in range(4):
        one = acc[:, head * 128:(head + 1) * 128] * inverse
        one = one * lax.rsqrt(jnp.mean(one * one, axis=-1, keepdims=True) + 1e-05)
        query[head * 128:(head + 1) * 128, :] = (one * q_gain * 128.0 ** -0.5).astype(BF)


def kv_kernel(
    tok_ref, w_ref, gain_ref, q_gain_ref, gate_ref, text_ref, wq_ref, wo_ref, attn_ref,
    pairs_ref, query_ref, wq_out_ref, wo_out_ref, attn_out_ref, small_out_ref,
    hidden, wq, attn, layer_small, acc, sq, small, tok, wgt, part, from_y1, from_y2, from_z, done,
    tok_sem, w_sem, loc_sem, core_send, core_recv, text_send, text_recv, send, recv, mirror_recv, load_sem, wq_sem,
):
    x, zh, zl, y, core = position()
    dp = x * 2 + zh
    half = tok_ref.shape[0]
    out_ref = pairs_ref.at[core]
    rows = half * 2 // PIECES
    y_up, y_dn = (y + 1) % 4, (y + 3) % 4
    x_up, x_dn = (x + 1) % 4, (x + 3) % 4
    to_y = (device(x, zh, zl, y_up, core), device(x, zh, zl, y_dn, core))
    to_x = (device(x_up, zh, zl, y, core), device(x_dn, zh, zl, y, core))
    to_z_lo = device(x, zh, 1 - zl, y, core)
    to_z_hi = device(x, 1 - zh, zl, y, core)
    to_core = device(x, zh, zl, y, 1 - core)
    peers = to_y + to_x + (to_z_lo, to_z_hi, to_core)

    barrier = pltpu.get_barrier_semaphore()
    for peer in peers:
        pl.semaphore_signal(barrier, inc=1, device_id=peer, device_id_type=MESH)

    def first_row(piece):
        return pl.multiple_of(((piece + core * (PIECES // 2)) % PIECES) * rows, rows)

    def rows_of(piece):
        return pl.ds(first_row(piece), rows)

    def head_of(ring, side):
        return side * 4 + ((y + 2) % 4, y_up, y_dn, y)[ring]

    def tok_copy(piece):
        return pltpu.make_async_copy(
            tok_ref.at[pl.ds(pl.multiple_of(piece * rows, rows), rows)],
            tok.at[pl.ds(pl.multiple_of(core * half + piece * rows, rows), rows)],
            tok_sem.at[piece],
        )

    def w_copy(ring, side):
        return pltpu.make_async_copy(
            w_ref.at[head_of(ring, side)], wgt.at[ring, side], w_sem.at[ring * 2 + side]
        )

    def to_other_core(kind):
        src, dst = (
            (tok_ref, tok.at[pl.ds(pl.multiple_of(core * half, half), half)]),
            (attn_ref, attn_out_ref),
            (small, small_out_ref.at[core]),
            (wq_ref, wq_out_ref),
            (wo_ref, wo_out_ref),
        )[kind]
        return pltpu.make_async_remote_copy(
            src_ref=src, dst_ref=dst, send_sem=core_send.at[kind], recv_sem=core_recv.at[kind],
            device_id=to_core, device_id_type=MESH,
        )

    def text_copy(kind):
        own = zl * 4
        other = (1 - zl) * 4
        block = (
            own + y, own + y, own + y, other + y, other + y, own + y_dn, own + y_up, other + y_dn, other + y_up
        )[kind]
        dst = hidden.at[block]
        src = text_ref.at[core] if kind < 3 else dst
        if kind >= 5:
            at = pl.ds(((kind - 5) % 2) * 64, 64)
            src, dst = src.at[at], dst.at[at]
        peer = to_z_lo if kind == 2 else to_y[(0, 1, 2, 0, 1, 0, 1, 0, 1)[kind]]
        return pltpu.make_async_remote_copy(
            src_ref=src, dst_ref=dst, send_sem=text_send.at[kind], recv_sem=text_recv.at[kind],
            device_id=peer, device_id_type=MESH,
        )

    def remote(kind, piece, src, dst, peer):
        return pltpu.make_async_remote_copy(
            src_ref=src, dst_ref=dst,
            send_sem=send.at[kind], recv_sem=recv.at[kind, piece],
            device_id=peer, device_id_type=MESH,
        )

    def y1_copy(way, piece):
        at = rows_of(piece)
        return remote(way, piece, part.at[0, way, at], from_y1.at[way, at], to_y[way])

    def y2_copy(way, piece):
        at = rows_of(piece)
        return remote(2 + way, piece, part.at[1 + way, :, at], from_y2.at[way, :, at], to_y[way])

    def z_copy(piece):
        at = rows_of(piece)
        return remote(4, piece, part.at[3, 1 - zl, at], from_z.at[at], to_z_lo)

    def own_copy(way, piece):
        at = rows_of(piece)
        return remote(5 + way, piece, done.at[at], out_ref.at[dp, at], to_z_hi if way == 0 else to_x[way - 1])

    def own_local(piece):
        at = rows_of(piece)
        return pltpu.make_async_copy(done.at[at], out_ref.at[dp, at], loc_sem.at[0])

    def pair_copy(way, piece):
        ref = out_ref.at[x * 2 + 1 - zh, rows_of(piece)]
        return remote(8 + way, piece, ref, ref, to_x[way])

    def forward_copy(way, piece):
        image = (x_dn * 2 + zh, x_up * 2 + 1 - zh)[way]
        ref = out_ref.at[image, rows_of(piece)]
        return remote(10 + way, piece, ref, ref, to_x[way])

    def mirror_copy(kind, at):
        across = (x + 2) % 4
        place = (
            (x, zh), (x, 1 - zh), (x_dn, zh), (x_up, zh), (x_dn, 1 - zh), (x_up, 1 - zh), (across, zh), (across, 1 - zh)
        )[kind]
        ref = out_ref.at[place[0] * 2 + place[1], at]
        return pltpu.make_async_remote_copy(
            src_ref=done.at[at] if kind == 0 else ref, dst_ref=ref,
            send_sem=send.at[12 + kind], recv_sem=mirror_recv.at[kind],
            device_id=to_core, device_id_type=MESH,
        )

    def mirror(kinds, piece):
        @pl.when(piece % GROUP == GROUP - 1)
        def _():
            at = pl.ds(first_row(piece - (GROUP - 1)), rows * GROUP)
            for kind in kinds:
                mirror_copy(kind, at).start()

    for ring in range(4):
        for side in range(2):
            w_copy(ring, side).start()

    def start_tok(piece, carry):
        tok_copy(piece).start()
        return carry

    lax.fori_loop(0, PIECES // 2, start_tok, 0)
    small[0:1, :] = q_gain_ref[...]
    small[1:2, :] = jnp.tanh(jnp.broadcast_to(gate_ref[0], (1, 128)))
    small_own = pltpu.make_async_copy(small, small_out_ref.at[core], loc_sem.at[1])
    small_own.start()
    text_own = pltpu.make_async_copy(text_ref.at[core], hidden.at[zl * 4 + y], load_sem.at[0])
    text_own.start()
    acc[...] = jnp.zeros_like(acc)
    sq[...] = jnp.zeros_like(sq)
    pl.semaphore_wait(barrier, len(peers))
    to_other_core(0).start()
    text_copy(2).start()
    for kind in range(1, 5):
        to_other_core(kind).start()

    own, other = zl * 4, (1 - zl) * 4
    blocks = [own + y, other + y, own + y_dn, own + y_up, other + y_dn, other + y_up]
    blocks += [own + (y + 2) % 4, other + (y + 2) % 4]
    columns = [pl.ds(pl.multiple_of(block * 1024, 1024), 1024) for block in blocks]

    def query_loads():
        return [
            LayerLoad(0, attn_ref, attn_out_ref, attn, load_sem.at[1]),
            pltpu.make_async_copy(small_out_ref.at[0], layer_small, load_sem.at[2]),
        ]

    def wq_load(k):
        return LayerLoad(0, wq_ref.at[columns[k]], wq_out_ref.at[columns[k]], wq.at[k], wq_sem.at[k])

    def use(*which):
        for k in which:
            wq_load(k).wait()
            add_to_query(acc, sq, hidden[blocks[k]], attn[:, columns[k]], wq[k])

    def add(ring, side, at, addend):
        part[ring, side, at, :] = (part[ring, side, at, :].astype(F32) + addend.astype(F32)).astype(BF)

    def step_fn(it, carry):
        @pl.when((it < PIECES) & (it % JOINT == 0))
        def _():
            piece = it

            @pl.when(piece < PIECES // 2)
            def _():
                for more in range(JOINT):
                    tok_copy(piece + more).wait()

            @pl.when(piece == PIECES // 2)
            def _():
                to_other_core(0).wait_recv()

            at = pl.ds(first_row(piece), rows * JOINT)
            for ring in range(4):
                for side in range(2):
                    @pl.when(it == 0)
                    def _():
                        w_copy(ring, side).wait()

                    part[ring, side, at, :] = jnp.dot(
                        tok[at, :], wgt[ring, side], preferred_element_type=F32
                    ).astype(BF)
                    if ring == 0:
                        for more in range(JOINT):
                            y1_copy(side, piece + more).start()

        @pl.when((it >= 1) & (it < PIECES + 1))
        def _():
            piece = it - 1
            at = rows_of(piece)
            for way in range(2):
                y1_copy(way, piece).wait_recv()
                add(1 + way, way, at, from_y1[way, at, :])
                y2_copy(way, piece).start()

            @pl.when(piece == PIECES - 1)
            def _():
                text_copy(2).wait_recv()
                for kind in (0, 1, 3, 4):
                    text_copy(kind).start()

        @pl.when((it >= 2) & (it < PIECES + 2))
        def _():
            piece = it - 2
            at = rows_of(piece)
            for way in range(2):
                y2_copy(way, piece).wait_recv()
            add(
                3, 1 - zl, at,
                from_y2[0, 1 - zl, at, :].astype(F32) + from_y2[1, 1 - zl, at, :].astype(F32),
            )
            z_copy(piece).start()

            @pl.when(piece == PIECES - 1)
            def _():
                small_own.wait()
                for kind in range(1, 4):
                    to_other_core(kind).wait_recv()
                for copy in query_loads():
                    copy.start()
                for k in range(8):
                    wq_load(k).start()

        @pl.when((it >= 3) & (it < PIECES + 3))
        def _():
            piece = it - 3
            at = rows_of(piece)
            z_copy(piece).wait_recv()
            total = (
                part[3, zl, at, :].astype(F32)
                + from_y2[0, zl, at, :].astype(F32) + from_y2[1, zl, at, :].astype(F32)
                + from_z[at, :].astype(F32)
            )
            keys = total[:, :128]
            keys = keys * lax.rsqrt(jnp.mean(keys * keys, axis=-1, keepdims=True) + 1e-05)
            done[at, 0:128] = (keys * gain_ref[...]).astype(BF)
            done[at, 128:256] = total[:, 128:].astype(BF)
            for way in range(3):
                own_copy(way, piece).start()
            own_local(piece).start()
            mirror((0,), piece)

        @pl.when((it >= 4) & (it < PIECES + 4))
        def _():
            piece = it - 4
            own_copy(0, piece).wait_recv()
            for way in range(2):
                pair_copy(way, piece).start()

            @pl.when(piece == PIECES - 1)
            def _():
                for kind in (0, 1):
                    text_copy(kind).wait_recv()
                    text_copy(kind + 5).start()
                text_own.wait()
                for copy in query_loads():
                    copy.wait()
                use(0, 1)
            mirror((1,), piece)

        @pl.when((it >= 5) & (it < PIECES + 5))
        def _():
            piece = it - 5
            own_copy(1, piece).wait_recv()
            pair_copy(1, piece).wait_recv()
            for way in range(2):
                forward_copy(way, piece).start()
            own_copy(2, piece).wait_recv()
            pair_copy(0, piece).wait_recv()
            mirror((2, 3, 4, 5), piece)

            @pl.when(piece == PIECES - 1)
            def _():
                for kind in (3, 4):
                    text_copy(kind).wait_recv()
                    text_copy(kind + 4).start()
                use(2, 3)

        @pl.when(it >= 6)
        def _():
            piece = it - 6
            for way in range(2):
                forward_copy(way, piece).wait_recv()
            mirror((6, 7), piece)

            @pl.when(piece == PIECES - 1)
            def _():
                use(4, 5)

        return carry

    lax.fori_loop(0, PIECES + 6, step_fn, 0)

    for kind in (5, 6):
        text_copy(kind).wait_recv()
    use(6)
    for kind in (7, 8):
        text_copy(kind).wait_recv()
    use(7)
    finish_query(acc, sq, layer_small[0:1, :], query_ref)

    whole = pl.ds(0, half * 2)

    def sent(kind, ref):
        pltpu.make_async_remote_copy(
            src_ref=ref, dst_ref=ref, send_sem=send.at[kind], recv_sem=recv.at[kind, 0],
            device_id=to_core, device_id_type=MESH,
        ).wait_send()

    for way in range(2):
        sent(way, part.at[0, way])
        sent(2 + way, part.at[1 + way])
    for kind in range(4, 12):
        sent(kind, done)
    for kind in range(8):
        mirror_copy(kind, whole).wait()
    pltpu.make_async_copy(done, out_ref.at[dp], loc_sem.at[0]).wait()
    for kind in range(4):
        to_other_core(kind).wait_send()
    to_other_core(4).wait()
    for kind in range(9):
        text_copy(kind).wait_send()


def image_pairs(tokens, weights, gain, q_gain, gate, text, w_query, w_out, attn_gain):
    half, width = tokens.shape
    heads = weights.shape[0]
    patches = half * 2
    any_spec = pl.BlockSpec(memory_space=pl.ANY)

    def like(array):
        return jax.ShapeDtypeStruct(array.shape, array.dtype)

    return pl.pallas_call(
        kv_kernel,
        name="kv",
        out_shape=[
            jax.ShapeDtypeStruct((2, 8, patches, 256), BF),
            jax.ShapeDtypeStruct((512, 128), BF),
            like(w_query),
            like(w_out),
            like(attn_gain),
            jax.ShapeDtypeStruct((2, 2, 128), F32),
        ],
        in_specs=[any_spec] * 2
        + [pl.BlockSpec(memory_space=pltpu.VMEM)] * 2
        + [pl.BlockSpec(memory_space=pltpu.SMEM)]
        + [any_spec] * 4,
        out_specs=[any_spec, pl.BlockSpec(memory_space=pltpu.VMEM)] + [any_spec] * 4,
        scratch_shapes=[
            pltpu.VMEM((8, 128, 1024), BF),
            pltpu.VMEM((8, 1024, 512), BF),
            pltpu.VMEM((1, 8192), F32),
            pltpu.VMEM((2, 128), F32),
            pltpu.VMEM((128, 512), F32),
            pltpu.VMEM((128, 128), F32),
            pltpu.VMEM((2, 128), F32),
            pltpu.VMEM((patches, width), BF),
            pltpu.VMEM((4, 2, width, 256), BF),
            pltpu.VMEM((4, 2, patches, 256), BF),
            pltpu.VMEM((2, patches, 256), BF),
            pltpu.VMEM((2, 2, patches, 256), BF),
            pltpu.VMEM((patches, 256), BF),
            pltpu.VMEM((patches, 256), BF),
            pltpu.SemaphoreType.DMA((PIECES // 2,)),
            pltpu.SemaphoreType.DMA((8,)),
            pltpu.SemaphoreType.DMA((2,)),
            pltpu.SemaphoreType.DMA((5,)),
            pltpu.SemaphoreType.DMA((5,)),
            pltpu.SemaphoreType.DMA((9,)),
            pltpu.SemaphoreType.DMA((9,)),
            pltpu.SemaphoreType.DMA((20,)),
            pltpu.SemaphoreType.DMA((12, PIECES)),
            pltpu.SemaphoreType.DMA((8,)),
            pltpu.SemaphoreType.DMA((3,)),
            pltpu.SemaphoreType.DMA((8,)),
        ],
        compiler_params=pltpu.CompilerParams(
            collective_id=0, has_side_effects=True, vmem_limit_bytes=60 * 2**20
        ),
        cost_estimate=pl.CostEstimate(
            flops=2 * patches * width * heads * 256, bytes_accessed=40 * 2**20, transcendentals=0
        ),
    )(tokens, weights, gain, q_gain, gate, text, w_query, w_out, attn_gain)


KEY_PARTS = ((0, 512), (512, 512), (1024, 576))


def add_tile(query, tiles, image, tile, total, norm, weight=None):
    for start, size in KEY_PARTS:
        at = slice(tile * TILE_TOK + start, tile * TILE_TOK + start + size)
        scores = lax.dot_general(
            query[...], tiles[image, at, 0:128], (((1,), (1,)), ((), ())), preferred_element_type=F32
        )
        expo = jnp.exp(scores)
        sums = jnp.sum(expo, axis=-1, keepdims=True)
        values = jnp.dot(expo.astype(BF), tiles[image, at, 128:256], preferred_element_type=F32)
        norm[...] += sums if weight is None else sums * weight
        total[...] += values if weight is None else values * weight


def side_by_side(total, norm, att_ref):
    for head in range(4):
        at = slice(head * 128, (head + 1) * 128)
        att_ref[:, at] = (total[at, :] / norm[at, :1]).astype(BF)


def attend(layer, choice_ref, valid_ref, query, pairs_ref, att_ref, tiles, total, norm, sem):
    core = lax.axis_index("section")
    first = choice_ref[core, 0, 0]
    second = choice_ref[core, 0, 1]
    other = second != first
    plan = (
        (first, 0, None),
        (first, 1, valid_ref[first] > 1),
        (second, 0, other),
        (second, 1, other & (valid_ref[second] > 1)),
    )

    def copy(slot):
        image, tile, _ = plan[slot]
        return pltpu.make_async_copy(
            pairs_ref.at[layer, image, pl.ds(tile * TILE_TOK, TILE_TOK)], tiles.at[slot], sem.at[slot]
        )

    def run(slot, fn):
        allowed = plan[slot][2]
        if allowed is None:
            fn()
        else:
            pl.when(allowed)(fn)

    for slot in range(4):
        run(slot, lambda slot=slot: copy(slot).start())
    total[...] = jnp.zeros_like(total)
    norm[...] = jnp.zeros_like(norm)

    def one(slot):
        copy(slot).wait()
        add_tile(query, tiles, slot, 0, total, norm)

    for slot in range(4):
        run(slot, functools.partial(one, slot))
    side_by_side(total, norm, att_ref)


def first_attention(choice_ref, valid_ref, pairs_ref, query_ref, att_ref, tiles, total, norm, sem):
    attend(0, choice_ref, valid_ref, query_ref, pairs_ref, att_ref, tiles, total, norm, sem)


ATTEND_SCRATCH = [
    pltpu.VMEM((4, TILE_TOK, 256), BF),
    pltpu.VMEM((512, 128), F32),
    pltpu.VMEM((512, 128), F32),
    pltpu.SemaphoreType.DMA((4,)),
]


def attention_first(choice, valid, pairs, query):
    any_spec = pl.BlockSpec(memory_space=pl.ANY)
    smem = pl.BlockSpec(memory_space=pltpu.SMEM)
    vmem = pl.BlockSpec(memory_space=pltpu.VMEM)
    return pl.pallas_call(
        first_attention,
        name="attend",
        out_shape=jax.ShapeDtypeStruct((128, 512), BF),
        in_specs=[smem, smem, any_spec, vmem],
        out_specs=vmem,
        scratch_shapes=ATTEND_SCRATCH,
        compiler_params=pltpu.CompilerParams(vmem_limit_bytes=60 * 2**20),
        cost_estimate=pl.CostEstimate(flops=2 * 10**9, bytes_accessed=4 * 2**20, transcendentals=3 * 10**6),
    )(choice, valid, pairs, query)


Y_ROWS = 64
NEAR = pl.ds(0, Y_ROWS)
REST = pl.ds(Y_ROWS, 128 - Y_ROWS)
HALF = (pl.ds(0, 512), pl.ds(512, 512))


OUT_ORDER = ((0, 0), (0, 1), (2, 0), (1, 1), (1, 0), (2, 1), (3, 0), (3, 1))


def load_out(layer, wo_ref, wo_other_ref, scratch):
    wo, wo_sem = scratch[0], scratch[8]
    y = position()[3]
    loads = {}
    for ring, side in OUT_ORDER:
        block = side * 4 + ((y + 2) % 4, (y + 1) % 4, (y + 3) % 4, y)[ring]
        at = pl.ds(pl.multiple_of(block * 1024, 1024), 1024)
        loads[ring, side] = LayerLoad(
            layer, wo_ref.at[:, at], wo_other_ref.at[:, at], wo.at[ring, side], wo_sem.at[ring * 2 + side]
        )
        loads[ring, side].start()
    return loads


def project_and_sum(att_ref, loads, scratch, greet=None):
    wo, part, from_y1, from_y2, from_z, from_c, from_c1, from_c2, _, send, recv = scratch
    x, zh, zl, y, core = position()
    to_y = (device(x, zh, zl, (y + 1) % 4, core), device(x, zh, zl, (y + 3) % 4, core))
    to_z = device(x, zh, 1 - zl, y, core)

    def remote(kind, src, dst, peer):
        return pltpu.make_async_remote_copy(
            src_ref=src, dst_ref=dst, send_sem=send.at[kind], recv_sem=recv.at[kind],
            device_id=peer, device_id_type=MESH,
        )

    far = [remote(way, part.at[0, way, NEAR], from_y1.at[way], to_y[way]) for way in range(2)]
    near = {
        (ring, side): remote(2 + ring * 2 + side - 2, part.at[ring, side, NEAR], from_y2.at[ring - 1, side], to_y[ring - 1])
        for ring in (1, 2) for side in range(2)
    }
    cross = [remote(6 + ring, part.at[ring, 1 - zl, REST], from_c.at[ring], to_z) for ring in range(4)]
    cross_far = [
        remote(10 + way, part.at[0, zl, REST, HALF[way]], from_c1.at[way], to_y[way]) for way in range(2)
    ]
    cross_near = [remote(12 + way, part.at[1 + way, zl, REST], from_c2.at[way], to_y[way]) for way in range(2)]
    last = remote(14, part.at[3, 1 - zl, NEAR], from_z, to_z)
    at_once = {(0, 0): far[0], (0, 1): far[1], (2, 0): near[2, 0], (1, 1): near[1, 1]}

    for ring, side in OUT_ORDER:
        loads[ring, side].wait()
        part[ring, side] = jnp.dot(att_ref[...], wo[ring, side], preferred_element_type=F32).astype(BF)
        if (ring, side) == (0, 0) and greet is not None:
            greet()
        if (ring, side) in at_once:
            at_once[ring, side].start()

        @pl.when(zl != side)
        def _():
            cross[ring].start()

    def add(ring, side, rows, columns, addend):
        part[ring, side, rows, columns] = (
            part[ring, side, rows, columns].astype(F32) + addend.astype(F32)
        ).astype(BF)

    every = slice(None)
    for way, key in ((0, (1, 0)), (1, (2, 1))):
        far[way].wait_recv()
        add(*key, NEAR, every, from_y1[way])
        near[key].start()
    cross[0].wait_recv()
    add(0, zl, REST, every, from_c[0])
    for way in range(2):
        cross_far[way].start()
    for ring in range(1, 4):
        cross[ring].wait_recv()
        add(ring, zl, REST, every, from_c[ring])
    for key in near:
        near[key].wait_recv()
    add(3, 1 - zl, NEAR, every, from_y2[0, 1 - zl].astype(F32) + from_y2[1, 1 - zl].astype(F32))
    last.start()
    for way in range(2):
        cross_far[way].wait_recv()
        add(1 + way, zl, REST, HALF[way], from_c1[way])
        cross_near[way].start()
    first = part[3, zl, NEAR, :].astype(F32) + from_y2[0, zl].astype(F32) + from_y2[1, zl].astype(F32)
    second = part[3, zl, REST, :].astype(F32)
    last.wait_recv()
    first = first + from_z[...].astype(F32)
    for way in range(2):
        cross_near[way].wait_recv()
        second = second + from_c2[way].astype(F32)

    def drain():
        for copy in far + list(near.values()) + cross + cross_far + cross_near + [last]:
            copy.wait_send()

    return first, second, drain


SUM_SCRATCH = [
    pltpu.VMEM((4, 2, 512, 1024), BF),
    pltpu.VMEM((4, 2, 128, 1024), BF),
    pltpu.VMEM((2, Y_ROWS, 1024), BF),
    pltpu.VMEM((2, 2, Y_ROWS, 1024), BF),
    pltpu.VMEM((Y_ROWS, 1024), BF),
    pltpu.VMEM((4, 128 - Y_ROWS, 1024), BF),
    pltpu.VMEM((2, 128 - Y_ROWS, 512), BF),
    pltpu.VMEM((2, 128 - Y_ROWS, 1024), BF),
    pltpu.SemaphoreType.DMA((8,)),
    pltpu.SemaphoreType.DMA((15,)),
    pltpu.SemaphoreType.DMA((15,)),
]


def greeting(peers):
    barrier = pltpu.get_barrier_semaphore()
    for peer in peers:
        pl.semaphore_signal(barrier, inc=1, device_id=peer, device_id_type=MESH)
    pl.semaphore_wait(barrier, len(peers))


def text_kernel(
    choice_ref, valid_ref, att_ref, pairs_ref, text_ref, wo_ref, wo_other_ref, wq_ref, wq_other_ref,
    attn_ref, attn_other_ref, small_ref, out_ref, *scratch,
):
    count = len(SUM_SCRATCH)
    sums, last_sums = scratch[:count], scratch[count:2 * count]
    (
        images, hidden, wq, attn, small, text, acc, sq, query, total, norm, att, new,
        wq_sem, ag_send, ag_recv, par_sem, core_send, core_recv,
    ) = scratch[2 * count:]
    x, zh, zl, y, core = position()
    y_up, y_dn = (y + 1) % 4, (y + 3) % 4
    to_up = device(x, zh, zl, y_up, core)
    to_dn = device(x, zh, zl, y_dn, core)
    to_z = device(x, zh, 1 - zl, y, core)
    to_core = device(x, zh, zl, y, 1 - core)
    loads = load_out(0, wo_ref, wo_other_ref, sums)
    par_copies = [
        pltpu.make_async_copy(small_ref, small, par_sem.at[0]),
        LayerLoad(1, attn_ref, attn_other_ref, attn, par_sem.at[1]),
        pltpu.make_async_copy(text_ref.at[core], text, par_sem.at[2]),
    ]
    for copy in par_copies:
        copy.start()
    images_copy = pltpu.make_async_copy(pairs_ref.at[1], images, par_sem.at[3])

    first, second, drain = project_and_sum(
        att_ref, loads, sums, lambda: greeting([to_up, to_dn, to_z, to_core])
    )
    mine, across = zl * 4, (1 - zl) * 4
    own, left, right, far = mine + y, mine + y_dn, mine + y_up, mine + (y + 2) % 4
    z_own, z_left, z_right, z_far = across + y, across + y_dn, across + y_up, across + (y + 2) % 4
    order = [own, left, right, z_own, z_left, z_right, far, z_far]
    chunks = []
    for k, block in enumerate(order):
        at = pl.ds(pl.multiple_of(block * 1024, 1024), 1024)
        chunks.append(LayerLoad(1, wq_ref.at[at], wq_other_ref.at[at], wq.at[k], wq_sem.at[k]))
        chunks[k].start()
    images_copy.start()
    last_loads = load_out(1, wo_ref, wo_other_ref, last_sums)
    for copy in par_copies:
        copy.wait()
    gate = small[0, 1:2, 0:1]

    def remote(kind, block, rows, peer, half=None):
        ref = hidden.at[block, rows] if half is None else hidden.at[block, rows, HALF[half]]
        return pltpu.make_async_remote_copy(
            src_ref=ref, dst_ref=ref, send_sem=ag_send.at[kind], recv_sem=ag_recv.at[kind],
            device_id=peer, device_id_type=MESH,
        )

    copies = [
        remote(0, own, NEAR, to_z), remote(1, own, NEAR, to_up), remote(2, own, NEAR, to_dn),
        remote(3, own, REST, to_up), remote(4, own, REST, to_dn), remote(5, own, REST, to_z),
        remote(6, left, REST, to_up, 0), remote(7, right, REST, to_dn, 1),
        remote(8, left, REST, to_z), remote(9, right, REST, to_z), remote(10, far, REST, to_z),
        remote(11, z_own, NEAR, to_up), remote(12, z_own, NEAR, to_dn),
        remote(13, left, NEAR, to_up, 0), remote(14, right, NEAR, to_dn, 1),
        remote(15, z_left, NEAR, to_up, 0), remote(16, z_right, NEAR, to_dn, 1),
    ]

    def begin(*kinds):
        for kind in kinds:
            copies[kind].start()

    def arrive(*kinds):
        for kind in kinds:
            copies[kind].wait_recv()

    def use(k):
        chunks[k].wait()
        block = order[k]
        at = pl.ds(pl.multiple_of(block * 1024, 1024), 1024)
        add_to_query(acc, sq, hidden[block], attn[:, at], wq[k])

    hidden[own, NEAR, :] = (text[NEAR, :].astype(F32) + gate * first).astype(BF)
    begin(0)
    hidden[own, REST, :] = (text[REST, :].astype(F32) + gate * second).astype(BF)
    begin(3, 4, 1, 2, 5)
    send_first = pltpu.make_async_remote_copy(
        src_ref=hidden.at[own], dst_ref=out_ref.at[1], send_sem=core_send.at[0], recv_sem=core_recv.at[0],
        device_id=to_core, device_id_type=MESH,
    )
    send_last = pltpu.make_async_remote_copy(
        src_ref=new, dst_ref=out_ref.at[0], send_sem=core_send.at[1], recv_sem=core_recv.at[1],
        device_id=to_core, device_id_type=MESH,
    )

    @pl.when(core == 1)
    def _():
        send_first.start()

    @pl.when(core == 0)
    def _():
        out_ref[0] = hidden[own]

    acc[...] = jnp.zeros_like(acc)
    sq[...] = jnp.zeros_like(sq)
    use(0)
    arrive(3)
    begin(6, 8)
    arrive(4)
    begin(7, 9)
    arrive(0)
    begin(11, 12)
    arrive(1)
    begin(13)
    arrive(2)
    begin(14)
    use(1)
    use(2)
    arrive(6, 7)
    begin(10)
    arrive(11)
    begin(15)
    arrive(12)
    begin(16)
    arrive(5)
    use(3)
    arrive(8)
    use(4)
    arrive(9)
    use(5)
    arrive(13, 14)
    use(6)
    arrive(10, 15, 16)
    use(7)
    finish_query(acc, sq, small[1, 0:1, :], query)

    total[...] = jnp.zeros_like(total)
    norm[...] = jnp.zeros_like(norm)
    one_image, two_image = choice_ref[core, 0, 0], choice_ref[core, 0, 1]
    other = jnp.where(two_image != one_image, 1.0, 0.0)
    images_copy.wait()
    add_tile(query, images, one_image, 0, total, norm)
    add_tile(query, images, one_image, 1, total, norm, (valid_ref[one_image] - 1).astype(F32))
    add_tile(query, images, two_image, 0, total, norm, other)
    add_tile(query, images, two_image, 1, total, norm, other * (valid_ref[two_image] - 1).astype(F32))
    side_by_side(total, norm, att)

    first, second, last_drain = project_and_sum(att, last_loads, last_sums)
    gate = small[1, 1:2, 0:1]
    new[NEAR, :] = (hidden[own, NEAR, :].astype(F32) + gate * first).astype(BF)
    new[REST, :] = (hidden[own, REST, :].astype(F32) + gate * second).astype(BF)

    @pl.when(core == 0)
    def _():
        send_last.start()
        send_first.wait_recv()
        send_last.wait_send()

    @pl.when(core == 1)
    def _():
        out_ref[1] = new[...]
        send_first.wait_send()
        send_last.wait_recv()

    drain()
    last_drain()
    for copy in copies:
        copy.wait_send()


def text_steps(choice, valid, att, *arrays):
    any_spec = pl.BlockSpec(memory_space=pl.ANY)
    vmem = pl.BlockSpec(memory_space=pltpu.VMEM)
    smem = pl.BlockSpec(memory_space=pltpu.SMEM)
    return pl.pallas_call(
        text_kernel,
        name="text",
        out_shape=jax.ShapeDtypeStruct((2, 128, 1024), BF),
        in_specs=[smem, smem, vmem] + [any_spec] * len(arrays),
        out_specs=vmem,
        scratch_shapes=SUM_SCRATCH * 2 + [
            pltpu.VMEM(arrays[0].shape[1:], BF),
            pltpu.VMEM((8, 128, 1024), BF),
            pltpu.VMEM((8, 1024, 512), BF),
            pltpu.VMEM((1, 8192), F32),
            pltpu.VMEM((2, 2, 128), F32),
            pltpu.VMEM((128, 1024), BF),
            pltpu.VMEM((128, 512), F32),
            pltpu.VMEM((128, 128), F32),
            pltpu.VMEM((512, 128), BF),
            pltpu.VMEM((512, 128), F32),
            pltpu.VMEM((512, 128), F32),
            pltpu.VMEM((128, 512), BF),
            pltpu.VMEM((128, 1024), BF),
            pltpu.SemaphoreType.DMA((8,)),
            pltpu.SemaphoreType.DMA((17,)),
            pltpu.SemaphoreType.DMA((17,)),
            pltpu.SemaphoreType.DMA((4,)),
            pltpu.SemaphoreType.DMA((2,)),
            pltpu.SemaphoreType.DMA((2,)),
        ],
        compiler_params=pltpu.CompilerParams(
            collective_id=1, has_side_effects=True, vmem_limit_bytes=60 * 2**20
        ),
    )(choice, valid, att, *arrays)


def local(
    text_hidden,
    image_tokens,
    attn_gain,
    w_query,
    w_keyval,
    q_gain,
    k_gain,
    w_out,
    gate,
    image_choice,
    valid_tiles,
):
    text = text_hidden[:, 0]
    weights = jnp.transpose(w_keyval[0], (1, 0, 2))
    wq, wo = w_query[0], w_out[0]
    pairs, query, wq_other, wo_other, attn_other, small = image_pairs(
        image_tokens[0], weights, k_gain, q_gain, gate, text, wq, wo, attn_gain
    )
    gains = (attn_gain, attn_other, small)
    att = attention_first(image_choice, valid_tiles, pairs, query)
    result = text_steps(
        image_choice, valid_tiles, att, pairs, text, wo, wo_other, wq, wq_other, *gains
    )
    return result[None, :, None]


def solution(mesh):
    placed = (
        P(None, "dp", None, "tensor"),
        P("dp", "section", "tensor"),
        P("section", None),
        P("section", None, "tensor"),
        P("section", "tensor", None, None),
        P("section", None),
        P("section", None),
        P("section", "tensor", None),
        P("section"),
        P(None, "dp", None),
        P(),
    )
    return jax.shard_map(
        local,
        mesh=mesh,
        in_specs=placed,
        out_specs=P("section", None, "dp", None, "tensor"),
        check_vma=False,
    )
```
